128 devices in a mesh: member: 8 (over z_hi, x), sector: 16 (over z_lo, y, core).
Axes of the slice: x: 4, y: 4, z: 4 (z_hi: 2, z_lo: 2; z = z_hi * 2 + z_lo), core: 2. Of those that a mesh axis runs over, the one named last changes fastest.
Arguments:
- ensemble: float32 [128, 5, 1440, 128], P('member', None, 'sector'), may hold values from -6 to 6
- ocean_depth: float32 [1440, 128], P('sector'), may hold values from 0.5 to 2
- planetary_vorticity: float32 [128], replicated, may hold values from -0.5 to 0.5
- land_mask: int32 [1440, 128], P('sector'), may hold values 0 or 1
- obs_values: float32 [1024], replicated, may hold values from -6 to 6
- obs_error: float32 [1024], replicated, may hold values from 0.2 to 2
- obs_lon: int32 [1024], replicated, may hold values from 0 to 1439
- obs_lat: int32 [1024], replicated, may hold values from 0 to 127
- obs_field: int32 [1024], replicated, may hold values from 2 to 4
- obs_order: int32 [1024], replicated, may hold values from 0 to 1023, each once
Outputs:
- analysis: float32 [5, 128, 1440, 128], P(None, 'member', 'sector')
The draws below stay inside these ranges and needn't reach their ends.
Inputs may be any that keep to these rules, and one draw needn't show every extreme that they name: `obs_field`: observed fields are height, temperature or salinity. `obs_order`: each observation index appears once.
All inputs are finite; a program needn't handle non-finite values. No bound on the sum of `land_mask` on one device may be relied on, other than what follows from the above.
Results may differ from the reference program's by a relative error of at most 0.0001.
Values sent between devices are 32-bit elements; how exact they have to be, the bound alone decides.
No kernel may reach another device: no remote copies, remote signals or barrier semaphores. Data moves between devices by JAX's collectives and lax.ppermute only.
A program may use at most 128 MiB of HBM per device.

```python
import math
import jax
import jax.numpy as jnp
from jax import lax

NLON = 1440
LAT = 128
FIELDS = 5
MEMBERS = 128
BATCH = 512
BATCHES = 2
LOC_RADIUS = 48
NOBS = 1024


def touch_ends(array, stream_key, least, largest):
    longest = array.shape.index(max(array.shape))
    spots = []
    for shift in (0, 1):
        where = [jax.random.randint(jax.random.fold_in(stream_key, axis), (), 0, length) for axis, length in enumerate(array.shape)]
        where[longest] = (where[longest] + shift) % array.shape[longest]
        spots.append(tuple(where))
    return array.at[spots[0]].set(least).at[spots[1]].set(largest)


def block_scale(own_key, shape, cuts, smallest, largest):
    level, own = 1.0, jax.random.fold_in(own_key, 6)
    for dim, shards_of in cuts:
        steps = jnp.exp(jax.random.uniform(jax.random.fold_in(own, dim), (shards_of,), jnp.float32, smallest / len(cuts), largest / len(cuts)))
        level = level * jnp.repeat(steps, shape[dim] // shards_of).reshape([-1 if axis == dim else 1 for axis in range(len(shape))])
    return level


def centred(own_key, extent, width, most, shards=(), kind=jnp.bfloat16):
    array = jax.random.normal(own_key, extent, jnp.float32) * width
    if len(shards) > 0:
        array = block_scale(own_key, extent, shards, -0.22, 0.18) * array
    return jnp.clip(array, min=-most, max=most).astype(kind)


def setup_inputs(seed: int = 0) -> dict:
    key_of = jax.random.split(jax.random.key(seed), 11)
    ensemble = centred(key_of[0], (MEMBERS, FIELDS, NLON, LAT), 1.0, 6.0, ((0, 8), (2, 16)), jnp.float32)
    ocean_depth = jnp.clip(jnp.exp(math.log(2.0) - 1.3862944 * jax.random.uniform(key_of[1], (NLON, LAT), jnp.float32) ** block_scale(key_of[1], (NLON, LAT), ((0, 16),), -0.2, 0.2)), 0.5, 2.0)
    planetary_vorticity = jnp.clip(jax.random.uniform(key_of[2], (LAT,), jnp.float32, -0.5, 0.5), -0.5, 0.5)
    land_mask = touch_ends((jax.random.randint(key_of[3], (NLON, LAT), 0, 4) < 3).astype(jnp.int32), jax.random.fold_in(key_of[3], 1), 0, 1)
    obs_values = centred(key_of[4], (NOBS,), 1.0, 6.0, (), jnp.float32)
    obs_error = jnp.clip(jnp.exp(jax.random.uniform(key_of[5], (NOBS,), jnp.float32, math.log(0.2), math.log(2.0))), 0.2, 2.0)
    obs_lon = touch_ends(jax.random.randint(key_of[6], (NOBS,), 0, NLON), jax.random.fold_in(key_of[6], 1), 0, NLON - 1).astype(jnp.int32)
    obs_lat = touch_ends(jax.random.randint(key_of[7], (NOBS,), 0, LAT), jax.random.fold_in(key_of[7], 1), 0, LAT - 1).astype(jnp.int32)
    obs_field = touch_ends(jax.random.randint(key_of[8], (NOBS,), 2, 5), jax.random.fold_in(key_of[8], 1), 2, 4).astype(jnp.int32)
    obs_order = jax.random.permutation(key_of[9], NOBS).astype(jnp.int32)
    return dict(ensemble=ensemble, ocean_depth=ocean_depth, planetary_vorticity=planetary_vorticity, land_mask=land_mask, obs_values=obs_values, obs_error=obs_error, obs_lon=obs_lon, obs_lat=obs_lat, obs_field=obs_field, obs_order=obs_order)


GRAVITY = 0.3
FLUX_RATE = 0.3
ADVECTION = 0.3
DIFFUSION = 0.1
ROTATION = 1.0
EPSILON = 1e-06

def east_diff(values):
    return 0.5 * (values[..., 2:, :] - values[..., :-2, :])

def north_pad(values):
    return jnp.pad(values, [(0, 0)] * (values.ndim - 1) + [(1, 1)])

def north_diff(values):
    padded = north_pad(values)
    return 0.5 * (padded[..., 2:] - padded[..., :-2])

def interior_grid_points(values):
    return values[..., 1:-1, :]

def model_time_stepper(tracer_layers_array, bathymetry_padded_copy, seafloor_flags_padded, planetary_vorticity):
    zonal = tracer_layers_array[..., 0, :, :]
    northward = tracer_layers_array[..., 1, :, :]
    height = tracer_layers_array[..., 2, :, :]
    thermal_grid = tracer_layers_array[..., 3, :, :]
    saltiness_grid = tracer_layers_array[..., 4, :, :]
    rotation_term = ROTATION * planetary_vorticity[None, :]
    sea_points = interior_grid_points(seafloor_flags_padded)
    zonal_flow_speed = sea_points * (interior_grid_points(zonal) + rotation_term * interior_grid_points(northward) - GRAVITY * east_diff(height))
    meridional_flow_speed = sea_points * (interior_grid_points(northward) - rotation_term * interior_grid_points(zonal) - GRAVITY * interior_grid_points(north_diff(height)))
    east_flux = interior_grid_points(bathymetry_padded_copy) * zonal_flow_speed
    north_flux = interior_grid_points(bathymetry_padded_copy) * meridional_flow_speed
    surface_elevation_next = interior_grid_points(interior_grid_points(height)) - FLUX_RATE * (east_diff(east_flux) + interior_grid_points(north_diff(north_flux)))

    def running_ocean_snapshot(tracer):
        gradient = interior_grid_points(zonal_flow_speed) * interior_grid_points(east_diff(tracer)) + interior_grid_points(meridional_flow_speed) * interior_grid_points(interior_grid_points(north_diff(tracer)))
        padded = north_pad(interior_grid_points(tracer))
        laplace = tracer[..., 2:, :] + tracer[..., :-2, :] + padded[..., 2:] + padded[..., :-2] - 4.0 * interior_grid_points(tracer)
        return interior_grid_points(interior_grid_points(tracer)) - ADVECTION * gradient + DIFFUSION * interior_grid_points(laplace)
    return jnp.stack([interior_grid_points(zonal_flow_speed), interior_grid_points(meridional_flow_speed), surface_elevation_next, running_ocean_snapshot(thermal_grid), running_ocean_snapshot(saltiness_grid)], axis=-3)

def periodic_longitude_pad(values, margin):
    return jnp.concatenate([values[..., -margin:, :], values, values[..., :margin, :]], axis=-2)

def localize(cell_lat, cell_lon, lat_sel, lon_sel, loop):
    east_gap = jnp.abs(cell_lon[:, None] - lon_sel[None, :])
    east_gap = jnp.minimum(east_gap, loop - east_gap)
    north_gap = cell_lat[:, None] - lat_sel[None, :]
    distance = (east_gap * east_gap + north_gap * north_gap).astype(jnp.float32)
    ratio = 1.0 - distance / float(LOC_RADIUS * LOC_RADIUS)
    return jnp.square(jnp.maximum(ratio, 0.0))

def obs_moments(picked):
    count = picked.shape[0]
    prior_mean = lax.optimization_barrier(jnp.mean(picked, axis=0))
    anomalies = picked - prior_mean
    variance = lax.optimization_barrier(jnp.sum(anomalies * anomalies, axis=0)) / (count - 1) + EPSILON
    return (prior_mean, anomalies, variance)

def obs_adjust(prior_mean, anomalies, variance, values, errors, ratio):
    root = jnp.sqrt(ratio)
    inflated = ratio * variance
    spread = root * anomalies
    post_var = 1.0 / (1.0 / inflated + 1.0 / errors)
    post_mean = post_var * (prior_mean / inflated + values / errors)
    increments = post_mean - prior_mean + (jnp.sqrt(post_var / inflated) - 1.0) * spread
    return (spread, increments, inflated, root)

def regress(states, taper, spread_obs, increments, inflated, root):
    count = states.shape[0]
    mean_state = lax.optimization_barrier(jnp.mean(states, axis=0))
    spread = root * (states - mean_state)
    prior = mean_state + spread
    cov = jnp.einsum('mfc,mk->fck', spread, spread_obs, precision=lax.Precision.HIGHEST) / (count - 1)
    weights = taper[None] * cov / inflated
    return prior + jnp.einsum('fck,mk->mfc', weights, increments, precision=lax.Precision.HIGHEST)

def reference(ensemble, ocean_depth, planetary_vorticity, land_mask, obs_values, obs_error, obs_lon, obs_lat, obs_field, obs_order):
    invariant_grids = periodic_longitude_pad(jnp.stack([ocean_depth, land_mask.astype(jnp.float32)]), 2)

    def advance(member):
        tracer_layers_array = member
        for repeat in range(2):
            tracer_layers_array = model_time_stepper(periodic_longitude_pad(tracer_layers_array, 2), invariant_grids[0], invariant_grids[1], planetary_vorticity)
        return tracer_layers_array
    states = lax.map(advance, ensemble)
    lon_cells = jnp.arange(NLON, dtype=jnp.int32)
    for batch_index in range(BATCHES):
        chosen = obs_order[batch_index * BATCH:(batch_index + 1) * BATCH]
        lon_sel = jnp.take(obs_lon, chosen)
        lat_sel = jnp.take(obs_lat, chosen)
        field_sel = jnp.take(obs_field, chosen)
        values = jnp.take(obs_values, chosen)
        errors = jnp.take(obs_error, chosen)
        picked = states[:, field_sel, lon_sel, lat_sel]
        prior_mean, anomalies, variance = obs_moments(picked)
        innovation = values - prior_mean
        ratio = jnp.sum(innovation * innovation) / jnp.sum(variance + errors)
        spread_obs, increments, inflated, root = obs_adjust(prior_mean, anomalies, variance, values, errors, ratio)
        rows = jnp.moveaxis(states, 3, 0)

        def update_row(item):
            row_states, row_index = item
            cell_lat = row_index + jnp.zeros((NLON,), jnp.int32)
            taper = localize(cell_lat, lon_cells, lat_sel, lon_sel, NLON)
            return regress(row_states, taper, spread_obs, increments, inflated, root)
        rows = lax.map(update_row, (rows, jnp.arange(LAT, dtype=jnp.int32)))
        states = jnp.moveaxis(rows, 0, 3)
    return jnp.transpose(states, (1, 3, 2, 0))
```

```python
import functools

import jax
import jax.numpy as jnp
from jax import lax
from jax.experimental import pallas as pl
from jax.experimental.pallas import tpu as pltpu
from jax.sharding import PartitionSpec as P

NLON = 1440
LAT = 128
FIELDS = 5
MEMBERS = 128
NOBS = 1024
BATCH = 512
RADIUS = 48
SHARE = 16
WIDTH = 90
EDGE = 4
EXT = WIDTH + 2 * EDGE
WHOLE = WIDTH // 8
GROUPS = FIELDS * WHOLE + 2
CHUNK = 64
CHUNKS = BATCH // CHUNK
F32 = jnp.float32
BF16 = jnp.bfloat16
VMEM_LIMIT = 56 * 1024 * 1024


def forecast_kernel(me_ref, ens, left, right, depth, mask, vort, *rest):
    outs = rest[:8]
    seen, now, nxt, dep, sea, flux, sems = rest[8:]
    load = pltpu.make_async_copy(ens, now.at[:, pl.ds(EDGE, WIDTH)], sems.at[0])
    load.start()
    for side, base in ((left, 0), (right, EDGE + WIDTH)):
        for f in range(FIELDS):
            for j in range(EDGE):
                now[f, base + j] = side[pl.ds((f * EDGE + j) * SHARE, SHARE), :]
    rows = FIELDS * EDGE * SHARE
    for grid, own, at in ((dep, depth, rows), (sea, mask, rows + EDGE)):
        grid[pl.ds(8, WIDTH), :] = own[...]
        grid[pl.ds(4, EDGE), :] = left[pl.ds(at, EDGE), :]
        grid[pl.ds(8 + WIDTH, EDGE), :] = right[pl.ds(at, EDGE), :]
    lane = lax.broadcasted_iota(jnp.int32, (SHARE, LAT), 1)
    first, last = lane == 0, lane == LAT - 1
    spin = jnp.broadcast_to(vort[...], (SHARE, LAT))

    def north(a):
        return jnp.where(last, 0.0, pltpu.roll(a, LAT - 1, 1))

    def south(a):
        return jnp.where(first, 0.0, pltpu.roll(a, 1, 1))

    def step(src, dst, lo, hi):
        def flow(e, _):
            u, v, h = src[0, e], src[1, e], src[2, e]
            m = sea[pl.ds(e + 4, 1), :]
            un = m * (u + spin * v - 0.15 * (src[2, e + 1] - src[2, e - 1]))
            dst[0, e] = un
            dst[1, e] = m * (v - spin * u - 0.15 * (north(h) - south(h)))
            flux[e] = dep[pl.ds(e + 4, 1), :] * un
            return 0

        def rest_of(e, _):
            un, vn = dst[0, e], dst[1, e]
            dv = dep[pl.ds(e + 4, 1), :] * vn
            dst[2, e] = src[2, e] - 0.15 * (flux[e + 1] - flux[e - 1] + (north(dv) - south(dv)))
            for c in (3, 4):
                a, ae, aw = src[c, e], src[c, e + 1], src[c, e - 1]
                an, ao = north(a), south(a)
                dst[c, e] = (
                    a
                    - 0.15 * (un * (ae - aw) + vn * (an - ao))
                    + 0.1 * (((ae + aw) + (an + ao)) - 4.0 * a)
                )
            return 0

        lax.fori_loop(lo, hi, flow, 0, unroll=4)
        lax.fori_loop(lo + 1, hi - 1, rest_of, 0, unroll=2)

    load.wait()
    step(now, nxt, 1, EXT - 1)
    step(nxt, now, 3, EXT - 3)
    keep = pltpu.make_async_copy(now.at[pl.ds(2, 3), pl.ds(EDGE, WIDTH)], seen, sems.at[1])
    keep.start()

    me = me_ref[0]

    def deal(tiles, g):
        v = list(tiles)
        for k in range(3):
            s = SHARE << k
            low = ((lane >> (4 + k)) & 1) == 0
            flip = ((me >> k) & 1) == 1
            w = list(v)
            for i in range(8):
                if i & (1 << k):
                    continue
                j = i | (1 << k)
                a = jnp.where(low, v[i], pltpu.roll(v[j], s, 1))
                b = jnp.where(low, pltpu.roll(v[i], LAT - s, 1), v[j])
                w[i] = jnp.where(flip, b, a)
                w[j] = jnp.where(flip, a, b)
            v = w
        for d in range(8):
            outs[d][g] = v[d]

    def whole(g, _):
        f, lon = g // WHOLE, EDGE + (g % WHOLE) * 8
        deal([now[f, lon + j] for j in range(8)], g)
        return 0

    lax.fori_loop(0, FIELDS * WHOLE, whole, 0)
    end = EDGE + WHOLE * 8
    deal([now[j // 2, end + j % 2] for j in range(8)], GROUPS - 2)
    deal([now[4, end + j % 2] for j in range(8)], GROUPS - 1)
    keep.wait()


def forecast(me, ens, left, right, depth, mask, vort):
    message = jax.ShapeDtypeStruct((GROUPS, SHARE, LAT), F32)
    vmem = pl.BlockSpec(memory_space=pltpu.VMEM)
    return pl.pallas_call(
        forecast_kernel,
        out_shape=[message] * 8 + [jax.ShapeDtypeStruct((3, WIDTH, SHARE, LAT), F32)],
        in_specs=[pl.BlockSpec(memory_space=pltpu.SMEM), pl.BlockSpec(memory_space=pl.ANY)] + [vmem] * 5,
        out_specs=[vmem] * 8 + [pl.BlockSpec(memory_space=pl.ANY)],
        scratch_shapes=[
            pltpu.VMEM((FIELDS, EXT, SHARE, LAT), F32),
            pltpu.VMEM((FIELDS, EXT, SHARE, LAT), F32),
            pltpu.VMEM((112, LAT), F32),
            pltpu.VMEM((112, LAT), F32),
            pltpu.VMEM((EXT, SHARE, LAT), F32),
            pltpu.SemaphoreType.DMA((2,)),
        ],
        compiler_params=pltpu.CompilerParams(vmem_limit_bytes=VMEM_LIMIT),
        name="forecast",
    )(me, ens, left, right, depth, mask, vort)


def pick_kernel(order, cell, lat, seen, out):
    lane = lax.broadcasted_iota(jnp.int32, (SHARE, LAT), 1)

    def block(b, _):
        def one(r, total):
            k = order[b * LAT + r]
            at = cell[k]
            tile = seen[jnp.maximum(at, 0)]
            tile = pltpu.roll(tile, (r - lat[k]) & (LAT - 1), 1)
            return jnp.where(lane == jnp.where(at < 0, -1, r), tile, total)

        out[b] = lax.fori_loop(0, LAT, one, jnp.zeros((SHARE, LAT), F32), unroll=8)
        return 0

    lax.fori_loop(0, NOBS // LAT, block, 0)


def pick(order, cell, lat, seen):
    smem = pl.BlockSpec(memory_space=pltpu.SMEM)
    vmem = pl.BlockSpec(memory_space=pltpu.VMEM)
    return pl.pallas_call(
        pick_kernel,
        out_shape=jax.ShapeDtypeStruct((NOBS // LAT, SHARE, LAT), F32),
        in_specs=[smem, smem, smem, vmem],
        out_specs=vmem,
        compiler_params=pltpu.CompilerParams(vmem_limit_bytes=VMEM_LIMIT),
        name="pick_priors",
    )(order, cell, lat, seen)


def split(a):
    high = a.astype(BF16)
    return high, (a - high.astype(F32)).astype(BF16)


def sort_kernel(order, facts, out):
    data = facts[...]
    high = data.astype(BF16)
    left = data - high.astype(F32)
    mid = left.astype(BF16)
    low = (left - mid.astype(F32)).astype(BF16)
    parts = jnp.concatenate([high, mid, low, jnp.zeros_like(low)], axis=0)
    row = lax.broadcasted_iota(jnp.int32, (NOBS, LAT), 0)

    def block(b, _):
        chosen = order[b]
        hot = jnp.where(row == chosen, 1.0, 0.0).astype(BF16)
        got = jnp.dot(parts, hot, preferred_element_type=F32)
        out[b] = got[0:8] + got[8:16] + got[16:24]
        return 0

    lax.fori_loop(0, NOBS // LAT, block, 0)


def in_order(order, facts):
    vmem = pl.BlockSpec(memory_space=pltpu.VMEM)
    blocks = NOBS // LAT
    return pl.pallas_call(
        sort_kernel,
        out_shape=jax.ShapeDtypeStruct((blocks, 8, LAT), F32),
        in_specs=[vmem, vmem],
        out_specs=vmem,
        compiler_params=pltpu.CompilerParams(vmem_limit_bytes=VMEM_LIMIT),
        name="obs_in_batch_order",
    )(order.reshape(blocks, 1, LAT), facts)


def dot_nt(a, b):
    return lax.dot_general(a, b, (((1,), (1,)), ((), ())), preferred_element_type=F32)


def filter_kernel(
    place, priors, facts, cols, first, second, dlon, base, counts, roots, table, spread_h, spread_l, gain_h, gain_l
):
    for d in range(8):
        for b in range(NOBS // LAT):
            table[pl.ds(d * SHARE, SHARE), pl.ds(b * LAT, LAT)] = priors[d, b]
    west, south = place[0].astype(F32), place[1].astype(F32)
    facts_of = [
        jnp.concatenate([facts[b * 4 + i] for i in range(4)], axis=1) for b in range(2)
    ]
    upper = (
        lax.broadcasted_iota(jnp.int32, (BATCH, BATCH), 0)
        <= lax.broadcasted_iota(jnp.int32, (BATCH, BATCH), 1)
    )
    upper = jnp.where(upper, 1.0, 0.0).astype(BF16)

    def adjust(picked, fact, b):
        values, errors = fact[2:3], fact[3:4]
        mean = jnp.sum(picked, axis=0, keepdims=True) * (1.0 / MEMBERS)
        anomalies = picked - mean
        variance = jnp.sum(anomalies * anomalies, axis=0, keepdims=True) / (MEMBERS - 1) + 1e-6
        innovation = values - mean
        ratio = jnp.sum(innovation * innovation, axis=1, keepdims=True) / jnp.sum(
            variance + errors, axis=1, keepdims=True
        )
        root = jnp.sqrt(ratio)
        inflated = ratio * variance
        spread = root * anomalies
        post_var = 1.0 / (1.0 / inflated + 1.0 / errors)
        post_mean = post_var * (mean / inflated + values / errors)
        increments = post_mean - mean + (jnp.sqrt(post_var / inflated) - 1.0) * spread
        scaled = spread / ((MEMBERS - 1) * inflated)
        roots[b] = jnp.sum(root)
        return root, scaled, increments

    def near_ones(fact, scaled, increments, b):
        rel = fact[0:1] - west
        rel = jnp.where(rel < -float(NLON // 2 - WIDTH // 2), rel + NLON, rel)
        rel = jnp.where(rel >= float(NLON // 2 + WIDTH // 2), rel - NLON, rel)
        lat = fact[1:2] - south
        dl = jnp.maximum(jnp.maximum(-rel, rel - (WIDTH - 1)), 0.0)
        dr = jnp.maximum(jnp.maximum(-lat, lat - (SHARE - 1)), 0.0)
        near = dl * dl + dr * dr < float(RADIUS * RADIUS)
        flag = jnp.where(near, 1.0, 0.0)
        upto = jnp.dot(
            jnp.broadcast_to(flag, (8, BATCH)).astype(BF16), upper, preferred_element_type=F32
        )[0:1]
        slot = jnp.where(near, upto - 1.0, -1.0)
        count = (jnp.sum(flag).astype(jnp.int32) + CHUNK - 1) // CHUNK
        counts[b] = count
        spread_h[...], spread_l[...] = split(scaled)
        gain_h[...], gain_l[...] = split(increments)
        number = lax.broadcasted_iota(jnp.int32, (CHUNK, BATCH), 0).astype(F32)
        row = (lax.broadcasted_iota(jnp.int32, (CHUNK, LAT), 1) % SHARE).astype(F32)

        def chunk(c, _):
            pickone = slot == number + (c * CHUNK).astype(F32)
            hot = jnp.where(pickone, 1.0, 0.0).astype(BF16)
            sh = dot_nt(hot, spread_h[...]).astype(BF16)
            sl = dot_nt(hot, spread_l[...]).astype(BF16)
            first[b, c] = jnp.concatenate([sh, sh, sl], axis=1)
            ih = dot_nt(gain_h[...], hot)
            il = dot_nt(gain_l[...], hot)
            second[b, c] = jnp.concatenate([ih, ih, il], axis=1).astype(BF16)
            lon_c = jnp.sum(jnp.where(pickone, rel, 0.0), axis=1, keepdims=True)
            lat_c = jnp.sum(jnp.where(pickone, lat, 0.0), axis=1, keepdims=True)
            dlon[b, c] = jnp.broadcast_to(-lon_c, (CHUNK, LAT))
            gap = row - lat_c
            base[b, c] = 1.0 - gap * gap * (1.0 / (RADIUS * RADIUS))
            return 0

        lax.fori_loop(0, count, chunk, 0)

    root, scaled, increments = adjust(table[:, pl.ds(0, BATCH)], facts_of[0], 0)
    near_ones(facts_of[0], scaled, increments, 0)

    later = table[:, pl.ds(BATCH, BATCH)]
    mean = jnp.sum(later, axis=0, keepdims=True) * (1.0 / MEMBERS)
    spread = root * (later - mean)
    scaled_t = jnp.transpose(scaled)
    cov = jnp.dot(scaled_t, spread, precision=lax.Precision.HIGHEST, preferred_element_type=F32)
    east = jnp.abs(cols[pl.ds(0, BATCH), 0:1] - facts_of[1][0:1])
    east = jnp.minimum(east, NLON - east)
    up = cols[pl.ds(0, BATCH), 1:2] - facts_of[1][1:2]
    taper = jnp.maximum(1.0 - (east * east + up * up) * (1.0 / (RADIUS * RADIUS)), 0.0)
    later = (mean + spread) + jnp.dot(
        increments, taper * taper * cov, precision=lax.Precision.HIGHEST, preferred_element_type=F32
    )
    root, scaled, increments = adjust(later, facts_of[1], 1)
    near_ones(facts_of[1], scaled, increments, 1)


def filter_obs(place, priors, facts, cols):
    smem = pl.BlockSpec(memory_space=pltpu.SMEM)
    vmem = pl.BlockSpec(memory_space=pltpu.VMEM)
    return pl.pallas_call(
        filter_kernel,
        out_shape=[
            jax.ShapeDtypeStruct((2, CHUNKS, CHUNK, 3 * MEMBERS), BF16),
            jax.ShapeDtypeStruct((2, CHUNKS, MEMBERS, 3 * CHUNK), BF16),
            jax.ShapeDtypeStruct((2, CHUNKS, CHUNK, LAT), F32),
            jax.ShapeDtypeStruct((2, CHUNKS, CHUNK, LAT), F32),
            jax.ShapeDtypeStruct((2,), jnp.int32),
            jax.ShapeDtypeStruct((2,), F32),
        ],
        in_specs=[smem, vmem, vmem, vmem],
        out_specs=[vmem] * 4 + [smem] * 2,
        scratch_shapes=[pltpu.VMEM((MEMBERS, NOBS), F32)] + [pltpu.VMEM((MEMBERS, BATCH), BF16)] * 4,
        compiler_params=pltpu.CompilerParams(vmem_limit_bytes=VMEM_LIMIT),
        name="filter_observations",
    )(place, priors, facts, cols)


def regress_kernel(me_ref, counts, roots, first, second, dlon, base, *rest):
    parts = rest[:8]
    out, state, turned, sems = rest[8:]
    copies = [
        pltpu.make_async_copy(
            parts[d], state.at[pl.ds(0, GROUPS), pl.ds(d * SHARE, SHARE)], sems.at[d]
        )
        for d in range(8)
    ]
    for c in copies:
        c.start()
    state[GROUPS] = jnp.zeros((MEMBERS, LAT), F32)
    lane = lax.broadcasted_iota(jnp.int32, (1, LAT), 1) // SHARE
    me = me_ref[0]
    for c in copies:
        c.wait()

    def lons(g):
        return jnp.where(g < FIELDS * WHOLE, (g % WHOLE) * 8 + lane, WHOLE * 8 + lane % 2).astype(F32)

    def pair(p, _):
        g = 2 * p
        lon = jnp.concatenate([lons(g), lons(g + 1)], axis=1)
        x = jnp.concatenate([state[g], state[g + 1]], axis=1)
        for b in range(2):
            mean = jnp.sum(x, axis=0, keepdims=True) * (1.0 / MEMBERS)
            spread = roots[b] * (x - mean)
            high, low = split(spread)
            stack = jnp.concatenate([high, low, high], axis=0)

            def chunk(c, total):
                cov = jnp.dot(first[b, c], stack, preferred_element_type=F32)
                gap = jnp.concatenate([dlon[b, c]] * 2, axis=1) + lon
                near = jnp.concatenate([base[b, c]] * 2, axis=1)
                taper = jnp.maximum(near - gap * gap * (1.0 / (RADIUS * RADIUS)), 0.0)
                wh, wl = split(taper * taper * cov)
                weights = jnp.concatenate([wh, wl, wh], axis=0)
                return total + jnp.dot(second[b, c], weights, preferred_element_type=F32)

            x = lax.fori_loop(0, counts[b], chunk, mean + spread)
        for half in range(2):
            for d in range(8):
                at = pl.multiple_of((me ^ d) * SHARE, SHARE)
                turned[pl.ds(at, SHARE), :] = x[d * SHARE : (d + 1) * SHARE, half * LAT : (half + 1) * LAT]
            turned[...] = jnp.transpose(turned[...])
            h = g + half

            @pl.when(h < FIELDS * WHOLE)
            def _():
                f, at = h // WHOLE, pl.multiple_of((h % WHOLE) * 8, 8)
                for r in range(SHARE):
                    out[f, r, pl.ds(at, 8), :] = turned[pl.ds(r, 8, stride=SHARE), :]

            @pl.when(h == FIELDS * WHOLE)
            def _():
                for f in range(4):
                    for r in range(SHARE):
                        out[f, r, pl.ds(WHOLE * 8, 2), :] = turned[pl.ds(f * 32 + r, 2, stride=SHARE), :]

            @pl.when(h == FIELDS * WHOLE + 1)
            def _():
                for r in range(SHARE):
                    out[4, r, pl.ds(WHOLE * 8, 2), :] = turned[pl.ds(r, 2, stride=SHARE), :]

        return 0

    lax.fori_loop(0, (GROUPS + 1) // 2, pair, 0)


def regress(me, counts, roots, first, second, dlon, base, parts):
    smem = pl.BlockSpec(memory_space=pltpu.SMEM)
    vmem = pl.BlockSpec(memory_space=pltpu.VMEM)
    return pl.pallas_call(
        regress_kernel,
        out_shape=jax.ShapeDtypeStruct((FIELDS, SHARE, WIDTH, MEMBERS), F32),
        in_specs=[smem] * 3 + [vmem] * 4 + [pl.BlockSpec(memory_space=pl.ANY)] * 8,
        out_specs=vmem,
        scratch_shapes=[
            pltpu.VMEM((GROUPS + 1, MEMBERS, LAT), F32),
            pltpu.VMEM((LAT, MEMBERS), F32),
            pltpu.SemaphoreType.DMA((8,)),
        ],
        compiler_params=pltpu.CompilerParams(vmem_limit_bytes=VMEM_LIMIT),
        name="regress_state",
    )(me, counts, roots, first, second, dlon, base, *parts)


def across(x, axis, bits):
    count = lax.axis_size(axis)
    return lax.ppermute(x, axis, [(i, i ^ bits) for i in range(count)])


def shards(
    ensemble,
    ocean_depth,
    planetary_vorticity,
    land_mask,
    obs_values,
    obs_error,
    obs_lon,
    obs_lat,
    obs_field,
    obs_order,
):
    member, sector = lax.axis_index("member"), lax.axis_index("sector")
    sectors = lax.axis_size("sector")
    me = member.reshape(1)
    sea = land_mask.astype(F32)
    ens = jnp.transpose(ensemble, (1, 2, 0, 3))

    def edge(lo):
        return jnp.concatenate(
            [
                ens[:, lo : lo + EDGE].reshape(FIELDS * EDGE * SHARE, LAT),
                ocean_depth[lo : lo + EDGE],
                sea[lo : lo + EDGE],
            ]
        )

    left = lax.ppermute(edge(WIDTH - EDGE), "sector", [(i, (i + 1) % sectors) for i in range(sectors)])
    right = lax.ppermute(edge(0), "sector", [((i + 1) % sectors, i) for i in range(sectors)])

    lon_f, lat_f = obs_lon.astype(F32), obs_lat.astype(F32)
    facts = in_order(
        obs_order, jnp.stack([lon_f, lat_f, obs_values, obs_error] + [jnp.zeros_like(lon_f)] * 4)
    )
    cols = jnp.transpose(facts, (0, 2, 1)).reshape(NOBS, 8)
    west = sector * WIDTH
    here = obs_lon - west
    cell = jnp.where((here >= 0) & (here < WIDTH), (obs_field - 2) * WIDTH + here, -1)

    *messages, seen = forecast(
        me, ens, left, right, ocean_depth, sea, planetary_vorticity.reshape(1, LAT)
    )
    parts = [messages[0]] + [across(messages[d], "member", d) for d in range(1, 8)]

    priors = pick(obs_order, cell, obs_lat, seen.reshape(3 * WIDTH, SHARE, LAT))
    for k in range(4):
        priors = priors + across(priors, "sector", 1 << k)
    priors = priors[None]
    for k in range(3):
        priors = jnp.concatenate([priors, across(priors, "member", 1 << k)])
    place = jnp.stack([west, member * SHARE])
    first, second, dlon, base, counts, roots = filter_obs(place, priors, facts, cols)
    return regress(me, counts, roots, first, second, dlon, base, parts)


def solution(mesh):
    placed = (
        P("member", None, "sector", None),
        P("sector", None),
        P(),
        P("sector", None),
        P(),
        P(),
        P(),
        P(),
        P(),
        P(),
    )
    return jax.shard_map(
        shards,
        mesh=mesh,
        in_specs=placed,
        out_specs=P(None, "member", "sector", None),
        check_vma=False,
    )
```

```python
import jax
import jax.numpy as jnp
from jax import lax
from jax.experimental import pallas as pl
from jax.experimental.pallas import tpu as pltpu
from jax.sharding import PartitionSpec as P

NLON = 1440
LAT = 128
FIELDS = 5
MEMBERS = 128
NOBS = 1024
BATCH = 512
BLOCKS = NOBS // LAT
RADIUS = 48
SHARE = 16
BANDS = 8
WIDTH = 90
EDGE = 4
INNER = 9
RIGHT = 80
INSIDE = FIELDS * INNER
OUTSIDE = 2 * FIELDS + 2
GROUPS = INSIDE + OUTSIDE
EDGE_ROWS = FIELDS * EDGE * SHARE
CUT = 48
SLOTS = 128
CHUNKS = BATCH // SLOTS
SCALE = 1.0 / (RADIUS * RADIUS)
F32 = jnp.float32
BF16 = jnp.bfloat16
SMEM = pl.BlockSpec(memory_space=pltpu.SMEM)
VMEM = pl.BlockSpec(memory_space=pltpu.VMEM)
ANY = pl.BlockSpec(memory_space=pl.ANY)
PARAMS = pltpu.CompilerParams(vmem_limit_bytes=56 * 1024 * 1024)


def edges_kernel(ens, depth, mask, west, east, sems):
    copies = []
    for i, (out, lon) in enumerate(((west, 0), (east, WIDTH - EDGE))):
        copies.append(
            pltpu.make_async_copy(ens.at[:, pl.ds(lon, EDGE)], out.at[pl.ds(0, FIELDS)], sems.at[i])
        )
        copies[-1].start()
        grids = jnp.concatenate(
            [depth[pl.ds(lon, EDGE), :], mask[pl.ds(lon, EDGE), :].astype(F32)], axis=0
        )
        out[FIELDS, 0, pl.ds(0, 8), :] = grids
    for c in copies:
        c.wait()


def edges(ens, depth, mask):
    side = jax.ShapeDtypeStruct((FIELDS + 1, EDGE, SHARE, LAT), F32)
    return pl.pallas_call(
        edges_kernel,
        out_shape=[side, side],
        in_specs=[ANY, VMEM, VMEM],
        out_specs=[VMEM, VMEM],
        scratch_shapes=[pltpu.SemaphoreType.DMA((2,))],
        compiler_params=PARAMS,
        name="pack_edges",
    )(ens, depth, mask)


def stepper(dep, sea, vort, flux):
    lane = lax.broadcasted_iota(jnp.int32, (SHARE, LAT), 1)
    first, last = lane == 0, lane == LAT - 1
    spin = jnp.broadcast_to(vort[...], (SHARE, LAT))

    def north(a):
        return jnp.where(last, 0.0, pltpu.roll(a, LAT - 1, 1))

    def south(a):
        return jnp.where(first, 0.0, pltpu.roll(a, 1, 1))

    def step(src, dst, lo, hi, row, unroll):
        def flow(e, _):
            u, v, h = src[0, e], src[1, e], src[2, e]
            m = sea[pl.ds(e + row, 1), :]
            un = m * (u + spin * v - 0.15 * (src[2, e + 1] - src[2, e - 1]))
            dst[0, e] = un
            dst[1, e] = m * (v - spin * u - 0.15 * (north(h) - south(h)))
            flux[e] = dep[pl.ds(e + row, 1), :] * un
            return 0

        def others(e, _):
            un, vn = dst[0, e], dst[1, e]
            dv = dep[pl.ds(e + row, 1), :] * vn
            dst[2, e] = src[2, e] - 0.15 * (flux[e + 1] - flux[e - 1] + (north(dv) - south(dv)))
            for c in (3, 4):
                a, ae, aw = src[c, e], src[c, e + 1], src[c, e - 1]
                an, ao = north(a), south(a)
                dst[c, e] = (
                    a
                    - 0.15 * (un * (ae - aw) + vn * (an - ao))
                    + 0.1 * (((ae + aw) + (an + ao)) - 4.0 * a)
                )
            return 0

        lax.fori_loop(lo, hi, flow, 0, unroll=2 * unroll)
        lax.fori_loop(lo + 1, hi - 1, others, 0, unroll=unroll)

    return step


def turn(tiles, out, g):
    tile = jnp.transpose(tiles.reshape(8 * SHARE, LAT))
    for b in range(BANDS):
        out[b, g] = tile[b * SHARE : (b + 1) * SHARE]


def inner_kernel(ens, depth, mask, vort, out, seen, now, nxt, flux, sea, made, sems):
    span = INNER * 8
    load = pltpu.make_async_copy(ens.at[:, pl.ds(EDGE, span + 2 * EDGE)], now, sems.at[0])
    load.start()
    sea[...] = mask[...].astype(F32)
    step = stepper(depth, sea, vort, flux)
    load.wait()
    step(now, nxt, 1, span + 7, EDGE, 4)
    step(nxt, now, 3, span + 5, EDGE, 4)
    keep = pltpu.make_async_copy(
        now.at[pl.ds(2, 3), pl.ds(EDGE, span)], seen.at[:, pl.ds(8, span)], sems.at[1]
    )
    keep.start()

    def field(f, _):
        for i in range(INNER):
            turn(now[f, pl.ds(EDGE + i * 8, 8)], made, f * INNER + i)
        return 0

    lax.fori_loop(0, FIELDS, field, 0)
    send = pltpu.make_async_copy(made, out.at[:, pl.ds(0, INSIDE)], sems.at[0])
    send.start()
    send.wait()
    keep.wait()


def forecast_inner(ens, depth, mask, vort):
    window = INNER * 8 + 2 * EDGE
    return pl.pallas_call(
        inner_kernel,
        out_shape=[
            jax.ShapeDtypeStruct((BANDS, GROUPS, SHARE, LAT), F32),
            jax.ShapeDtypeStruct((3, WIDTH, SHARE, LAT), F32),
        ],
        in_specs=[ANY, VMEM, VMEM, VMEM],
        out_specs=[ANY, ANY],
        scratch_shapes=[
            pltpu.VMEM((FIELDS, window, SHARE, LAT), F32),
            pltpu.VMEM((FIELDS, window, SHARE, LAT), F32),
            pltpu.VMEM((window, SHARE, LAT), F32),
            pltpu.VMEM((WIDTH, LAT), F32),
            pltpu.VMEM((BANDS, INSIDE, SHARE, LAT), F32),
            pltpu.SemaphoreType.DMA((2,)),
        ],
        compiler_params=PARAMS,
        name="forecast_inner",
    )(ens, depth, mask, vort)


def outer_kernel(
    ens, left, right, depth, mask, vort, _, _2, out, seen, now, nxt, flux, dep, sea, made, sems
):
    near, far = 3 * EDGE, 3 * EDGE + 2
    second = near + EDGE
    loads = [
        pltpu.make_async_copy(ens.at[:, pl.ds(0, near)], now.at[:, pl.ds(EDGE, near)], sems.at[0]),
        pltpu.make_async_copy(
            ens.at[:, pl.ds(WIDTH - far, far)], now.at[:, pl.ds(second, far)], sems.at[1]
        ),
        pltpu.make_async_copy(left.at[pl.ds(0, FIELDS)], now.at[:, pl.ds(0, EDGE)], sems.at[2]),
        pltpu.make_async_copy(
            right.at[pl.ds(0, FIELDS)], now.at[:, pl.ds(second + far, EDGE)], sems.at[3]
        ),
    ]
    for c in loads:
        c.start()
    for grid, own, at in ((dep, depth, 0), (sea, mask, EDGE)):
        grid[pl.ds(8, WIDTH), :] = own[...].astype(F32)
        grid[pl.ds(4, EDGE), :] = left[FIELDS, 0, pl.ds(at, EDGE), :]
        grid[pl.ds(8 + WIDTH, EDGE), :] = right[FIELDS, 0, pl.ds(at, EDGE), :]
    step = stepper(dep, sea, vort, flux)
    for c in loads:
        c.wait()
    end = second + far + EDGE
    skip = 8 + WIDTH - far - second
    step(now, nxt, 1, second - 1, 4, 4)
    step(now, nxt, second + 1, end - 1, skip, 4)
    step(nxt, now, 3, second - 3, 4, 4)
    step(nxt, now, second + 3, end - 3, skip, 5)
    right_at = second + EDGE
    keeps = [
        pltpu.make_async_copy(
            now.at[pl.ds(2, 3), pl.ds(EDGE, 8)], seen.at[:, pl.ds(0, 8)], sems.at[1]
        ),
        pltpu.make_async_copy(
            now.at[pl.ds(2, 3), pl.ds(right_at, WIDTH - RIGHT)],
            seen.at[:, pl.ds(RIGHT, WIDTH - RIGHT)],
            sems.at[2],
        ),
    ]
    for c in keeps:
        c.start()
    for f in range(FIELDS):
        turn(now[f, pl.ds(EDGE, 8)], made, 2 * f)
        turn(now[f, pl.ds(right_at, 8)], made, 2 * f + 1)
    turn(now[pl.ds(0, 4), pl.ds(right_at + 8, 2)], made, 2 * FIELDS)
    last = now[4, pl.ds(right_at + 8, 2)]
    turn(jnp.concatenate([last] * 4, axis=0), made, 2 * FIELDS + 1)
    send = pltpu.make_async_copy(made, out.at[:, pl.ds(INSIDE, OUTSIDE)], sems.at[0])
    send.start()
    send.wait()
    for c in keeps:
        c.wait()


def forecast_outer(ens, left, right, depth, mask, vort, messages, seen):
    window = 6 * EDGE + 2 + 2 * EDGE
    return pl.pallas_call(
        outer_kernel,
        out_shape=[
            jax.ShapeDtypeStruct(messages.shape, F32),
            jax.ShapeDtypeStruct(seen.shape, F32),
        ],
        in_specs=[ANY] + [VMEM] * 5 + [ANY] * 2,
        out_specs=[ANY, ANY],
        scratch_shapes=[
            pltpu.VMEM((FIELDS, window, SHARE, LAT), F32),
            pltpu.VMEM((FIELDS, window, SHARE, LAT), F32),
            pltpu.VMEM((window, SHARE, LAT), F32),
            pltpu.VMEM((112, LAT), F32),
            pltpu.VMEM((112, LAT), F32),
            pltpu.VMEM((BANDS, OUTSIDE, SHARE, LAT), F32),
            pltpu.SemaphoreType.DMA((4,)),
        ],
        input_output_aliases={6: 0, 7: 1},
        compiler_params=PARAMS,
        name="forecast_outer",
    )(ens, left, right, depth, mask, vort, messages, seen)


def list_kernel(order, cell, out, count):
    def one(j, n):
        at = cell[order[j]]
        out[n] = at + j * (1 << 16)
        return n + jnp.where(at >= 0, 1, 0)

    count[0] = lax.fori_loop(0, NOBS, one, 0, unroll=8)


def own_list(order, cell):
    return pl.pallas_call(
        list_kernel,
        out_shape=[
            jax.ShapeDtypeStruct((NOBS + LAT,), jnp.int32),
            jax.ShapeDtypeStruct((1,), jnp.int32),
        ],
        in_specs=[SMEM, SMEM],
        out_specs=[SMEM, SMEM],
        compiler_params=PARAMS,
        name="own_observations",
    )(order, cell)


def pick_kernel(own, count, seen, out):
    lane = lax.broadcasted_iota(jnp.int32, (SHARE, LAT), 1)
    out[...] = jnp.zeros_like(out)

    def one(i, _):
        code = own[i]
        j, at, lat = code >> 16, (code >> 7) & 511, code & 127
        tile = pltpu.roll(seen[at], (j - lat) & (LAT - 1), 1)
        b = j >> 7
        out[b] = jnp.where(lane == (j & 127), tile, out[b])
        return 0

    lax.fori_loop(0, count[0], one, 0)


def pick(own, count, seen):
    return pl.pallas_call(
        pick_kernel,
        out_shape=jax.ShapeDtypeStruct((BLOCKS, SHARE, LAT), F32),
        in_specs=[SMEM, SMEM, VMEM],
        out_specs=VMEM,
        compiler_params=PARAMS,
        name="pick_priors",
    )(own, count, seen)


def split(a):
    high = a.astype(BF16)
    return high, (a - high.astype(F32)).astype(BF16)


def sort_kernel(order, facts, out):
    data = facts[...]
    high, rest = split(data)
    left = data - high.astype(F32)
    mid, low = split(left)
    parts = jnp.concatenate([high, mid, low, jnp.zeros_like(rest)], axis=0)
    row = lax.broadcasted_iota(jnp.int32, (NOBS, LAT), 0)

    def block(b, _):
        hot = jnp.where(row == order[b], 1.0, 0.0).astype(BF16)
        got = jnp.dot(parts, hot, preferred_element_type=F32)
        out[b] = got[0:8] + got[8:16] + got[16:24]
        return 0

    lax.fori_loop(0, BLOCKS, block, 0)


def in_order(order, facts):
    return pl.pallas_call(
        sort_kernel,
        out_shape=jax.ShapeDtypeStruct((BLOCKS, 8, LAT), F32),
        in_specs=[VMEM, VMEM],
        out_specs=VMEM,
        compiler_params=PARAMS,
        name="obs_in_batch_order",
    )(order.reshape(BLOCKS, 1, LAT), facts)


def dot_nt(a, b):
    return lax.dot_general(a, b, (((1,), (1,)), ((), ())), preferred_element_type=F32)


def exact(a, b, dims):
    return lax.dot_general(
        a, b, (dims, ((), ())), precision=lax.Precision.HIGHEST, preferred_element_type=F32
    )


def paired(high, low):
    top = jnp.concatenate([high, low], axis=1)
    bottom = jnp.concatenate([high, jnp.zeros_like(low)], axis=1)
    return jnp.concatenate([top, bottom], axis=0).astype(BF16)


def filter_kernel(
    place, priors, facts, lead, link, gain, where, many_lead, many_gain, many_where, counts, roots, table
):
    me = place[2]
    for d in range(BANDS):
        at = pl.multiple_of((me ^ d) * SHARE, SHARE)
        for b in range(BLOCKS):
            table[pl.ds(at, SHARE), pl.ds(b * LAT, LAT)] = priors[d, b]
    west, south = place[0].astype(F32), place[1].astype(F32)
    fact = [jnp.concatenate([facts[b * 4 + i] for i in range(4)], axis=1) for b in range(2)]
    later_than = lax.broadcasted_iota(jnp.int32, (BATCH, BATCH), 0)
    later_than = later_than <= lax.broadcasted_iota(jnp.int32, (BATCH, BATCH), 1)
    upper = jnp.where(later_than, 1.0, 0.0).astype(BF16)

    def adjust(picked, b):
        values, errors = fact[b][2:3], fact[b][3:4]
        mean = jnp.sum(picked, axis=0, keepdims=True) * (1.0 / MEMBERS)
        anomalies = picked - mean
        variance = jnp.sum(anomalies * anomalies, axis=0, keepdims=True) / (MEMBERS - 1) + 1e-6
        innovation = values - mean
        ratio = jnp.sum(innovation * innovation, axis=1, keepdims=True) / jnp.sum(
            variance + errors, axis=1, keepdims=True
        )
        root = jnp.sqrt(ratio)
        inflated = ratio * variance
        spread = root * anomalies
        post_var = 1.0 / (1.0 / inflated + 1.0 / errors)
        post_mean = post_var * (mean / inflated + values / errors)
        increments = post_mean - mean + (jnp.sqrt(post_var / inflated) - 1.0) * spread
        return root, spread / ((MEMBERS - 1) * inflated), increments

    root1, scaled1, inc1 = adjust(table[:, pl.ds(0, BATCH)], 0)

    later = table[:, pl.ds(BATCH, BATCH)]
    mean = jnp.sum(later, axis=0, keepdims=True) * (1.0 / MEMBERS)
    spread = root1 * (later - mean)
    cov = exact(scaled1, spread, ((0,), (0,)))

    def column(a):
        tall = jnp.transpose(jnp.broadcast_to(a, (LAT, BATCH)))
        return jnp.concatenate([tall] * (BATCH // LAT), axis=1)

    east = jnp.abs(column(fact[0][0:1]) - fact[1][0:1])
    east = jnp.minimum(east, NLON - east)
    up = column(fact[0][1:2]) - fact[1][1:2]
    taper = jnp.maximum(1.0 - (east * east + up * up) * SCALE, 0.0)
    later = (mean + spread) + exact(inc1, taper * taper * cov, ((1,), (0,)))
    root2, scaled2, inc2 = adjust(later, 1)
    roots[0] = jnp.sum(root1)
    roots[1] = jnp.sum(root2)

    rel, lat = [], []
    for b in range(2):
        r = fact[b][0:1] - west
        r = jnp.where(r < -float(NLON // 2 - WIDTH // 2), r + NLON, r)
        r = jnp.where(r >= float(NLON // 2 + WIDTH // 2), r - NLON, r)
        rel.append(r)
        lat.append(fact[b][1:2] - south)

    def near(b, lo, hi):
        dl = jnp.maximum(jnp.maximum(lo - rel[b], rel[b] - hi), 0.0)
        dr = jnp.maximum(jnp.maximum(-lat[b], lat[b] - (SHARE - 1.0)), 0.0)
        flag = jnp.where(dl * dl + dr * dr < float(RADIUS * RADIUS), 1.0, 0.0)
        upto = jnp.dot(
            jnp.broadcast_to(flag, (16, BATCH)).astype(BF16), upper, preferred_element_type=F32
        )[0:1]
        return jnp.where(flag > 0.0, upto - 1.0, -float(NOBS)), jnp.sum(flag)

    number = lax.broadcasted_iota(jnp.int32, (SLOTS, BATCH), 0).astype(F32)
    lane = lax.broadcasted_iota(jnp.int32, (1, SLOTS), 1).astype(F32)
    row = lax.broadcasted_iota(jnp.int32, (SHARE, SLOTS), 0).astype(F32)

    def hot(slot, shift):
        return jnp.where(slot == number + shift, 1.0, 0.0).astype(BF16)

    def spot(b, h):
        both = jnp.concatenate(
            [jnp.broadcast_to(rel[b], (8, BATCH)), jnp.broadcast_to(lat[b], (8, BATCH))], axis=0
        )
        high, low = split(both)
        got = dot_nt(high, h) + dot_nt(low, h)
        return got[0:1], got[8:9]

    def placed(lon, up, used):
        gap = row - up
        base = jnp.where(lane < used, 1.0 - gap * gap * SCALE, -1.0)
        return jnp.concatenate([base, jnp.broadcast_to(lon, (8, SLOTS))], axis=0)

    sp1, sp2 = split(root1 * scaled1), split(root1 * root2 * scaled2)
    shift1 = jnp.sum(inc1, axis=0, keepdims=True) * (1.0 / MEMBERS)
    free1 = inc1 - shift1
    g1, g2 = split(root2 * free1 + shift1), split(inc2)
    f1, s2 = split(free1), split(root2 * scaled2)
    full = jnp.float32(0.0)
    for q, (lo, hi) in enumerate(((0.0, CUT - 1.0), (float(CUT), WIDTH - 1.0))):
        slot1, n1 = near(0, lo, hi)
        slot2, n2 = near(1, lo, hi)
        full = jnp.maximum(full, n1 + n2)
        h1, h2 = hot(slot1, 0.0), hot(slot2, -n1)
        lead[q] = paired(*[dot_nt(a, h1) + dot_nt(b, h2) for a, b in zip(sp1, sp2)])
        gain[q] = paired(*[dot_nt(h1, a) + dot_nt(h2, b) for a, b in zip(g1, g2)])
        one = dot_nt(h1, f1[0]) + dot_nt(h1, f1[1])
        two = dot_nt(h2, s2[0]) + dot_nt(h2, s2[1])
        link[q] = paired(*split(exact(one, two, ((1,), (1,)))))
        (lon1, lat1), (lon2, lat2) = spot(0, h1), spot(1, h2)
        where[q] = placed(lon1 + lon2, lat1 + lat2, n1 + n2)
    counts[0] = jnp.where(full > SLOTS, 1, 0)

    @pl.when(full > SLOTS)
    def _():
        for b, (sp, g) in enumerate(((split(scaled1), split(inc1)), (split(scaled2), g2))):
            slot, n = near(b, 0.0, WIDTH - 1.0)
            counts[1 + b] = (n.astype(jnp.int32) + SLOTS - 1) // SLOTS
            for c in range(CHUNKS):
                h = hot(slot, float(c * SLOTS))
                many_lead[b, c] = paired(dot_nt(sp[0], h), dot_nt(sp[1], h))
                many_gain[b, c] = paired(dot_nt(h, g[0]), dot_nt(h, g[1]))
                lon, up = spot(b, h)
                many_where[b, c] = placed(lon, up, n - float(c * SLOTS))


def filter_obs(place, priors, facts):
    square = (2 * SLOTS, 2 * MEMBERS)
    return pl.pallas_call(
        filter_kernel,
        out_shape=[jax.ShapeDtypeStruct((2,) + square, BF16)] * 3
        + [jax.ShapeDtypeStruct((2, SHARE + 8, SLOTS), F32)]
        + [jax.ShapeDtypeStruct((2, CHUNKS) + square, BF16)] * 2
        + [jax.ShapeDtypeStruct((2, CHUNKS, SHARE + 8, SLOTS), F32)]
        + [jax.ShapeDtypeStruct((3,), jnp.int32), jax.ShapeDtypeStruct((2,), F32)],
        in_specs=[SMEM, VMEM, VMEM],
        out_specs=[VMEM] * 7 + [SMEM] * 2,
        scratch_shapes=[pltpu.VMEM((MEMBERS, NOBS), F32)],
        compiler_params=PARAMS,
        name="filter_observations",
    )(place, priors, facts)


def gather_members(tiles, lane):
    v = list(tiles)
    for k in range(3):
        s = SHARE << k
        low = ((lane >> (4 + k)) & 1) == 0
        w = list(v)
        for i in range(8):
            if i & (1 << k):
                continue
            j = i | (1 << k)
            w[i] = jnp.where(low, v[i], pltpu.roll(v[j], s, 1))
            w[j] = jnp.where(low, pltpu.roll(v[i], LAT - s, 1), v[j])
        v = w
    return v


def regress_kernel(
    counts, roots, lead, link, gain, where, many_lead, many_gain, many_where, parts, out, state, made, big, sems
):
    load = pltpu.make_async_copy(parts, state, sems.at[0])
    load.start()
    lane = lax.broadcasted_iota(jnp.int32, (SHARE, LAT), 1)
    load.wait()

    def fetch(g):
        return gather_members([state[s, g] for s in range(8)], lane)

    def matrices(a):
        return jnp.concatenate(split(a), axis=1)

    def product(a, m):
        got = jnp.dot(matrices(a), m, preferred_element_type=F32)
        return got[:, :MEMBERS] + got[:, MEMBERS:]

    def taper(spots, lons):
        base, at = spots[0:SHARE], spots[SHARE : SHARE + 1]
        tiles = []
        for lon in lons:
            gap = at - lon
            t = jnp.maximum(base - gap * gap * SCALE, 0.0)
            tiles.append(t * t)
        return jnp.concatenate(tiles, axis=0)

    def centre(x):
        mean = jnp.sum(x, axis=1, keepdims=True) * (1.0 / MEMBERS)
        return mean, x - mean

    def short(x, lons, q):
        mean, anomaly = centre(x)
        cov = product(anomaly, lead[q])
        t = taper(where[q], lons)
        cov = cov + product(t * cov, link[q])
        return (mean + roots[0] * roots[1] * anomaly) + product(t * cov, gain[q])

    def block(groups, q):
        tiles, lons = [], []
        for g, at in groups:
            tiles += fetch(g)
            lons += [at + j for j in range(8)] if len(groups) > 0 and at is not None else []
        return jnp.concatenate(tiles, axis=0), lons

    def put(f, lon, x, n):
        made[f, pl.ds(lon, n)] = x.reshape(n, SHARE, MEMBERS)

    @pl.when(counts[0] == 0)
    def _():
        def field(f, _):
            for q, lo, n in ((0, 0, 5), (1, 5, 4)):
                groups = [(f * INNER + lo + i, 8.0 * (lo + i + 1)) for i in range(n)]
                x, lons = block(groups, q)
                put(f, 8 * (lo + 1), short(x, lons, q), 8 * n)
            for q, lon in ((0, 0), (1, RIGHT)):
                x, lons = block([(INSIDE + 2 * f + q, float(lon))], q)
                put(f, lon, short(x, lons, q), 8)
            return 0

        lax.fori_loop(0, FIELDS, field, 0)
        tail = [float(RIGHT + 8 + j % 2) for j in range(8)]
        x = short(jnp.concatenate(fetch(GROUPS - 2), axis=0), tail, 1)
        for f in range(4):
            put(f, RIGHT + 8, x[f * 2 * SHARE : (f + 1) * 2 * SHARE], 2)
        x = short(jnp.concatenate(fetch(GROUPS - 1)[:2], axis=0), tail[:2], 1)
        put(4, RIGHT + 8, x, 2)

    @pl.when(counts[0] != 0)
    def _():
        lons_of = [
            (f * INNER + i, f, 8 * (i + 1)) for f in range(FIELDS) for i in range(INNER)
        ]

        def long(x, lons):
            for b in range(2):
                mean, anomaly = centre(x)
                anomaly = roots[b] * anomaly
                big[pl.ds(0, x.shape[0]), :] = mean + anomaly

                def chunk(c, _):
                    t = taper(many_where[b, c], lons)
                    w = t * product(anomaly, many_lead[b, c])
                    big[pl.ds(0, x.shape[0]), :] += product(w, many_gain[b, c])
                    return 0

                lax.fori_loop(0, counts[1 + b], chunk, 0)
                x = big[pl.ds(0, x.shape[0]), :]
            return x

        def each(g, _):
            inside = g < INSIDE
            h = g - INSIDE
            f = jnp.where(inside, g // INNER, h // 2)
            lon = jnp.where(inside, 8 * (g % INNER + 1), RIGHT * (h % 2))
            at = lon.astype(F32)
            x = jnp.concatenate(fetch(g), axis=0)
            put(f, lon, long(x, [at + j for j in range(8)]), 8)
            return 0

        lax.fori_loop(0, GROUPS - 2, each, 0)
        tail = [float(RIGHT + 8 + j % 2) for j in range(8)]
        x = long(jnp.concatenate(fetch(GROUPS - 2), axis=0), tail)
        for f in range(4):
            put(f, RIGHT + 8, x[f * 2 * SHARE : (f + 1) * 2 * SHARE], 2)
        x = long(jnp.concatenate(fetch(GROUPS - 1)[:2], axis=0), tail[:2])
        put(4, RIGHT + 8, x, 2)

    store = pltpu.make_async_copy(made, out, sems.at[0])
    store.start()
    store.wait()


def regress(tables, parts):
    *tables, counts, roots = tables
    return pl.pallas_call(
        regress_kernel,
        out_shape=jax.ShapeDtypeStruct((FIELDS, WIDTH, SHARE, MEMBERS), F32),
        in_specs=[SMEM] * 2 + [VMEM] * 7 + [ANY],
        out_specs=ANY,
        scratch_shapes=[
            pltpu.VMEM((BANDS, GROUPS, SHARE, LAT), F32),
            pltpu.VMEM((FIELDS, WIDTH, SHARE, MEMBERS), F32),
            pltpu.VMEM((8 * SHARE, MEMBERS), F32),
            pltpu.SemaphoreType.DMA((1,)),
        ],
        compiler_params=PARAMS,
        name="regress_state",
    )(counts, roots, *tables, parts)


def across(x, axis, bits):
    count = lax.axis_size(axis)
    return lax.ppermute(x, axis, [(i, i ^ bits) for i in range(count)])


def shards(
    ensemble,
    ocean_depth,
    planetary_vorticity,
    land_mask,
    obs_values,
    obs_error,
    obs_lon,
    obs_lat,
    obs_field,
    obs_order,
):
    member, sector = lax.axis_index("member"), lax.axis_index("sector")
    sectors = lax.axis_size("sector")
    vort = planetary_vorticity.reshape(1, LAT)
    ens = jnp.transpose(ensemble, (1, 2, 0, 3))
    west_side, east_side = edges(ens, ocean_depth, land_mask)
    left = lax.ppermute(east_side, "sector", [(i, (i + 1) % sectors) for i in range(sectors)])
    right = lax.ppermute(west_side, "sector", [((i + 1) % sectors, i) for i in range(sectors)])

    lon_f, lat_f = obs_lon.astype(F32), obs_lat.astype(F32)
    facts = in_order(
        obs_order, jnp.stack([lon_f, lat_f, obs_values, obs_error] + [jnp.zeros_like(lon_f)] * 4)
    )
    west = sector * WIDTH
    here = obs_lon - west
    cell = ((obs_field - 2) * WIDTH + here) * LAT + obs_lat
    own, count = own_list(obs_order, jnp.where((here >= 0) & (here < WIDTH), cell, -1))

    messages, seen = forecast_inner(ens, ocean_depth, land_mask, vort)
    messages, seen = forecast_outer(
        ens, left, right, ocean_depth, land_mask, vort, messages, seen
    )
    parts = lax.all_to_all(messages, "member", split_axis=0, concat_axis=0, tiled=True)

    priors = pick(own, count, seen.reshape(3 * WIDTH, SHARE, LAT))
    for k in range(4):
        priors = priors + across(priors, "sector", 1 << k)
    priors = priors[None]
    for k in range(3):
        priors = jnp.concatenate([priors, across(priors, "member", 1 << k)])
    place = jnp.stack([west, member * SHARE, member])
    analysis = regress(filter_obs(place, priors, facts), parts)
    return jnp.transpose(analysis, (0, 2, 1, 3))


def solution(mesh):
    placed = (
        P("member", None, "sector", None),
        P("sector", None),
        P(),
        P("sector", None),
        P(),
        P(),
        P(),
        P(),
        P(),
        P(),
    )
    return jax.shard_map(
        shards,
        mesh=mesh,
        in_specs=placed,
        out_specs=P(None, "member", "sector", None),
        check_vma=False,
    )
```

```python
import jax
import jax.numpy as jnp
from jax import lax
from jax.experimental import pallas as pl
from jax.experimental.pallas import tpu as pltpu
from jax.sharding import PartitionSpec as P

NLON = 1440
LAT = 128
FIELDS = 5
MEMBERS = 128
NOBS = 1024
BATCH = 512
BLOCKS = NOBS // LAT
RADIUS = 48
SHARE = 16
BANDS = 8
WIDTH = 90
EDGE = 4
INNER = 9
RIGHT = 80
INSIDE = FIELDS * INNER
OUTSIDE = 2 * FIELDS + 2
GROUPS = INSIDE + OUTSIDE
SETS = (GROUPS + 7) // 8
CUT = 48
SLOTS = 128
CHUNKS = BATCH // SLOTS
FLOW, REST = 39, 38
SCALE = 1.0 / (RADIUS * RADIUS)
F32 = jnp.float32
BF16 = jnp.bfloat16
SMEM = pl.BlockSpec(memory_space=pltpu.SMEM)
VMEM = pl.BlockSpec(memory_space=pltpu.VMEM)
ANY = pl.BlockSpec(memory_space=pl.ANY)
PARAMS = pltpu.CompilerParams(vmem_limit_bytes=56 * 1024 * 1024)


def edges_kernel(ens, depth, mask, west, east, sems):
    copies = []
    for i, (out, lon) in enumerate(((west, 0), (east, WIDTH - EDGE))):
        copies.append(
            pltpu.make_async_copy(ens.at[:, pl.ds(lon, EDGE)], out.at[pl.ds(0, FIELDS)], sems.at[i])
        )
        copies[-1].start()
        grids = jnp.concatenate(
            [depth[pl.ds(lon, EDGE), :], mask[pl.ds(lon, EDGE), :].astype(F32)], axis=0
        )
        out[FIELDS, 0, pl.ds(0, 8), :] = grids
    for c in copies:
        c.wait()


def edges(ens, depth, mask):
    side = jax.ShapeDtypeStruct((FIELDS + 1, EDGE, SHARE, LAT), F32)
    return pl.pallas_call(
        edges_kernel,
        out_shape=[side, side],
        in_specs=[ANY, VMEM, VMEM],
        out_specs=[VMEM, VMEM],
        scratch_shapes=[pltpu.SemaphoreType.DMA((2,))],
        compiler_params=PARAMS,
        name="pack_edges",
    )(ens, depth, mask)


def split(a):
    high = a.astype(BF16)
    return high, (a - high.astype(F32)).astype(BF16)


def bands(out):
    row = lax.broadcasted_iota(jnp.int32, (2 * LAT, 2 * LAT), 0) % LAT
    col = lax.broadcasted_iota(jnp.int32, (2 * LAT, 2 * LAT), 1)
    gap = row - col % LAT
    value = jnp.where(jnp.abs(gap) == 1, jnp.where(col < LAT, gap, 1), 0)
    out[...] = value.astype(F32).astype(BF16)


def stepper(dep, sea, vort, flux, band):
    spin = jnp.broadcast_to(vort[...], (SHARE, LAT))

    def halves(tiles):
        return jnp.concatenate(split(jnp.concatenate(tiles, axis=0)), axis=1)

    def difference(tiles):
        got = jnp.dot(halves(tiles), band[:, 0:LAT], preferred_element_type=F32)
        return [got[i * SHARE : (i + 1) * SHARE] for i in range(len(tiles))]

    def both(tiles):
        got = jnp.dot(halves(tiles), band[...], preferred_element_type=F32)
        rows = [got[i * SHARE : (i + 1) * SHARE] for i in range(len(tiles))]
        return [r[:, 0:LAT] for r in rows], [r[:, LAT:] for r in rows]

    def flow(src, dst, places):
        slope = difference([src[2, e] for e, _ in places])
        for (e, row), dh in zip(places, slope):
            u, v = src[0, e], src[1, e]
            m = sea[pl.ds(row, 1), :]
            un = m * (u + spin * v - 0.15 * (src[2, e + 1] - src[2, e - 1]))
            dst[0, e] = un
            dst[1, e] = m * (v - spin * u - 0.15 * dh)
            flux[e] = dep[pl.ds(row, 1), :] * un

    def others(src, dst, places):
        slope = difference([dep[pl.ds(row, 1), :] * dst[1, e] for e, row in places])
        for (e, _), dv in zip(places, slope):
            dst[2, e] = src[2, e] - 0.15 * (flux[e + 1] - flux[e - 1] + dv)
        for c in (3, 4):
            slope, total = both([src[c, e] for e, _ in places])
            for (e, _), dc, around in zip(places, slope, total):
                a, ae, aw = src[c, e], src[c, e + 1], src[c, e - 1]
                dst[c, e] = (
                    a
                    - 0.15 * (dst[0, e] * (ae - aw) + dst[1, e] * dc)
                    + 0.1 * (((ae + aw) + around) - 4.0 * a)
                )

    return flow, others


def in_blocks(stage, src, dst, lo, hi, row, n):
    def block(i, _):
        e = jnp.minimum(lo + i * n, hi - n)
        stage(src, dst, [(e + k, e + k + row) for k in range(n)])
        return 0

    lax.fori_loop(0, (hi - lo + n - 1) // n, block, 0)


def turn(tiles, out, g):
    tile = jnp.transpose(tiles.reshape(8 * SHARE, LAT))
    for b in range(BANDS):
        out[b, g] = tile[b * SHARE : (b + 1) * SHARE]


def inner_kernel(ens, depth, mask, vort, out, seen, now, nxt, flux, sea, band, made, sems):
    span = INNER * 8
    load = pltpu.make_async_copy(ens.at[:, pl.ds(EDGE, span + 2 * EDGE)], now, sems.at[0])
    load.start()
    sea[...] = mask[...].astype(F32)
    bands(band)
    flow, others = stepper(depth, sea, vort, flux, band)
    load.wait()
    in_blocks(flow, now, nxt, 1, span + 7, EDGE, FLOW)
    in_blocks(others, now, nxt, 2, span + 6, EDGE, REST)
    in_blocks(flow, nxt, now, 3, span + 5, EDGE, FLOW)
    in_blocks(others, nxt, now, 4, span + 4, EDGE, REST)
    keep = pltpu.make_async_copy(
        now.at[pl.ds(2, 3), pl.ds(EDGE, span)], seen.at[:, pl.ds(8, span)], sems.at[1]
    )
    keep.start()

    def field(f, _):
        for i in range(INNER):
            turn(now[f, pl.ds(EDGE + i * 8, 8)], made, f * INNER + i)
        return 0

    lax.fori_loop(0, FIELDS, field, 0)
    send = pltpu.make_async_copy(made, out.at[:, pl.ds(0, INSIDE)], sems.at[0])
    send.start()
    send.wait()
    keep.wait()


def forecast_inner(ens, depth, mask, vort):
    window = INNER * 8 + 2 * EDGE
    return pl.pallas_call(
        inner_kernel,
        out_shape=[
            jax.ShapeDtypeStruct((BANDS, GROUPS, SHARE, LAT), F32),
            jax.ShapeDtypeStruct((3, WIDTH, SHARE, LAT), F32),
        ],
        in_specs=[ANY, VMEM, VMEM, VMEM],
        out_specs=[ANY, ANY],
        scratch_shapes=[
            pltpu.VMEM((FIELDS, window, SHARE, LAT), F32),
            pltpu.VMEM((FIELDS, window, SHARE, LAT), F32),
            pltpu.VMEM((window, SHARE, LAT), F32),
            pltpu.VMEM((WIDTH, LAT), F32),
            pltpu.VMEM((2 * LAT, 2 * LAT), BF16),
            pltpu.VMEM((BANDS, INSIDE, SHARE, LAT), F32),
            pltpu.SemaphoreType.DMA((2,)),
        ],
        compiler_params=PARAMS,
        name="forecast_inner",
    )(ens, depth, mask, vort)


def outer_kernel(
    ens, left, right, depth, mask, vort, _, _2, out, seen, now, nxt, flux, dep, sea, band, made, sems
):
    near, far = 3 * EDGE, 3 * EDGE + 2
    second = near + EDGE
    loads = [
        pltpu.make_async_copy(ens.at[:, pl.ds(0, near)], now.at[:, pl.ds(EDGE, near)], sems.at[0]),
        pltpu.make_async_copy(
            ens.at[:, pl.ds(WIDTH - far, far)], now.at[:, pl.ds(second, far)], sems.at[1]
        ),
        pltpu.make_async_copy(left.at[pl.ds(0, FIELDS)], now.at[:, pl.ds(0, EDGE)], sems.at[2]),
        pltpu.make_async_copy(
            right.at[pl.ds(0, FIELDS)], now.at[:, pl.ds(second + far, EDGE)], sems.at[3]
        ),
    ]
    for c in loads:
        c.start()
    for grid, own, at in ((dep, depth, 0), (sea, mask, EDGE)):
        grid[pl.ds(8, WIDTH), :] = own[...].astype(F32)
        grid[pl.ds(4, EDGE), :] = left[FIELDS, 0, pl.ds(at, EDGE), :]
        grid[pl.ds(8 + WIDTH, EDGE), :] = right[FIELDS, 0, pl.ds(at, EDGE), :]
    bands(band)
    flow, others = stepper(dep, sea, vort, flux, band)
    for c in loads:
        c.wait()
    end = second + far + EDGE
    skip = 8 + WIDTH - far - second
    for d, stage, src, dst in (
        (1, flow, now, nxt),
        (2, others, now, nxt),
        (3, flow, nxt, now),
        (4, others, nxt, now),
    ):
        places = [(e, e + 4) for e in range(d, second - d)]
        stage(src, dst, places + [(e, e + skip) for e in range(second + d, end - d)])
    right_at = second + EDGE
    keeps = [
        pltpu.make_async_copy(
            now.at[pl.ds(2, 3), pl.ds(EDGE, 8)], seen.at[:, pl.ds(0, 8)], sems.at[1]
        ),
        pltpu.make_async_copy(
            now.at[pl.ds(2, 3), pl.ds(right_at, WIDTH - RIGHT)],
            seen.at[:, pl.ds(RIGHT, WIDTH - RIGHT)],
            sems.at[2],
        ),
    ]
    for c in keeps:
        c.start()
    for f in range(FIELDS):
        turn(now[f, pl.ds(EDGE, 8)], made, 2 * f)
        turn(now[f, pl.ds(right_at, 8)], made, 2 * f + 1)
    turn(now[pl.ds(0, 4), pl.ds(right_at + 8, 2)], made, 2 * FIELDS)
    last = now[4, pl.ds(right_at + 8, 2)]
    turn(jnp.concatenate([last] * 4, axis=0), made, 2 * FIELDS + 1)
    send = pltpu.make_async_copy(made, out.at[:, pl.ds(INSIDE, OUTSIDE)], sems.at[0])
    send.start()
    for c in [send] + keeps:
        c.wait()


def forecast_outer(ens, left, right, depth, mask, vort, messages, seen):
    window = 6 * EDGE + 2 + 2 * EDGE
    return pl.pallas_call(
        outer_kernel,
        out_shape=[
            jax.ShapeDtypeStruct(messages.shape, F32),
            jax.ShapeDtypeStruct(seen.shape, F32),
        ],
        in_specs=[ANY] + [VMEM] * 5 + [ANY] * 2,
        out_specs=[ANY, ANY],
        scratch_shapes=[
            pltpu.VMEM((FIELDS, window, SHARE, LAT), F32),
            pltpu.VMEM((FIELDS, window, SHARE, LAT), F32),
            pltpu.VMEM((window, SHARE, LAT), F32),
            pltpu.VMEM((112, LAT), F32),
            pltpu.VMEM((112, LAT), F32),
            pltpu.VMEM((2 * LAT, 2 * LAT), BF16),
            pltpu.VMEM((BANDS, OUTSIDE, SHARE, LAT), F32),
            pltpu.SemaphoreType.DMA((4,)),
        ],
        input_output_aliases={6: 0, 7: 1},
        compiler_params=PARAMS,
        name="forecast_outer",
    )(ens, left, right, depth, mask, vort, messages, seen)


def pick_kernel(order, cell, seen, _, _2, out, own):
    lane = lax.broadcasted_iota(jnp.int32, (SHARE, LAT), 1)

    def listed(i, n):
        codes = [cell[order[i * 16 + k]] for k in range(16)]
        for k, at in enumerate(codes):
            own[n] = at + (i * 16 + k) * (1 << 16)
            n = n + jnp.where(at >= 0, 1, 0)
        return n

    total = lax.fori_loop(0, NOBS // 16, listed, 0)
    out[...] = jnp.zeros_like(out)

    def some(i, _):
        found = []
        for k in range(8):
            valid = i * 8 + k < total
            code = jnp.where(valid, own[i * 8 + k], 0)
            j, at, lat = code >> 16, (code >> 7) & 511, code & 127
            tile = pltpu.roll(seen[at], (j - lat) & (LAT - 1), 1)
            found.append((j >> 7, jnp.where(valid, j & 127, -1), tile))
        for b, r, tile in found:
            out[b] = jnp.where(lane == r, tile, out[b])
        return 0

    lax.fori_loop(0, (total + 7) // 8, some, 0)


def pick(order, cell, seen, before):
    return pl.pallas_call(
        pick_kernel,
        out_shape=jax.ShapeDtypeStruct((BLOCKS, SHARE, LAT), F32),
        in_specs=[SMEM, SMEM, VMEM, ANY, ANY],
        out_specs=VMEM,
        scratch_shapes=[pltpu.SMEM((NOBS + 16,), jnp.int32)],
        compiler_params=PARAMS,
        name="pick_priors",
    )(order, cell, seen, *before)


def sort_kernel(order, facts, out):
    data = facts[...]
    high, rest = split(data)
    left = data - high.astype(F32)
    mid, low = split(left)
    parts = jnp.concatenate([high, mid, low, jnp.zeros_like(rest)], axis=0)
    row = lax.broadcasted_iota(jnp.int32, (NOBS, LAT), 0)

    def block(b, _):
        hot = jnp.where(row == order[b], 1.0, 0.0).astype(BF16)
        got = jnp.dot(parts, hot, preferred_element_type=F32)
        out[b] = got[0:8] + got[8:16] + got[16:24]
        return 0

    lax.fori_loop(0, BLOCKS, block, 0)


def in_order(order, facts):
    return pl.pallas_call(
        sort_kernel,
        out_shape=jax.ShapeDtypeStruct((BLOCKS, 8, LAT), F32),
        in_specs=[VMEM, VMEM],
        out_specs=VMEM,
        compiler_params=PARAMS,
        name="obs_in_batch_order",
    )(order.reshape(BLOCKS, 1, LAT), facts)


def dot_nt(a, b):
    return lax.dot_general(a, b, (((1,), (1,)), ((), ())), preferred_element_type=F32)


def exact(a, b, dims):
    return lax.dot_general(
        a, b, (dims, ((), ())), precision=lax.Precision.HIGHEST, preferred_element_type=F32
    )


def paired(high, low):
    top = jnp.concatenate([high, low], axis=1)
    bottom = jnp.concatenate([high, jnp.zeros_like(low)], axis=1)
    return jnp.concatenate([top, bottom], axis=0).astype(BF16)


def filter_kernel(
    place, p0, p1, p2, p3, facts, _, lead, link, gain, where, many_lead, many_gain, many_where, counts, roots, table, long_lead, long_gain, long_where
):
    me = place[2]
    for x, got in enumerate((p0, p1, p2, p3)):
        for z in range(2):
            at = pl.multiple_of((me ^ (4 * z + x)) * SHARE, SHARE)
            for b in range(BLOCKS):
                table[pl.ds(at, SHARE), pl.ds(b * LAT, LAT)] = got[z, b]
    west, south = place[0].astype(F32), place[1].astype(F32)
    fact = [jnp.concatenate([facts[b * 4 + i] for i in range(4)], axis=1) for b in range(2)]
    later_than = lax.broadcasted_iota(jnp.int32, (BATCH, BATCH), 0)
    later_than = later_than <= lax.broadcasted_iota(jnp.int32, (BATCH, BATCH), 1)
    upper = jnp.where(later_than, 1.0, 0.0).astype(BF16)

    def adjust(picked, b):
        values, errors = fact[b][2:3], fact[b][3:4]
        mean = jnp.sum(picked, axis=0, keepdims=True) * (1.0 / MEMBERS)
        anomalies = picked - mean
        variance = jnp.sum(anomalies * anomalies, axis=0, keepdims=True) / (MEMBERS - 1) + 1e-6
        innovation = values - mean
        ratio = jnp.sum(innovation * innovation, axis=1, keepdims=True) / jnp.sum(
            variance + errors, axis=1, keepdims=True
        )
        root = jnp.sqrt(ratio)
        inflated = ratio * variance
        spread = root * anomalies
        post_var = 1.0 / (1.0 / inflated + 1.0 / errors)
        post_mean = post_var * (mean / inflated + values / errors)
        increments = post_mean - mean + (jnp.sqrt(post_var / inflated) - 1.0) * spread
        return root, spread / ((MEMBERS - 1) * inflated), increments

    root1, scaled1, inc1 = adjust(table[:, pl.ds(0, BATCH)], 0)

    later = table[:, pl.ds(BATCH, BATCH)]
    mean = jnp.sum(later, axis=0, keepdims=True) * (1.0 / MEMBERS)
    spread = root1 * (later - mean)
    cov = exact(scaled1, spread, ((0,), (0,)))

    def column(a):
        tall = jnp.transpose(jnp.broadcast_to(a, (LAT, BATCH)))
        return jnp.concatenate([tall] * (BATCH // LAT), axis=1)

    east = jnp.abs(column(fact[0][0:1]) - fact[1][0:1])
    east = jnp.minimum(east, NLON - east)
    up = column(fact[0][1:2]) - fact[1][1:2]
    taper = jnp.maximum(1.0 - (east * east + up * up) * SCALE, 0.0)
    later = (mean + spread) + exact(inc1, taper * taper * cov, ((1,), (0,)))
    root2, scaled2, inc2 = adjust(later, 1)
    roots[0] = jnp.sum(root1)
    roots[1] = jnp.sum(root2)

    rel, lat = [], []
    for b in range(2):
        r = fact[b][0:1] - west
        r = jnp.where(r < -float(NLON // 2 - WIDTH // 2), r + NLON, r)
        r = jnp.where(r >= float(NLON // 2 + WIDTH // 2), r - NLON, r)
        rel.append(r)
        lat.append(fact[b][1:2] - south)

    def near(b, lo, hi):
        dl = jnp.maximum(jnp.maximum(lo - rel[b], rel[b] - hi), 0.0)
        dr = jnp.maximum(jnp.maximum(-lat[b], lat[b] - (SHARE - 1.0)), 0.0)
        flag = jnp.where(dl * dl + dr * dr < float(RADIUS * RADIUS), 1.0, 0.0)
        upto = jnp.dot(
            jnp.broadcast_to(flag, (16, BATCH)).astype(BF16), upper, preferred_element_type=F32
        )[0:1]
        return jnp.where(flag > 0.0, upto - 1.0, -float(NOBS)), jnp.sum(flag)

    number = lax.broadcasted_iota(jnp.int32, (SLOTS, BATCH), 0).astype(F32)
    lane = lax.broadcasted_iota(jnp.int32, (1, SLOTS), 1).astype(F32)
    row = lax.broadcasted_iota(jnp.int32, (SHARE, SLOTS), 0).astype(F32)

    def hot(slot, shift):
        return jnp.where(slot == number + shift, 1.0, 0.0).astype(BF16)

    def spot(b, h):
        both = jnp.concatenate(
            [jnp.broadcast_to(rel[b], (8, BATCH)), jnp.broadcast_to(lat[b], (8, BATCH))], axis=0
        )
        high, low = split(both)
        got = dot_nt(high, h) + dot_nt(low, h)
        return got[0:1], got[8:9]

    def placed(lon, up, used):
        gap = row - up
        base = jnp.where(lane < used, 1.0 - gap * gap * SCALE, -1.0)
        return jnp.concatenate([base, jnp.broadcast_to(lon, (8, SLOTS))], axis=0)

    sp1, sp2 = split(root1 * scaled1), split(root1 * root2 * scaled2)
    shift1 = jnp.sum(inc1, axis=0, keepdims=True) * (1.0 / MEMBERS)
    free1 = inc1 - shift1
    g1, g2 = split(root2 * free1 + shift1), split(inc2)
    f1, s2 = split(free1), split(root2 * scaled2)
    full = jnp.float32(0.0)
    for q, (lo, hi) in enumerate(((0.0, CUT - 1.0), (float(CUT), WIDTH - 1.0))):
        slot1, n1 = near(0, lo, hi)
        slot2, n2 = near(1, lo, hi)
        full = jnp.maximum(full, n1 + n2)
        h1, h2 = hot(slot1, 0.0), hot(slot2, -n1)
        lead[q] = paired(*[dot_nt(a, h1) + dot_nt(b, h2) for a, b in zip(sp1, sp2)])
        gain[q] = paired(*[dot_nt(h1, a) + dot_nt(h2, b) for a, b in zip(g1, g2)])
        one = dot_nt(h1, f1[0]) + dot_nt(h1, f1[1])
        two = dot_nt(h2, s2[0]) + dot_nt(h2, s2[1])
        link[q] = paired(*split(exact(one, two, ((1,), (1,)))))
        (lon1, lat1), (lon2, lat2) = spot(0, h1), spot(1, h2)
        where[q] = placed(lon1 + lon2, lat1 + lat2, n1 + n2)
    counts[0] = jnp.where(full > SLOTS, 1, 0)

    @pl.when(full > SLOTS)
    def _():
        for b, (sp, g) in enumerate(((split(scaled1), split(inc1)), (split(scaled2), g2))):
            slot, n = near(b, 0.0, WIDTH - 1.0)
            counts[1 + b] = (n.astype(jnp.int32) + SLOTS - 1) // SLOTS
            for c in range(CHUNKS):
                h = hot(slot, float(c * SLOTS))
                long_lead[b, c] = paired(dot_nt(sp[0], h), dot_nt(sp[1], h))
                long_gain[b, c] = paired(dot_nt(h, g[0]), dot_nt(h, g[1]))
                lon, up = spot(b, h)
                long_where[b, c] = placed(lon, up, n - float(c * SLOTS))
        pltpu.sync_copy(long_lead, many_lead)
        pltpu.sync_copy(long_gain, many_gain)
        pltpu.sync_copy(long_where, many_where)


def filter_obs(place, priors, facts, before):
    square = (2 * SLOTS, 2 * MEMBERS)
    return pl.pallas_call(
        filter_kernel,
        out_shape=[jax.ShapeDtypeStruct((2,) + square, BF16)] * 3
        + [jax.ShapeDtypeStruct((2, SHARE + 8, SLOTS), F32)]
        + [jax.ShapeDtypeStruct((2, CHUNKS) + square, BF16)] * 2
        + [jax.ShapeDtypeStruct((2, CHUNKS, SHARE + 8, SLOTS), F32)]
        + [jax.ShapeDtypeStruct((3,), jnp.int32), jax.ShapeDtypeStruct((2,), F32)],
        in_specs=[SMEM] + [VMEM] * 5 + [ANY],
        out_specs=[VMEM] * 4 + [ANY] * 3 + [SMEM] * 2,
        scratch_shapes=[
            pltpu.VMEM((MEMBERS, NOBS), F32),
            pltpu.VMEM((2, CHUNKS) + square, BF16),
            pltpu.VMEM((2, CHUNKS) + square, BF16),
            pltpu.VMEM((2, CHUNKS, SHARE + 8, SLOTS), F32),
        ],
        compiler_params=PARAMS,
        name="filter_observations",
    )(place, *priors, facts, before)


def arrange_kernel(parts, full, free, state, mid, made, halves, sems, stores):
    sets = [(g, min(8, GROUPS - g)) for g in range(0, GROUPS, 8)]
    loads = [
        pltpu.make_async_copy(parts.at[:, pl.ds(g, n)], state.at[:, pl.ds(g, n)], sems.at[t])
        for t, (g, n) in enumerate(sets)
    ]
    for c in loads:
        c.start()
    saves = []
    for t, (g, n) in enumerate(sets):
        loads[t].wait()
        for s in range(8):
            tile = jnp.transpose(state[s, pl.ds(g, 8)].reshape(8 * SHARE, LAT))
            for j in range(8):
                mid[j, pl.ds(s * SHARE, SHARE), :] = tile[j * SHARE : (j + 1) * SHARE]
        for j in range(8):
            tile = mid[j]
            mean = jnp.sum(tile, axis=0, keepdims=True) * (1.0 / MEMBERS)
            value = jnp.transpose(tile)
            pair = jnp.concatenate(split(jnp.transpose(tile - mean)), axis=1)
            for i in range(n):
                made[g + i, j] = value[i * SHARE : (i + 1) * SHARE]
                halves[g + i, j] = pair[i * SHARE : (i + 1) * SHARE]
        for k, (a, b) in enumerate(((made, full), (halves, free))):
            saves.append(
                pltpu.make_async_copy(a.at[pl.ds(g, n)], b.at[pl.ds(g, n)], stores.at[t, k])
            )
            saves[-1].start()
    for c in saves:
        c.wait()


def arrange(parts):
    shapes = [
        jax.ShapeDtypeStruct((GROUPS, 8, SHARE, MEMBERS), F32),
        jax.ShapeDtypeStruct((GROUPS, 8, SHARE, 2 * MEMBERS), BF16),
    ]
    return pl.pallas_call(
        arrange_kernel,
        out_shape=shapes,
        in_specs=[ANY],
        out_specs=[ANY, ANY],
        scratch_shapes=[
            pltpu.VMEM((BANDS, SETS * 8, SHARE, LAT), F32),
            pltpu.VMEM((8, MEMBERS, LAT), F32),
            pltpu.VMEM(shapes[0].shape, F32),
            pltpu.VMEM(shapes[1].shape, BF16),
            pltpu.SemaphoreType.DMA((SETS,)),
            pltpu.SemaphoreType.DMA((SETS, 2)),
        ],
        compiler_params=PARAMS,
        name="arrange_members",
    )(parts)


def regress_kernel(
    counts, roots, lead, link, gain, where, many_lead, many_gain, many_where, full_all, free_all, out,
    full, free, made, big, long_lead, long_gain, long_where, sems, stores
):
    def copies(at, sem):
        return (
            pltpu.make_async_copy(full_all.at[at], full.at[at], sem.at[0]),
            pltpu.make_async_copy(free_all.at[at], free.at[at], sem.at[1]),
        )

    def inside(f):
        return copies(pl.ds(f * INNER, INNER), sems.at[f])

    outside = copies(pl.ds(INSIDE, OUTSIDE), sems.at[FIELDS])
    for c in outside:
        c.start()
    for f in range(FIELDS):
        for c in inside(f):
            c.start()
    for c in outside:
        c.wait()

    def matrices(a):
        return jnp.concatenate(split(a), axis=1)

    def times(pair, m):
        got = jnp.dot(pair, m, preferred_element_type=F32)
        return got[:, :MEMBERS] + got[:, MEMBERS:]

    def product(a, m):
        return times(matrices(a), m)

    def taper(spots, lons):
        base, at = spots[0:SHARE], spots[SHARE : SHARE + 1]
        tiles = []
        for lon in lons:
            gap = at - lon
            t = jnp.maximum(base - gap * gap * SCALE, 0.0)
            tiles.append(t * t)
        return jnp.concatenate(tiles, axis=0)

    def short(x, pair, lons, q):
        cov = times(pair, lead[q])
        t = taper(where[q], lons)
        cov = cov + product(t * cov, link[q])
        anomaly = pair[:, :MEMBERS].astype(F32) + pair[:, MEMBERS:].astype(F32)
        return (x + (roots[0] * roots[1] - 1.0) * anomaly) + product(t * cov, gain[q])

    def block(g, n, lons=8):
        rows = n * lons * SHARE
        if lons == 8:
            x, pair = full[pl.ds(g, n)], free[pl.ds(g, n)]
        else:
            x, pair = full[g, pl.ds(0, lons)], free[g, pl.ds(0, lons)]
        return x.reshape(rows, MEMBERS), pair.reshape(rows, 2 * MEMBERS)

    def put(f, lon, x, n):
        made[f, pl.ds(lon, n)] = x.reshape(n, SHARE, MEMBERS)

    def store(f):
        return pltpu.make_async_copy(made.at[f], out.at[f], stores.at[f])

    tail = [float(RIGHT + 8 + j % 2) for j in range(8)]

    @pl.when(counts[0] == 0)
    def _():
        x = short(*block(GROUPS - 2, 1), tail, 1)
        for f in range(4):
            put(f, RIGHT + 8, x[f * 2 * SHARE : (f + 1) * 2 * SHARE], 2)
        put(4, RIGHT + 8, short(*block(GROUPS - 1, 1, 2), tail[:2], 1), 2)

        def field(f, _):
            for c in inside(f):
                c.wait()
            for q, lo, n in ((0, 0, 5), (1, 5, 4)):
                lons = [8.0 * (lo + 1) + i for i in range(8 * n)]
                put(f, 8 * (lo + 1), short(*block(f * INNER + lo, n), lons, q), 8 * n)
            for q, lon in ((0, 0), (1, RIGHT)):
                lons = [float(lon + i) for i in range(8)]
                put(f, lon, short(*block(INSIDE + 2 * f + q, 1), lons, q), 8)
            store(f).start()
            return 0

        lax.fori_loop(0, FIELDS, field, 0)

    @pl.when(counts[0] != 0)
    def _():
        for f in range(FIELDS):
            for c in inside(f):
                c.wait()
        pltpu.sync_copy(many_lead, long_lead)
        pltpu.sync_copy(many_gain, long_gain)
        pltpu.sync_copy(many_where, long_where)

        def long(x, _, lons):
            for b in range(2):
                mean = jnp.sum(x, axis=1, keepdims=True) * (1.0 / MEMBERS)
                anomaly = x - mean
                big[pl.ds(0, x.shape[0]), :] = x + (roots[b] - 1.0) * anomaly
                anomaly = roots[b] * anomaly

                def chunk(c, _):
                    t = taper(long_where[b, c], lons)
                    w = t * product(anomaly, long_lead[b, c])
                    big[pl.ds(0, x.shape[0]), :] += product(w, long_gain[b, c])
                    return 0

                lax.fori_loop(0, counts[1 + b], chunk, 0)
                x = big[pl.ds(0, x.shape[0]), :]
            return x

        def each(g, _):
            inner = g < INSIDE
            h = g - INSIDE
            f = jnp.where(inner, g // INNER, h // 2)
            lon = jnp.where(inner, 8 * (g % INNER + 1), RIGHT * (h % 2))
            at = lon.astype(F32)
            put(f, lon, long(*block(g, 1), [at + j for j in range(8)]), 8)
            return 0

        lax.fori_loop(0, GROUPS - 2, each, 0)
        x = long(*block(GROUPS - 2, 1), tail)
        for f in range(4):
            put(f, RIGHT + 8, x[f * 2 * SHARE : (f + 1) * 2 * SHARE], 2)
        put(4, RIGHT + 8, long(*block(GROUPS - 1, 1, 2), tail[:2]), 2)
        for f in range(FIELDS):
            store(f).start()

    for f in range(FIELDS):
        store(f).wait()


def regress(tables, state):
    *tables, counts, roots = tables
    square = (2, CHUNKS, 2 * SLOTS, 2 * MEMBERS)
    return pl.pallas_call(
        regress_kernel,
        out_shape=jax.ShapeDtypeStruct((FIELDS, WIDTH, SHARE, MEMBERS), F32),
        in_specs=[SMEM] * 2 + [VMEM] * 4 + [ANY] * 5,
        out_specs=ANY,
        scratch_shapes=[
            pltpu.VMEM((GROUPS, 8, SHARE, MEMBERS), F32),
            pltpu.VMEM((GROUPS, 8, SHARE, 2 * MEMBERS), BF16),
            pltpu.VMEM((FIELDS, WIDTH, SHARE, MEMBERS), F32),
            pltpu.VMEM((8 * SHARE, MEMBERS), F32),
            pltpu.VMEM(square, BF16),
            pltpu.VMEM(square, BF16),
            pltpu.VMEM((2, CHUNKS, SHARE + 8, SLOTS), F32),
            pltpu.SemaphoreType.DMA((FIELDS + 1, 2)),
            pltpu.SemaphoreType.DMA((FIELDS,)),
        ],
        compiler_params=PARAMS,
        name="regress_state",
    )(counts, roots, *tables, *state)


def across(x, axis, bits):
    count = lax.axis_size(axis)
    return lax.ppermute(x, axis, [(i, i ^ bits) for i in range(count)])


def shards(
    ensemble,
    ocean_depth,
    planetary_vorticity,
    land_mask,
    obs_values,
    obs_error,
    obs_lon,
    obs_lat,
    obs_field,
    obs_order,
):
    member, sector = lax.axis_index("member"), lax.axis_index("sector")
    sectors = lax.axis_size("sector")
    vort = planetary_vorticity.reshape(1, LAT)
    ens = jnp.transpose(ensemble, (1, 2, 0, 3))
    west_side, east_side = edges(ens, ocean_depth, land_mask)
    left = lax.ppermute(east_side, "sector", [(i, (i + 1) % sectors) for i in range(sectors)])
    right = lax.ppermute(west_side, "sector", [((i + 1) % sectors, i) for i in range(sectors)])

    lon_f, lat_f = obs_lon.astype(F32), obs_lat.astype(F32)
    facts = in_order(
        obs_order, jnp.stack([lon_f, lat_f, obs_values, obs_error] + [jnp.zeros_like(lon_f)] * 4)
    )
    west = sector * WIDTH
    here = obs_lon - west
    cell = ((obs_field - 2) * WIDTH + here) * LAT + obs_lat
    cell = jnp.where((here >= 0) & (here < WIDTH), cell, -1)
    place = jnp.stack([west, member * SHARE, member])

    messages, seen = forecast_inner(ens, ocean_depth, land_mask, vort)
    messages, seen = forecast_outer(
        ens, left, right, ocean_depth, land_mask, vort, messages, seen
    )
    parts = lax.all_to_all(messages, "member", split_axis=0, concat_axis=0, tiled=True)

    priors = pick(obs_order, cell, seen.reshape(3 * WIDTH, SHARE, LAT), [facts, place])
    for bit in (2, 4, 1):
        priors = priors + across(priors, "sector", bit)
    both = ("member", "sector")
    count = lax.axis_size("member") * sectors
    crossed = lax.ppermute(priors, both, [(i, i ^ (4 * sectors + 8)) for i in range(count)])
    priors = jnp.stack(
        [priors + across(priors, "sector", 8), across(priors, "member", 4) + crossed]
    )
    priors = [priors] + [across(priors, "member", x) for x in (1, 2, 3)]
    state = arrange(parts)
    analysis = regress(filter_obs(place, priors, facts, state[0]), state)
    return jnp.transpose(analysis, (0, 2, 1, 3))


def solution(mesh):
    placed = (
        P("member", None, "sector", None),
        P("sector", None),
        P(),
        P("sector", None),
        P(),
        P(),
        P(),
        P(),
        P(),
        P(),
    )
    return jax.shard_map(
        shards,
        mesh=mesh,
        in_specs=placed,
        out_specs=P(None, "member", "sector", None),
        check_vma=False,
    )
```

```python
import jax
import jax.numpy as jnp
from jax import lax
from jax.experimental import pallas as pl
from jax.experimental.pallas import tpu as pltpu
from jax.sharding import PartitionSpec as P

NLON = 1440
LAT = 128
FIELDS = 5
MEMBERS = 128
NOBS = 1024
BATCH = 512
BLOCKS = NOBS // LAT
RADIUS = 48
SHARE = 16
BANDS = 8
WIDTH = 90
EDGE = 4
INNER = 9
RIGHT = 80
INSIDE = FIELDS * INNER
OUTSIDE = 2 * FIELDS + 2
GROUPS = INSIDE + OUTSIDE
SETS = (GROUPS + 7) // 8
CUT = 48
SLOTS = 128
CHUNKS = BATCH // SLOTS
MEAN = SLOTS - 1
FLOW, REST = 39, 38
SCALE = 1.0 / (RADIUS * RADIUS)
F32 = jnp.float32
BF16 = jnp.bfloat16
SMEM = pl.BlockSpec(memory_space=pltpu.SMEM)
VMEM = pl.BlockSpec(memory_space=pltpu.VMEM)
ANY = pl.BlockSpec(memory_space=pl.ANY)
PARAMS = pltpu.CompilerParams(vmem_limit_bytes=56 * 1024 * 1024)


def edges_kernel(ens, depth, mask, west, east, deep, sea, sems):
    sides = ((west, 0), (east, WIDTH - EDGE))
    grids = ((0, 0, 8), (RIGHT, 8, WIDTH - RIGHT))
    copies = [
        pltpu.make_async_copy(ens.at[:, pl.ds(lon, EDGE)], out.at[pl.ds(0, FIELDS)], sems.at[i])
        for i, (out, lon) in enumerate(sides)
    ]
    for i, (lon, at, n) in enumerate(grids):
        for j, (grid, to) in enumerate(((depth, deep), (mask, sea))):
            copies.append(
                pltpu.make_async_copy(
                    grid.at[pl.ds(lon, n)], to.at[pl.ds(at, n)], sems.at[2 + 2 * i + j]
                )
            )
    for c in copies:
        c.start()
    for c in copies:
        c.wait()
    for (out, lon), (start, at, _) in zip(sides, grids):
        rows = pl.ds(at + lon - start, EDGE)
        out[FIELDS, 0, pl.ds(0, 8), :] = jnp.concatenate([deep[rows, :], sea[rows, :].astype(F32)], axis=0)


def edges(ens, depth, mask):
    side = jax.ShapeDtypeStruct((FIELDS + 1, EDGE, SHARE, LAT), F32)
    return pl.pallas_call(
        edges_kernel,
        out_shape=[side, side],
        in_specs=[ANY, ANY, ANY],
        out_specs=[VMEM, VMEM],
        scratch_shapes=[
            pltpu.VMEM((24, LAT), F32),
            pltpu.VMEM((24, LAT), jnp.int32),
            pltpu.SemaphoreType.DMA((6,)),
        ],
        compiler_params=PARAMS,
        name="pack_edges",
    )(ens, depth, mask)


def split(a):
    high = a.astype(BF16)
    return high, (a - high.astype(F32)).astype(BF16)


def bands(out):
    row = lax.broadcasted_iota(jnp.int32, (2 * LAT, 2 * LAT), 0) % LAT
    col = lax.broadcasted_iota(jnp.int32, (2 * LAT, 2 * LAT), 1)
    gap = row - col % LAT
    value = jnp.where(jnp.abs(gap) == 1, jnp.where(col < LAT, gap, 1), 0)
    out[...] = value.astype(F32).astype(BF16)


def stepper(dep, sea, vort, flux, band):
    spin = jnp.broadcast_to(vort[...], (SHARE, LAT))

    def halves(tiles):
        return jnp.concatenate(split(jnp.concatenate(tiles, axis=0)), axis=1)

    def difference(tiles):
        got = jnp.dot(halves(tiles), band[:, 0:LAT], preferred_element_type=F32)
        return [got[i * SHARE : (i + 1) * SHARE] for i in range(len(tiles))]

    def both(tiles):
        got = jnp.dot(halves(tiles), band[...], preferred_element_type=F32)
        rows = [got[i * SHARE : (i + 1) * SHARE] for i in range(len(tiles))]
        return [r[:, 0:LAT] for r in rows], [r[:, LAT:] for r in rows]

    def flow(src, dst, places):
        slope = difference([src[2, e] for e, _ in places])
        for (e, row), dh in zip(places, slope):
            u, v = src[0, e], src[1, e]
            m = sea[pl.ds(row, 1), :]
            un = m * (u + spin * v - 0.15 * (src[2, e + 1] - src[2, e - 1]))
            dst[0, e] = un
            dst[1, e] = m * (v - spin * u - 0.15 * dh)
            flux[e] = dep[pl.ds(row, 1), :] * un

    def others(src, dst, places):
        slope = difference([dep[pl.ds(row, 1), :] * dst[1, e] for e, row in places])
        for (e, _), dv in zip(places, slope):
            dst[2, e] = src[2, e] - 0.15 * (flux[e + 1] - flux[e - 1] + dv)
        for c in (3, 4):
            slope, total = both([src[c, e] for e, _ in places])
            for (e, _), dc, around in zip(places, slope, total):
                a, ae, aw = src[c, e], src[c, e + 1], src[c, e - 1]
                dst[c, e] = (
                    a
                    - 0.15 * (dst[0, e] * (ae - aw) + dst[1, e] * dc)
                    + 0.1 * (((ae + aw) + around) - 4.0 * a)
                )

    return flow, others


def in_blocks(stage, src, dst, lo, hi, row, n):
    def block(i, _):
        e = jnp.minimum(lo + i * n, hi - n)
        stage(src, dst, [(e + k, e + k + row) for k in range(n)])
        return 0

    lax.fori_loop(0, (hi - lo + n - 1) // n, block, 0)


def turn(tiles, out, g):
    tile = jnp.transpose(tiles.reshape(8 * SHARE, LAT))
    for b in range(BANDS):
        out[b, g] = tile[b * SHARE : (b + 1) * SHARE]


def inner_kernel(ens, depth, mask, vort, out, seen, now, nxt, flux, sea, band, made, sems):
    span = INNER * 8
    first = FLOW + 2
    loads = [
        pltpu.make_async_copy(
            ens.at[:, pl.ds(EDGE + at, n)], now.at[:, pl.ds(at, n)], sems.at[2 + i]
        )
        for i, (at, n) in enumerate(((0, first), (first, span + 2 * EDGE - first)))
    ]
    for c in loads:
        c.start()
    sea[...] = mask[...].astype(F32)
    bands(band)
    flow, others = stepper(depth, sea, vort, flux, band)
    for at, c in zip((1, 1 + FLOW), loads):
        c.wait()
        flow(now, nxt, [(at + k, at + k + EDGE) for k in range(FLOW)])
    in_blocks(others, now, nxt, 2, span + 6, EDGE, REST)
    in_blocks(flow, nxt, now, 3, span + 5, EDGE, FLOW)
    in_blocks(others, nxt, now, 4, span + 4, EDGE, REST)
    keep = pltpu.make_async_copy(
        now.at[pl.ds(2, 3), pl.ds(EDGE, span)], seen.at[:, pl.ds(8, span)], sems.at[1]
    )
    keep.start()

    def send(f):
        at = pl.ds(f * INNER, INNER)
        return pltpu.make_async_copy(made.at[:, at], out.at[:, at], sems.at[2 + f])

    def field(f, _):
        for i in range(INNER):
            turn(now[f, pl.ds(EDGE + i * 8, 8)], made, f * INNER + i)
        send(f).start()
        return 0

    lax.fori_loop(0, FIELDS, field, 0)
    for f in range(FIELDS):
        send(f).wait()
    keep.wait()


def forecast_inner(ens, depth, mask, vort):
    window = INNER * 8 + 2 * EDGE
    return pl.pallas_call(
        inner_kernel,
        out_shape=[
            jax.ShapeDtypeStruct((BANDS, GROUPS, SHARE, LAT), F32),
            jax.ShapeDtypeStruct((3, WIDTH, SHARE, LAT), F32),
        ],
        in_specs=[ANY, VMEM, VMEM, VMEM],
        out_specs=[ANY, ANY],
        scratch_shapes=[
            pltpu.VMEM((FIELDS, window, SHARE, LAT), F32),
            pltpu.VMEM((FIELDS, window, SHARE, LAT), F32),
            pltpu.VMEM((window, SHARE, LAT), F32),
            pltpu.VMEM((WIDTH, LAT), F32),
            pltpu.VMEM((2 * LAT, 2 * LAT), BF16),
            pltpu.VMEM((BANDS, INSIDE, SHARE, LAT), F32),
            pltpu.SemaphoreType.DMA((2 + FIELDS,)),
        ],
        compiler_params=PARAMS,
        name="forecast_inner",
    )(ens, depth, mask, vort)


def outer_kernel(
    ens, left, right, depth, mask, vort, _, _2, out, seen, now, nxt, flux, dep, sea, band, made, sems
):
    near, far = 3 * EDGE, 3 * EDGE + 2
    second = near + EDGE
    loads = [
        pltpu.make_async_copy(ens.at[:, pl.ds(0, near)], now.at[:, pl.ds(EDGE, near)], sems.at[0]),
        pltpu.make_async_copy(
            ens.at[:, pl.ds(WIDTH - far, far)], now.at[:, pl.ds(second, far)], sems.at[1]
        ),
        pltpu.make_async_copy(left.at[pl.ds(0, FIELDS)], now.at[:, pl.ds(0, EDGE)], sems.at[2]),
        pltpu.make_async_copy(
            right.at[pl.ds(0, FIELDS)], now.at[:, pl.ds(second + far, EDGE)], sems.at[3]
        ),
    ]
    for c in loads:
        c.start()
    for grid, own, at in ((dep, depth, 0), (sea, mask, EDGE)):
        grid[pl.ds(8, WIDTH), :] = own[...].astype(F32)
        grid[pl.ds(4, EDGE), :] = left[FIELDS, 0, pl.ds(at, EDGE), :]
        grid[pl.ds(8 + WIDTH, EDGE), :] = right[FIELDS, 0, pl.ds(at, EDGE), :]
    bands(band)
    flow, others = stepper(dep, sea, vort, flux, band)
    for c in loads:
        c.wait()
    end = second + far + EDGE
    skip = 8 + WIDTH - far - second
    for d, stage, src, dst in (
        (1, flow, now, nxt),
        (2, others, now, nxt),
        (3, flow, nxt, now),
        (4, others, nxt, now),
    ):
        places = [(e, e + 4) for e in range(d, second - d)]
        stage(src, dst, places + [(e, e + skip) for e in range(second + d, end - d)])
    right_at = second + EDGE
    keeps = [
        pltpu.make_async_copy(
            now.at[pl.ds(2, 3), pl.ds(EDGE, 8)], seen.at[:, pl.ds(0, 8)], sems.at[1]
        ),
        pltpu.make_async_copy(
            now.at[pl.ds(2, 3), pl.ds(right_at, WIDTH - RIGHT)],
            seen.at[:, pl.ds(RIGHT, WIDTH - RIGHT)],
            sems.at[2],
        ),
    ]
    for c in keeps:
        c.start()
    for f in range(FIELDS):
        turn(now[f, pl.ds(EDGE, 8)], made, 2 * f)
        turn(now[f, pl.ds(right_at, 8)], made, 2 * f + 1)
    turn(now[pl.ds(0, 4), pl.ds(right_at + 8, 2)], made, 2 * FIELDS)
    last = now[4, pl.ds(right_at + 8, 2)]
    turn(jnp.concatenate([last] * 4, axis=0), made, 2 * FIELDS + 1)
    send = pltpu.make_async_copy(made, out.at[:, pl.ds(INSIDE, OUTSIDE)], sems.at[0])
    send.start()
    for c in [send] + keeps:
        c.wait()


def forecast_outer(ens, left, right, depth, mask, vort, messages, seen):
    window = 6 * EDGE + 2 + 2 * EDGE
    return pl.pallas_call(
        outer_kernel,
        out_shape=[
            jax.ShapeDtypeStruct(messages.shape, F32),
            jax.ShapeDtypeStruct(seen.shape, F32),
        ],
        in_specs=[ANY] + [VMEM] * 5 + [ANY] * 2,
        out_specs=[ANY, ANY],
        scratch_shapes=[
            pltpu.VMEM((FIELDS, window, SHARE, LAT), F32),
            pltpu.VMEM((FIELDS, window, SHARE, LAT), F32),
            pltpu.VMEM((window, SHARE, LAT), F32),
            pltpu.VMEM((112, LAT), F32),
            pltpu.VMEM((112, LAT), F32),
            pltpu.VMEM((2 * LAT, 2 * LAT), BF16),
            pltpu.VMEM((BANDS, OUTSIDE, SHARE, LAT), F32),
            pltpu.SemaphoreType.DMA((4,)),
        ],
        input_output_aliases={6: 0, 7: 1},
        compiler_params=PARAMS,
        name="forecast_outer",
    )(ens, left, right, depth, mask, vort, messages, seen)


def pick_kernel(order, cell, seen, _, out, own):
    lane = lax.broadcasted_iota(jnp.int32, (SHARE, LAT), 1)

    def listed(i, n):
        codes = [cell[order[i * 16 + k]] for k in range(16)]
        for k, at in enumerate(codes):
            own[n] = at + (i * 16 + k) * (1 << 16)
            n = n + jnp.where(at >= 0, 1, 0)
        return n

    total = lax.fori_loop(0, NOBS // 16, listed, 0)
    out[...] = jnp.zeros_like(out)

    def some(i, _):
        found = []
        for k in range(8):
            valid = i * 8 + k < total
            code = jnp.where(valid, own[i * 8 + k], 0)
            j, at, lat = code >> 16, (code >> 7) & 511, code & 127
            tile = pltpu.roll(seen[at], (j - lat) & (LAT - 1), 1)
            found.append((j >> 7, jnp.where(valid, j & 127, -1), tile))
        for b, r, tile in found:
            out[b] = jnp.where(lane == r, tile, out[b])
        return 0

    lax.fori_loop(0, (total + 7) // 8, some, 0)


def pick(order, cell, seen, before):
    return pl.pallas_call(
        pick_kernel,
        out_shape=jax.ShapeDtypeStruct((BLOCKS, SHARE, LAT), F32),
        in_specs=[SMEM, SMEM, VMEM, ANY],
        out_specs=VMEM,
        scratch_shapes=[pltpu.SMEM((NOBS + 16,), jnp.int32)],
        compiler_params=PARAMS,
        name="pick_priors",
    )(order, cell, seen, before)


def sort_kernel(order, facts, out):
    data = facts[...]
    high, rest = split(data)
    left = data - high.astype(F32)
    mid, low = split(left)
    parts = jnp.concatenate([high, mid, low, jnp.zeros_like(rest)], axis=0)
    row = lax.broadcasted_iota(jnp.int32, (NOBS, LAT), 0)

    def block(b, _):
        hot = jnp.where(row == order[b], 1.0, 0.0).astype(BF16)
        got = jnp.dot(parts, hot, preferred_element_type=F32)
        out[b] = got[0:8] + got[8:16] + got[16:24]
        return 0

    lax.fori_loop(0, BLOCKS, block, 0)


def in_order(order, facts):
    return pl.pallas_call(
        sort_kernel,
        out_shape=jax.ShapeDtypeStruct((BLOCKS, 8, LAT), F32),
        in_specs=[VMEM, VMEM],
        out_specs=VMEM,
        compiler_params=PARAMS,
        name="obs_in_batch_order",
    )(order.reshape(BLOCKS, 1, LAT), facts)


def dot_nt(a, b):
    return lax.dot_general(a, b, (((1,), (1,)), ((), ())), preferred_element_type=F32)


def exact(a, b, dims):
    (ah, al), (bh, bl) = split(a), split(b)

    def dot(x, y):
        return lax.dot_general(x, y, (dims, ((), ())), preferred_element_type=F32)

    return dot(ah, bh) + (dot(ah, bl) + dot(al, bh))


def paired(high, low):
    top = jnp.concatenate([high, low], axis=1)
    bottom = jnp.concatenate([high, jnp.zeros_like(low)], axis=1)
    return jnp.concatenate([top, bottom], axis=0).astype(BF16)


def batch_facts(facts):
    return [jnp.concatenate([facts[b * 4 + i] for i in range(4)], axis=1) for b in range(2)]


def finder(place, fact):
    west, south = place[0].astype(F32), place[1].astype(F32)
    later_than = lax.broadcasted_iota(jnp.int32, (BATCH, BATCH), 0)
    later_than = later_than <= lax.broadcasted_iota(jnp.int32, (BATCH, BATCH), 1)
    upper = jnp.where(later_than, 1.0, 0.0).astype(BF16)
    number = lax.broadcasted_iota(jnp.int32, (SLOTS, BATCH), 0).astype(F32)
    lane = lax.broadcasted_iota(jnp.int32, (1, SLOTS), 1).astype(F32)
    row = lax.broadcasted_iota(jnp.int32, (SHARE, SLOTS), 0).astype(F32)
    rel, lat = [], []
    for b in range(2):
        r = fact[b][0:1] - west
        r = jnp.where(r < -float(NLON // 2 - WIDTH // 2), r + NLON, r)
        r = jnp.where(r >= float(NLON // 2 + WIDTH // 2), r - NLON, r)
        rel.append(r)
        lat.append(fact[b][1:2] - south)

    def near(b, lo, hi):
        dl = jnp.maximum(jnp.maximum(lo - rel[b], rel[b] - hi), 0.0)
        dr = jnp.maximum(jnp.maximum(-lat[b], lat[b] - (SHARE - 1.0)), 0.0)
        flag = jnp.where(dl * dl + dr * dr < float(RADIUS * RADIUS), 1.0, 0.0)
        upto = jnp.dot(
            jnp.broadcast_to(flag, (16, BATCH)).astype(BF16), upper, preferred_element_type=F32
        )[0:1]
        return jnp.where(flag > 0.0, upto - 1.0, -float(NOBS)), jnp.sum(flag)

    def hot(slot, shift):
        return jnp.where(slot == number + shift, 1.0, 0.0).astype(BF16)

    def spot(b, h):
        both = jnp.concatenate(
            [jnp.broadcast_to(rel[b], (8, BATCH)), jnp.broadcast_to(lat[b], (8, BATCH))], axis=0
        )
        high, low = split(both)
        got = dot_nt(high, h) + dot_nt(low, h)
        return got[0:1], got[8:9]

    def placed(lon, up, used, mean):
        gap = row - up
        base = jnp.where(lane < used, 1.0 - gap * gap * SCALE, -1.0)
        base = jnp.where(lane == mean, 1.0, base)
        scale = jnp.where(lane == mean, 0.0, SCALE)
        rows = [jnp.broadcast_to(a, (8, SLOTS)) for a in (lon, scale)]
        return jnp.concatenate([base] + rows, axis=0)

    return near, hot, spot, placed


def prepare_kernel(place, facts, hots, taper, where, count):
    fact = batch_facts(facts)
    near, hot, spot, placed = finder(place, fact)

    def column(a):
        tall = jnp.transpose(jnp.broadcast_to(a, (LAT, BATCH)))
        return jnp.concatenate([tall] * (BATCH // LAT), axis=1)

    east = jnp.abs(column(fact[0][0:1]) - fact[1][0:1])
    east = jnp.minimum(east, NLON - east)
    up = column(fact[0][1:2]) - fact[1][1:2]
    t = jnp.maximum(1.0 - (east * east + up * up) * SCALE, 0.0)
    taper[...] = t * t
    full = jnp.float32(0.0)
    for q, (lo, hi) in enumerate(((0.0, CUT - 1.0), (float(CUT), WIDTH - 1.0))):
        slot1, n1 = near(0, lo, hi)
        slot2, n2 = near(1, lo, hi)
        full = jnp.maximum(full, n1 + n2)
        h1, h2 = hot(slot1, 0.0), hot(slot2, -n1)
        hots[q, 0], hots[q, 1] = h1, h2
        (lon1, lat1), (lon2, lat2) = spot(0, h1), spot(1, h2)
        where[q] = placed(lon1 + lon2, lat1 + lat2, n1 + n2, MEAN)
    count[0] = jnp.where(full > MEAN, 1, 0)


def prepare(place, facts):
    return pl.pallas_call(
        prepare_kernel,
        out_shape=[
            jax.ShapeDtypeStruct((2, 2, SLOTS, BATCH), BF16),
            jax.ShapeDtypeStruct((BATCH, BATCH), F32),
            jax.ShapeDtypeStruct((2, SHARE + 16, SLOTS), F32),
            jax.ShapeDtypeStruct((1,), jnp.int32),
        ],
        in_specs=[SMEM, VMEM],
        out_specs=[VMEM] * 3 + [SMEM],
        compiler_params=PARAMS,
        name="list_observations",
    )(place, facts)


def arrange_kernel(parts, out, state, mid, halves, sems, stores):
    sets = [(g, min(8, GROUPS - g)) for g in range(0, GROUPS, 8)]
    loads = [
        pltpu.make_async_copy(parts.at[:, pl.ds(g, n)], state.at[:, pl.ds(g, n)], sems.at[t])
        for t, (g, n) in enumerate(sets)
    ]
    for c in loads:
        c.start()
    saves = []
    for t, (g, n) in enumerate(sets):
        loads[t].wait()
        for s in range(8):
            tile = jnp.transpose(state[s, pl.ds(g, 8)].reshape(8 * SHARE, LAT))
            for j in range(8):
                mid[j, pl.ds(s * SHARE, SHARE), :] = tile[j * SHARE : (j + 1) * SHARE]
        for j in range(8):
            pair = jnp.concatenate(split(jnp.transpose(mid[j])), axis=1)
            for i in range(n):
                halves[g + i, j] = pair[i * SHARE : (i + 1) * SHARE]
        saves.append(
            pltpu.make_async_copy(halves.at[pl.ds(g, n)], out.at[pl.ds(g, n)], stores.at[t])
        )
        saves[-1].start()
    for c in saves:
        c.wait()


def arrange(parts):
    shape = jax.ShapeDtypeStruct((GROUPS, 8, SHARE, 2 * MEMBERS), BF16)
    return pl.pallas_call(
        arrange_kernel,
        out_shape=shape,
        in_specs=[ANY],
        out_specs=ANY,
        scratch_shapes=[
            pltpu.VMEM((BANDS, SETS * 8, SHARE, LAT), F32),
            pltpu.VMEM((8, MEMBERS, LAT), F32),
            pltpu.VMEM(shape.shape, BF16),
            pltpu.SemaphoreType.DMA((SETS,)),
            pltpu.SemaphoreType.DMA((SETS,)),
        ],
        compiler_params=PARAMS,
        name="arrange_members",
    )(parts)


def analyse_kernel(
    place, many, p0, p1, p2, p3, facts, where, hots_in, taper_in, given, out,
    hots, taper, state, table, lead, link, gain, shapes, made, big, long_lead, long_gain, long_where, sems, stores,
):
    loads = [
        pltpu.make_async_copy(taper_in, taper, sems.at[FIELDS + 1]),
        pltpu.make_async_copy(hots_in, hots, sems.at[FIELDS + 2]),
    ]

    def inside(f):
        at = pl.ds(f * INNER, INNER)
        return pltpu.make_async_copy(given.at[at], state.at[at], sems.at[f])

    at = pl.ds(INSIDE, OUTSIDE)
    outside = pltpu.make_async_copy(given.at[at], state.at[at], sems.at[FIELDS])
    for c in loads + [outside] + [inside(f) for f in range(FIELDS)]:
        c.start()

    me = place[2]
    for x, got in enumerate((p0, p1, p2, p3)):
        for z in range(2):
            at = pl.multiple_of((me ^ (4 * z + x)) * SHARE, SHARE)
            for b in range(BLOCKS):
                table[pl.ds(at, SHARE), pl.ds(b * LAT, LAT)] = got[z, b]
    fact = batch_facts(facts)

    def adjust(picked, b):
        values, errors = fact[b][2:3], fact[b][3:4]
        mean = jnp.sum(picked, axis=0, keepdims=True) * (1.0 / MEMBERS)
        anomalies = picked - mean
        variance = jnp.sum(anomalies * anomalies, axis=0, keepdims=True) / (MEMBERS - 1) + 1e-6
        innovation = values - mean
        ratio = jnp.sum(innovation * innovation, axis=1, keepdims=True) / jnp.sum(
            variance + errors, axis=1, keepdims=True
        )
        root = jnp.sqrt(ratio)
        inflated = ratio * variance
        spread = root * anomalies
        post_var = 1.0 / (1.0 / inflated + 1.0 / errors)
        post_mean = post_var * (mean / inflated + values / errors)
        increments = post_mean - mean + (jnp.sqrt(post_var / inflated) - 1.0) * spread
        return root, spread * (1.0 / ((MEMBERS - 1) * inflated)), increments

    root1, scaled1, inc1 = adjust(table[:, pl.ds(0, BATCH)], 0)

    later = table[:, pl.ds(BATCH, BATCH)]
    mean = jnp.sum(later, axis=0, keepdims=True) * (1.0 / MEMBERS)
    spread = root1 * (later - mean)
    cov = exact(jnp.transpose(scaled1), spread, ((1,), (0,)))
    for c in loads:
        c.wait()
    later = (mean + spread) + exact(inc1, taper[...] * cov, ((1,), (0,)))
    root2, scaled2, inc2 = adjust(later, 1)
    both_roots = jnp.sum(root1 * root2)

    sp1, sp2 = split(root1 * scaled1), split(root1 * root2 * scaled2)
    shift1 = jnp.sum(inc1, axis=0, keepdims=True) * (1.0 / MEMBERS)
    free1 = inc1 - shift1
    g1, g2 = split(root2 * free1 + shift1), split(inc2)
    f1, s2 = split(free1), split(root2 * scaled2)
    lane = lax.broadcasted_iota(jnp.int32, (1, SLOTS), 1)
    tall = lax.broadcasted_iota(jnp.int32, (SLOTS, 1), 0)
    rest = [a.astype(F32) for a in split(1.0 - root1 * root2)]
    for q in range(2):
        h1, h2 = hots[q, 0], hots[q, 1]
        lead_h, lead_l = [dot_nt(a, h1) + dot_nt(b, h2) for a, b in zip(sp1, sp2)]
        lead[q] = paired(jnp.where(lane == MEAN, 1.0 / MEMBERS, lead_h), lead_l)
        gain_h, gain_l = [dot_nt(h1, a) + dot_nt(h2, b) for a, b in zip(g1, g2)]
        gain[q] = paired(
            jnp.where(tall == MEAN, rest[0], gain_h), jnp.where(tall == MEAN, rest[1], gain_l)
        )
        one = dot_nt(h1, f1[0]) + dot_nt(h1, f1[1])
        two = dot_nt(h2, s2[0]) + dot_nt(h2, s2[1])
        link[q] = paired(*split(exact(one, two, ((1,), (1,)))))

    outside.wait()

    def times(pair, m):
        got = jnp.dot(pair, m, preferred_element_type=F32)
        return got[:, :MEMBERS] + got[:, MEMBERS:]

    def product(a, m):
        return times(jnp.concatenate(split(a), axis=1), m)

    def taper_of(spots, lon):
        base, at, scale = spots[0:SHARE], spots[SHARE : SHARE + 1], spots[SHARE + 8 : SHARE + 9]
        gap = at - lon
        t = jnp.maximum(base - gap * gap * scale, 0.0)
        return t * t

    def whole(pair):
        return pair[:, :MEMBERS].astype(F32) + pair[:, MEMBERS:].astype(F32)

    def short(pair, t, q):
        cov = times(pair, lead[q])
        cov = cov + product(t * cov, link[q])
        return both_roots * whole(pair) + product(t * cov, gain[q])

    def block(g, n, lons=8):
        pair = state[pl.ds(g, n)] if lons == 8 else state[g, pl.ds(0, lons)]
        return pair.reshape(n * lons * SHARE, 2 * MEMBERS)

    def put(f, lon, x, n):
        made[f, pl.ds(lon, n)] = x.reshape(n, SHARE, MEMBERS)

    def store(f):
        return pltpu.make_async_copy(made.at[f], out.at[f], stores.at[f])

    @pl.when(many[0] == 0)
    def _():
        for q, (lo, hi) in enumerate(((0, CUT), (CUT, WIDTH))):
            for lon in range(lo, hi):
                shapes[lon] = taper_of(where[q], float(lon))

        def shape(lon, n):
            return shapes[pl.ds(lon, n)].reshape(n * SHARE, SLOTS)

        x = short(block(GROUPS - 2, 1), jnp.concatenate([shape(RIGHT + 8, 2)] * 4, axis=0), 1)
        for f in range(4):
            put(f, RIGHT + 8, x[f * 2 * SHARE : (f + 1) * 2 * SHARE], 2)
        put(4, RIGHT + 8, short(block(GROUPS - 1, 1, 2), shape(RIGHT + 8, 2), 1), 2)

        def some(fs):
            for f in fs:
                inside(f).wait()
            for q, lo, n, edge in ((0, 0, 5, 0), (1, 5, 4, RIGHT)):
                lon = 8 * (lo + 1)
                pair = jnp.concatenate(
                    [a for f in fs for a in (block(f * INNER + lo, n), block(INSIDE + 2 * f + q, 1))],
                    axis=0,
                )
                t = jnp.concatenate([shape(lon, 8 * n), shape(edge, 8)] * len(fs), axis=0)
                x = short(pair, t, q)
                r = 8 * (n + 1) * SHARE
                for i, f in enumerate(fs):
                    put(f, lon, x[i * r : i * r + 8 * n * SHARE], 8 * n)
                    put(f, edge, x[i * r + 8 * n * SHARE : (i + 1) * r], 8)
            for f in fs:
                store(f).start()

        some([0, 1])
        some([2, 3])
        some([4])

    @pl.when(many[0] != 0)
    def _():
        near, hot, spot, placed = finder(place, fact)
        roots = [jnp.sum(root1), jnp.sum(root2)]
        chunks = []
        for b, (sp, g) in enumerate(((split(scaled1), split(inc1)), (split(scaled2), g2))):
            slot, n = near(b, 0.0, WIDTH - 1.0)
            chunks.append((n.astype(jnp.int32) + SLOTS - 1) // SLOTS)
            for c in range(CHUNKS):
                h = hot(slot, float(c * SLOTS))
                long_lead[b, c] = paired(dot_nt(sp[0], h), dot_nt(sp[1], h))
                long_gain[b, c] = paired(dot_nt(h, g[0]), dot_nt(h, g[1]))
                lon, up = spot(b, h)
                long_where[b, c] = placed(lon, up, n - float(c * SLOTS), -1)
        for f in range(FIELDS):
            inside(f).wait()

        def long(pair, lons):
            x = whole(pair)
            for b in range(2):
                mean = jnp.sum(x, axis=1, keepdims=True) * (1.0 / MEMBERS)
                anomaly = x - mean
                big[pl.ds(0, x.shape[0]), :] = x + (roots[b] - 1.0) * anomaly
                anomaly = roots[b] * anomaly

                def chunk(c, _):
                    t = jnp.concatenate([taper_of(long_where[b, c], lon) for lon in lons], axis=0)
                    w = t * product(anomaly, long_lead[b, c])
                    big[pl.ds(0, x.shape[0]), :] += product(w, long_gain[b, c])
                    return 0

                lax.fori_loop(0, chunks[b], chunk, 0)
                x = big[pl.ds(0, x.shape[0]), :]
            return x

        def each(g, _):
            inner = g < INSIDE
            h = g - INSIDE
            f = jnp.where(inner, g // INNER, h // 2)
            lon = jnp.where(inner, 8 * (g % INNER + 1), RIGHT * (h % 2))
            at = lon.astype(F32)
            put(f, lon, long(block(g, 1), [at + j for j in range(8)]), 8)
            return 0

        lax.fori_loop(0, GROUPS - 2, each, 0)
        tail = [float(RIGHT + 8 + j % 2) for j in range(8)]
        x = long(block(GROUPS - 2, 1), tail)
        for f in range(4):
            put(f, RIGHT + 8, x[f * 2 * SHARE : (f + 1) * 2 * SHARE], 2)
        put(4, RIGHT + 8, long(block(GROUPS - 1, 1, 2), tail[:2]), 2)
        for f in range(FIELDS):
            store(f).start()

    for f in range(FIELDS):
        store(f).wait()


def analyse(place, many, priors, facts, where, hots, taper, state):
    square = (2 * SLOTS, 2 * MEMBERS)
    return pl.pallas_call(
        analyse_kernel,
        out_shape=jax.ShapeDtypeStruct((FIELDS, WIDTH, SHARE, MEMBERS), F32),
        in_specs=[SMEM] * 2 + [VMEM] * 6 + [ANY] * 3,
        out_specs=ANY,
        scratch_shapes=[
            pltpu.VMEM(hots.shape, BF16),
            pltpu.VMEM(taper.shape, F32),
            pltpu.VMEM(state.shape, BF16),
            pltpu.VMEM((MEMBERS, NOBS), F32),
            pltpu.VMEM((2,) + square, BF16),
            pltpu.VMEM((2,) + square, BF16),
            pltpu.VMEM((2,) + square, BF16),
            pltpu.VMEM((WIDTH, SHARE, SLOTS), F32),
            pltpu.VMEM((FIELDS, WIDTH, SHARE, MEMBERS), F32),
            pltpu.VMEM((8 * SHARE, MEMBERS), F32),
            pltpu.VMEM((2, CHUNKS) + square, BF16),
            pltpu.VMEM((2, CHUNKS) + square, BF16),
            pltpu.VMEM((2, CHUNKS, SHARE + 16, SLOTS), F32),
            pltpu.SemaphoreType.DMA((FIELDS + 3,)),
            pltpu.SemaphoreType.DMA((FIELDS,)),
        ],
        compiler_params=PARAMS,
        name="analyse",
    )(place, many, *priors, facts, where, hots, taper, state)


def across(x, axis, bits):
    count = lax.axis_size(axis)
    return lax.ppermute(x, axis, [(i, i ^ bits) for i in range(count)])


def shards(
    ensemble,
    ocean_depth,
    planetary_vorticity,
    land_mask,
    obs_values,
    obs_error,
    obs_lon,
    obs_lat,
    obs_field,
    obs_order,
):
    member, sector = lax.axis_index("member"), lax.axis_index("sector")
    sectors = lax.axis_size("sector")
    vort = planetary_vorticity.reshape(1, LAT)
    ens = jnp.transpose(ensemble, (1, 2, 0, 3))
    west_side, east_side = edges(ens, ocean_depth, land_mask)
    left = lax.ppermute(east_side, "sector", [(i, (i + 1) % sectors) for i in range(sectors)])
    right = lax.ppermute(west_side, "sector", [((i + 1) % sectors, i) for i in range(sectors)])

    lon_f, lat_f = obs_lon.astype(F32), obs_lat.astype(F32)
    facts = in_order(
        obs_order, jnp.stack([lon_f, lat_f, obs_values, obs_error] + [jnp.zeros_like(lon_f)] * 4)
    )
    west = sector * WIDTH
    here = obs_lon - west
    cell = ((obs_field - 2) * WIDTH + here) * LAT + obs_lat
    cell = jnp.where((here >= 0) & (here < WIDTH), cell, -1)
    place = jnp.stack([west, member * SHARE, member])
    hots, taper, where, many = prepare(place, facts)

    messages, seen = forecast_inner(ens, ocean_depth, land_mask, vort)
    messages, seen = forecast_outer(
        ens, left, right, ocean_depth, land_mask, vort, messages, seen
    )
    parts = lax.all_to_all(messages, "member", split_axis=0, concat_axis=0, tiled=True)

    priors = pick(obs_order, cell, seen.reshape(3 * WIDTH, SHARE, LAT), where)
    for bit in (2, 4, 1):
        priors = priors + across(priors, "sector", bit)
    both = ("member", "sector")
    count = lax.axis_size("member") * sectors
    crossed = lax.ppermute(priors, both, [(i, i ^ (4 * sectors + 8)) for i in range(count)])
    priors = jnp.stack(
        [priors + across(priors, "sector", 8), across(priors, "member", 4) + crossed]
    )
    priors = [priors] + [across(priors, "member", x) for x in (1, 2, 3)]
    analysis = analyse(place, many, priors, facts, where, hots, taper, arrange(parts))
    return jnp.transpose(analysis, (0, 2, 1, 3))


def solution(mesh):
    placed = (
        P("member", None, "sector", None),
        P("sector", None),
        P(),
        P("sector", None),
        P(),
        P(),
        P(),
        P(),
        P(),
        P(),
    )
    return jax.shard_map(
        shards,
        mesh=mesh,
        in_specs=placed,
        out_specs=P(None, "member", "sector", None),
        check_vma=False,
    )
```

```python
import jax
import jax.numpy as jnp
from jax import lax
from jax.experimental import pallas as pl
from jax.experimental.pallas import tpu as pltpu
from jax.sharding import PartitionSpec as P

NLON = 1440
LAT = 128
FIELDS = 5
MEMBERS = 128
NOBS = 1024
BATCH = 512
BLOCKS = NOBS // LAT
RADIUS = 48
SHARE = 16
BANDS = 8
WIDTH = 90
EDGE = 4
INNER = 10
REST_AT = EDGE + 8 * INNER
INSIDE = FIELDS * INNER + 2
GROUPS = INSIDE + FIELDS
RIGHT = 80
SETS = (INSIDE + 7) // 8
CUT = 44
SLOTS = 128
CHUNKS = BATCH // SLOTS
MEAN = SLOTS - 1
SCALE = 1.0 / (RADIUS * RADIUS)
F32 = jnp.float32
BF16 = jnp.bfloat16
SMEM = pl.BlockSpec(memory_space=pltpu.SMEM)
VMEM = pl.BlockSpec(memory_space=pltpu.VMEM)
ANY = pl.BlockSpec(memory_space=pl.ANY)
PARAMS = pltpu.CompilerParams(vmem_limit_bytes=56 * 1024 * 1024)


def edges_kernel(ens, depth, mask, west, east, deep, sea, sems):
    sides = ((west, 0), (east, WIDTH - EDGE))
    grids = ((0, 0, 8), (RIGHT, 8, WIDTH - RIGHT))
    copies = [
        pltpu.make_async_copy(ens.at[:, pl.ds(lon, EDGE)], out.at[pl.ds(0, FIELDS)], sems.at[i])
        for i, (out, lon) in enumerate(sides)
    ]
    for i, (lon, at, n) in enumerate(grids):
        for j, (grid, to) in enumerate(((depth, deep), (mask, sea))):
            copies.append(
                pltpu.make_async_copy(
                    grid.at[pl.ds(lon, n)], to.at[pl.ds(at, n)], sems.at[2 + 2 * i + j]
                )
            )
    for c in copies:
        c.start()
    for c in copies:
        c.wait()
    for (out, lon), (start, at, _) in zip(sides, grids):
        rows = pl.ds(at + lon - start, EDGE)
        out[FIELDS, 0, pl.ds(0, 8), :] = jnp.concatenate([deep[rows, :], sea[rows, :].astype(F32)], axis=0)


def edges(ens, depth, mask):
    side = jax.ShapeDtypeStruct((FIELDS + 1, EDGE, SHARE, LAT), F32)
    return pl.pallas_call(
        edges_kernel,
        out_shape=[side, side],
        in_specs=[ANY, ANY, ANY],
        out_specs=[VMEM, VMEM],
        scratch_shapes=[
            pltpu.VMEM((24, LAT), F32),
            pltpu.VMEM((24, LAT), jnp.int32),
            pltpu.SemaphoreType.DMA((6,)),
        ],
        compiler_params=PARAMS,
        name="pack_edges",
    )(ens, depth, mask)


def split(a):
    high = a.astype(BF16)
    return high, (a - high.astype(F32)).astype(BF16)


def bands(out):
    row = lax.broadcasted_iota(jnp.int32, (2 * LAT, 2 * LAT), 0) % LAT
    col = lax.broadcasted_iota(jnp.int32, (2 * LAT, 2 * LAT), 1)
    gap = row - col % LAT
    value = jnp.where(jnp.abs(gap) == 1, jnp.where(col < LAT, gap, 1), 0)
    out[...] = value.astype(F32).astype(BF16)


def stepper(dep, sea, vort, flux, band):
    spin = jnp.broadcast_to(vort[...], (SHARE, LAT))

    def halves(tiles):
        return jnp.concatenate(split(jnp.concatenate(tiles, axis=0)), axis=1)

    def difference(tiles):
        got = jnp.dot(halves(tiles), band[:, 0:LAT], preferred_element_type=F32)
        return [got[i * SHARE : (i + 1) * SHARE] for i in range(len(tiles))]

    def both(tiles):
        got = jnp.dot(halves(tiles), band[...], preferred_element_type=F32)
        rows = [got[i * SHARE : (i + 1) * SHARE] for i in range(len(tiles))]
        return [r[:, 0:LAT] for r in rows], [r[:, LAT:] for r in rows]

    def flow(src, dst, places):
        slope = difference([src[2, e] for e, _ in places])
        for (e, row), dh in zip(places, slope):
            u, v = src[0, e], src[1, e]
            m = sea[pl.ds(row, 1), :]
            un = m * (u + spin * v - 0.15 * (src[2, e + 1] - src[2, e - 1]))
            dst[0, e] = un
            dst[1, e] = m * (v - spin * u - 0.15 * dh)
            flux[e] = dep[pl.ds(row, 1), :] * un

    def others(src, dst, places):
        slope = difference([dep[pl.ds(row, 1), :] * dst[1, e] for e, row in places])
        for (e, _), dv in zip(places, slope):
            dst[2, e] = src[2, e] - 0.15 * (flux[e + 1] - flux[e - 1] + dv)
        for c in (3, 4):
            slope, total = both([src[c, e] for e, _ in places])
            for (e, _), dc, around in zip(places, slope, total):
                a, ae, aw = src[c, e], src[c, e + 1], src[c, e - 1]
                dst[c, e] = (
                    a
                    - 0.15 * (dst[0, e] * (ae - aw) + dst[1, e] * dc)
                    + 0.1 * (((ae + aw) + around) - 4.0 * a)
                )

    return flow, others


def in_blocks(stage, src, dst, lo, hi, row, n):
    def block(i, _):
        e = jnp.minimum(lo + i * n, hi - n)
        stage(src, dst, [(e + k, e + k + row) for k in range(n)])
        return 0

    lax.fori_loop(0, (hi - lo + n - 1) // n, block, 0)


def turn(tiles, out, g):
    tile = jnp.transpose(tiles.reshape(8 * SHARE, LAT))
    for b in range(BANDS):
        out[b, g] = tile[b * SHARE : (b + 1) * SHARE]


def inner_kernel(ens, depth, mask, vort, out, seen, now, nxt, flux, sea, band, made, sems):
    half = WIDTH // 2
    loads = [
        pltpu.make_async_copy(ens.at[:, pl.ds(at, n)], now.at[:, pl.ds(at, n)], sems.at[2 + i])
        for i, (at, n) in enumerate(((0, half + 1), (half + 1, half - 1)))
    ]
    for c in loads:
        c.start()
    sea[...] = mask[...].astype(F32)
    bands(band)
    flow, others = stepper(depth, sea, vort, flux, band)
    for at, c in zip((1, half), loads):
        c.wait()
        flow(now, nxt, [(at + k, at + k) for k in range(half - 1)])
    for d, stage, src, dst in ((2, others, now, nxt), (3, flow, nxt, now), (4, others, nxt, now)):
        in_blocks(stage, src, dst, d, WIDTH - d, 0, half - d)
    keep = pltpu.make_async_copy(
        now.at[pl.ds(2, 3), pl.ds(EDGE, WIDTH - 2 * EDGE)],
        seen.at[:, pl.ds(EDGE, WIDTH - 2 * EDGE)],
        sems.at[1],
    )
    keep.start()

    def send(f):
        at = pl.ds(f * INNER, INNER if isinstance(f, jax.Array) or f < FIELDS else 2)
        return pltpu.make_async_copy(made.at[:, at], out.at[:, at], sems.at[2 + f])

    turn(now[pl.ds(0, 4), pl.ds(REST_AT, 2)], made, INSIDE - 2)
    turn(jnp.concatenate([now[4, pl.ds(REST_AT, 2)]] * 4, axis=0), made, INSIDE - 1)
    send(FIELDS).start()

    def field(f, _):
        for i in range(INNER):
            turn(now[f, pl.ds(EDGE + i * 8, 8)], made, f * INNER + i)
        send(f).start()
        return 0

    lax.fori_loop(0, FIELDS, field, 0)
    for f in range(FIELDS + 1):
        send(f).wait()
    keep.wait()


def forecast_inner(ens, depth, mask, vort):
    return pl.pallas_call(
        inner_kernel,
        out_shape=[
            jax.ShapeDtypeStruct((BANDS, INSIDE, SHARE, LAT), F32),
            jax.ShapeDtypeStruct((3, WIDTH, SHARE, LAT), F32),
        ],
        in_specs=[ANY, VMEM, VMEM, VMEM],
        out_specs=[ANY, ANY],
        scratch_shapes=[
            pltpu.VMEM((FIELDS, WIDTH, SHARE, LAT), F32),
            pltpu.VMEM((FIELDS, WIDTH, SHARE, LAT), F32),
            pltpu.VMEM((WIDTH, SHARE, LAT), F32),
            pltpu.VMEM((WIDTH, LAT), F32),
            pltpu.VMEM((2 * LAT, 2 * LAT), BF16),
            pltpu.VMEM((BANDS, INSIDE, SHARE, LAT), F32),
            pltpu.SemaphoreType.DMA((3 + FIELDS,)),
        ],
        compiler_params=PARAMS,
        name="forecast_inner",
    )(ens, depth, mask, vort)


def outer_kernel(
    ens, left, right, depth, mask, vort, _, out, seen, now, nxt, flux, dep, sea, band, made, sems
):
    own = 2 * EDGE
    second = own + EDGE
    loads = [
        pltpu.make_async_copy(ens.at[:, pl.ds(0, own)], now.at[:, pl.ds(EDGE, own)], sems.at[0]),
        pltpu.make_async_copy(
            ens.at[:, pl.ds(WIDTH - own, own)], now.at[:, pl.ds(second, own)], sems.at[1]
        ),
        pltpu.make_async_copy(left.at[pl.ds(0, FIELDS)], now.at[:, pl.ds(0, EDGE)], sems.at[2]),
        pltpu.make_async_copy(
            right.at[pl.ds(0, FIELDS)], now.at[:, pl.ds(second + own, EDGE)], sems.at[3]
        ),
    ]
    for c in loads:
        c.start()
    for grid, whole, at in ((dep, depth, 0), (sea, mask, EDGE)):
        grid[pl.ds(8, WIDTH), :] = whole[...].astype(F32)
        grid[pl.ds(4, EDGE), :] = left[FIELDS, 0, pl.ds(at, EDGE), :]
        grid[pl.ds(8 + WIDTH, EDGE), :] = right[FIELDS, 0, pl.ds(at, EDGE), :]
    bands(band)
    flow, others = stepper(dep, sea, vort, flux, band)
    for c in loads:
        c.wait()
    end = second + own + EDGE
    skip = 8 + WIDTH - own - second
    for d, stage, src, dst in (
        (1, flow, now, nxt),
        (2, others, now, nxt),
        (3, flow, nxt, now),
        (4, others, nxt, now),
    ):
        places = [(e, e + 4) for e in range(d, second - d)]
        stage(src, dst, places + [(e, e + skip) for e in range(second + d, end - d)])
    keeps = [
        pltpu.make_async_copy(
            now.at[pl.ds(2, 3), pl.ds(at, EDGE)], seen.at[:, pl.ds(lon, EDGE)], sems.at[i]
        )
        for i, (at, lon) in enumerate(((EDGE, 0), (second + EDGE, WIDTH - EDGE)))
    ]
    for c in keeps:
        c.start()
    for f in range(FIELDS):
        sides = [now[f, pl.ds(EDGE, EDGE)], now[f, pl.ds(second + EDGE, EDGE)]]
        turn(jnp.concatenate(sides, axis=0), made, f)
    send = pltpu.make_async_copy(made, out, sems.at[2])
    send.start()
    for c in [send] + keeps:
        c.wait()


def forecast_outer(ens, left, right, depth, mask, vort, seen):
    window = 6 * EDGE
    messages = jax.ShapeDtypeStruct((BANDS, FIELDS, SHARE, LAT), F32)
    return pl.pallas_call(
        outer_kernel,
        out_shape=[messages, jax.ShapeDtypeStruct(seen.shape, F32)],
        in_specs=[ANY] + [VMEM] * 5 + [ANY],
        out_specs=[ANY] * 2,
        scratch_shapes=[
            pltpu.VMEM((FIELDS, window, SHARE, LAT), F32),
            pltpu.VMEM((FIELDS, window, SHARE, LAT), F32),
            pltpu.VMEM((window, SHARE, LAT), F32),
            pltpu.VMEM((112, LAT), F32),
            pltpu.VMEM((112, LAT), F32),
            pltpu.VMEM((2 * LAT, 2 * LAT), BF16),
            pltpu.VMEM((BANDS, FIELDS, SHARE, LAT), F32),
            pltpu.SemaphoreType.DMA((4,)),
        ],
        input_output_aliases={6: 1},
        compiler_params=PARAMS,
        name="forecast_outer",
    )(ens, left, right, depth, mask, vort, seen)


def pick_kernel(order, cell, seen, _, out, own):
    lane = lax.broadcasted_iota(jnp.int32, (SHARE, LAT), 1)

    def listed(i, n):
        codes = [cell[order[i * 16 + k]] for k in range(16)]
        for k, at in enumerate(codes):
            own[n] = at + (i * 16 + k) * (1 << 16)
            n = n + jnp.where(at >= 0, 1, 0)
        return n

    total = lax.fori_loop(0, NOBS // 16, listed, 0)
    out[...] = jnp.zeros_like(out)

    def some(i, _):
        found = []
        for k in range(8):
            valid = i * 8 + k < total
            code = jnp.where(valid, own[i * 8 + k], 0)
            j, at, lat = code >> 16, (code >> 7) & 511, code & 127
            tile = pltpu.roll(seen[at], (j - lat) & (LAT - 1), 1)
            found.append((j >> 7, jnp.where(valid, j & 127, -1), tile))
        for b, r, tile in found:
            out[b] = jnp.where(lane == r, tile, out[b])
        return 0

    lax.fori_loop(0, (total + 7) // 8, some, 0)


def pick(order, cell, seen, before):
    return pl.pallas_call(
        pick_kernel,
        out_shape=jax.ShapeDtypeStruct((BLOCKS, SHARE, LAT), F32),
        in_specs=[SMEM, SMEM, VMEM, ANY],
        out_specs=VMEM,
        scratch_shapes=[pltpu.SMEM((NOBS + 16,), jnp.int32)],
        compiler_params=PARAMS,
        name="pick_priors",
    )(order, cell, seen, before)


def sort_kernel(order, facts, out):
    data = facts[...]
    high, rest = split(data)
    left = data - high.astype(F32)
    mid, low = split(left)
    parts = jnp.concatenate([high, mid, low, jnp.zeros_like(rest)], axis=0)
    row = lax.broadcasted_iota(jnp.int32, (NOBS, LAT), 0)

    def block(b, _):
        hot = jnp.where(row == order[b], 1.0, 0.0).astype(BF16)
        got = jnp.dot(parts, hot, preferred_element_type=F32)
        out[b] = got[0:8] + got[8:16] + got[16:24]
        return 0

    lax.fori_loop(0, BLOCKS, block, 0)


def in_order(order, facts):
    return pl.pallas_call(
        sort_kernel,
        out_shape=jax.ShapeDtypeStruct((BLOCKS, 8, LAT), F32),
        in_specs=[VMEM, VMEM],
        out_specs=VMEM,
        compiler_params=PARAMS,
        name="obs_in_batch_order",
    )(order.reshape(BLOCKS, 1, LAT), facts)


def dot_nt(a, b):
    return lax.dot_general(a, b, (((1,), (1,)), ((), ())), preferred_element_type=F32)


def exact(a, b, dims):
    (ah, al), (bh, bl) = split(a), split(b)

    def dot(x, y):
        return lax.dot_general(x, y, (dims, ((), ())), preferred_element_type=F32)

    return dot(ah, bh) + (dot(ah, bl) + dot(al, bh))


def paired(high, low):
    top = jnp.concatenate([high, low], axis=1)
    bottom = jnp.concatenate([high, jnp.zeros_like(low)], axis=1)
    return jnp.concatenate([top, bottom], axis=0).astype(BF16)


def batch_facts(facts):
    return [jnp.concatenate([facts[b * 4 + i] for i in range(4)], axis=1) for b in range(2)]


def finder(place, fact):
    west, south = place[0].astype(F32), place[1].astype(F32)
    later_than = lax.broadcasted_iota(jnp.int32, (BATCH, BATCH), 0)
    later_than = later_than <= lax.broadcasted_iota(jnp.int32, (BATCH, BATCH), 1)
    upper = jnp.where(later_than, 1.0, 0.0).astype(BF16)
    number = lax.broadcasted_iota(jnp.int32, (SLOTS, BATCH), 0).astype(F32)
    lane = lax.broadcasted_iota(jnp.int32, (1, SLOTS), 1).astype(F32)
    row = lax.broadcasted_iota(jnp.int32, (SHARE, SLOTS), 0).astype(F32)
    rel, lat = [], []
    for b in range(2):
        r = fact[b][0:1] - west
        r = jnp.where(r < -float(NLON // 2 - WIDTH // 2), r + NLON, r)
        r = jnp.where(r >= float(NLON // 2 + WIDTH // 2), r - NLON, r)
        rel.append(r)
        lat.append(fact[b][1:2] - south)

    def near(b, lo, hi):
        dl = jnp.maximum(jnp.maximum(lo - rel[b], rel[b] - hi), 0.0)
        dr = jnp.maximum(jnp.maximum(-lat[b], lat[b] - (SHARE - 1.0)), 0.0)
        flag = jnp.where(dl * dl + dr * dr < float(RADIUS * RADIUS), 1.0, 0.0)
        upto = jnp.dot(
            jnp.broadcast_to(flag, (16, BATCH)).astype(BF16), upper, preferred_element_type=F32
        )[0:1]
        return jnp.where(flag > 0.0, upto - 1.0, -float(NOBS)), jnp.sum(flag)

    def hot(slot, shift):
        return jnp.where(slot == number + shift, 1.0, 0.0).astype(BF16)

    def spot(b, h):
        both = jnp.concatenate(
            [jnp.broadcast_to(rel[b], (8, BATCH)), jnp.broadcast_to(lat[b], (8, BATCH))], axis=0
        )
        high, low = split(both)
        got = dot_nt(high, h) + dot_nt(low, h)
        return got[0:1], got[8:9]

    def placed(lon, up, used, mean):
        gap = row - up
        base = jnp.where(lane < used, 1.0 - gap * gap * SCALE, -1.0)
        base = jnp.where(lane == mean, 1.0, base)
        scale = jnp.where(lane == mean, 0.0, SCALE)
        rows = [jnp.broadcast_to(a, (8, SLOTS)) for a in (lon, scale)]
        return jnp.concatenate([base] + rows, axis=0)

    return near, hot, spot, placed


def prepare_kernel(place, facts, hots, taper, where, count):
    fact = batch_facts(facts)
    near, hot, spot, placed = finder(place, fact)

    def column(a):
        tall = jnp.transpose(jnp.broadcast_to(a, (LAT, BATCH)))
        return jnp.concatenate([tall] * (BATCH // LAT), axis=1)

    east = jnp.abs(column(fact[0][0:1]) - fact[1][0:1])
    east = jnp.minimum(east, NLON - east)
    up = column(fact[0][1:2]) - fact[1][1:2]
    t = jnp.maximum(1.0 - (east * east + up * up) * SCALE, 0.0)
    taper[...] = t * t
    full = jnp.float32(0.0)
    for q, (lo, hi) in enumerate(((0.0, CUT - 1.0), (float(CUT), WIDTH - 1.0))):
        slot1, n1 = near(0, lo, hi)
        slot2, n2 = near(1, lo, hi)
        full = jnp.maximum(full, n1 + n2)
        h1, h2 = hot(slot1, 0.0), hot(slot2, -n1)
        hots[q, 0], hots[q, 1] = h1, h2
        (lon1, lat1), (lon2, lat2) = spot(0, h1), spot(1, h2)
        where[q] = placed(lon1 + lon2, lat1 + lat2, n1 + n2, MEAN)
    count[0] = jnp.where(full > MEAN, 1, 0)


def prepare(place, facts):
    return pl.pallas_call(
        prepare_kernel,
        out_shape=[
            jax.ShapeDtypeStruct((2, 2, SLOTS, BATCH), BF16),
            jax.ShapeDtypeStruct((BATCH, BATCH), F32),
            jax.ShapeDtypeStruct((2, SHARE + 16, SLOTS), F32),
            jax.ShapeDtypeStruct((1,), jnp.int32),
        ],
        in_specs=[SMEM, VMEM],
        out_specs=[VMEM] * 3 + [SMEM],
        compiler_params=PARAMS,
        name="list_observations",
    )(place, facts)


def members_to_lanes(state, g, n, mid, halves):
    for s in range(8):
        tile = jnp.transpose(state[s, pl.ds(g, 8)].reshape(8 * SHARE, LAT))
        for j in range(8):
            mid[j, pl.ds(s * SHARE, SHARE), :] = tile[j * SHARE : (j + 1) * SHARE]
    for j in range(8):
        pair = jnp.concatenate(split(jnp.transpose(mid[j])), axis=1)
        for i in range(n):
            halves(i, j, pair[i * SHARE : (i + 1) * SHARE])


def arrange_kernel(parts, out, state, mid, halves, sems, stores):
    sets = [(g, min(8, INSIDE - g)) for g in range(0, INSIDE, 8)]
    loads = [
        pltpu.make_async_copy(parts.at[:, pl.ds(g, n)], state.at[:, pl.ds(g, n)], sems.at[t])
        for t, (g, n) in enumerate(sets)
    ]
    for c in loads:
        c.start()
    saves = []
    for t, (g, n) in enumerate(sets):
        loads[t].wait()

        def put(i, j, pair):
            halves[g + i, j] = pair

        members_to_lanes(state, g, n, mid, put)
        saves.append(
            pltpu.make_async_copy(halves.at[pl.ds(g, n)], out.at[pl.ds(g, n)], stores.at[t])
        )
        saves[-1].start()
    for c in saves:
        c.wait()


def arrange(parts):
    shape = jax.ShapeDtypeStruct((INSIDE, 8, SHARE, 2 * MEMBERS), BF16)
    return pl.pallas_call(
        arrange_kernel,
        out_shape=shape,
        in_specs=[ANY],
        out_specs=ANY,
        scratch_shapes=[
            pltpu.VMEM((BANDS, SETS * 8, SHARE, LAT), F32),
            pltpu.VMEM((8, MEMBERS, LAT), F32),
            pltpu.VMEM(shape.shape, BF16),
            pltpu.SemaphoreType.DMA((SETS,)),
            pltpu.SemaphoreType.DMA((SETS,)),
        ],
        compiler_params=PARAMS,
        name="arrange_members",
    )(parts)


def analyse_kernel(
    place, many, p0, p1, p2, p3, facts, where, hots_in, taper_in, given, given_edges, out,
    hots, taper, state, edges, mid, table, lead, link, gain, shapes, made, big, long_lead, long_gain, long_where, sems, stores,
):
    loads = [
        pltpu.make_async_copy(taper_in, taper, sems.at[FIELDS + 1]),
        pltpu.make_async_copy(hots_in, hots, sems.at[FIELDS + 2]),
    ]

    def inside(f):
        at = pl.ds(f * INNER, INNER)
        return pltpu.make_async_copy(given.at[at], state.at[at], sems.at[f])

    at = pl.ds(FIELDS * INNER, 2)
    tail = pltpu.make_async_copy(given.at[at], state.at[at], sems.at[FIELDS])
    sides = pltpu.make_async_copy(given_edges, edges.at[:, pl.ds(0, FIELDS)], sems.at[FIELDS + 3])
    for c in loads + [sides, tail] + [inside(f) for f in range(FIELDS)]:
        c.start()

    me = place[2]
    for x, got in enumerate((p0, p1, p2, p3)):
        for z in range(2):
            at = pl.multiple_of((me ^ (4 * z + x)) * SHARE, SHARE)
            for b in range(BLOCKS):
                table[pl.ds(at, SHARE), pl.ds(b * LAT, LAT)] = got[z, b]
    fact = batch_facts(facts)

    def adjust(picked, b):
        values, errors = fact[b][2:3], fact[b][3:4]
        mean = jnp.sum(picked, axis=0, keepdims=True) * (1.0 / MEMBERS)
        anomalies = picked - mean
        variance = jnp.sum(anomalies * anomalies, axis=0, keepdims=True) / (MEMBERS - 1) + 1e-6
        innovation = values - mean
        ratio = jnp.sum(innovation * innovation, axis=1, keepdims=True) / jnp.sum(
            variance + errors, axis=1, keepdims=True
        )
        root = jnp.sqrt(ratio)
        inflated = ratio * variance
        spread = root * anomalies
        post_var = 1.0 / (1.0 / inflated + 1.0 / errors)
        post_mean = post_var * (mean / inflated + values / errors)
        increments = post_mean - mean + (jnp.sqrt(post_var / inflated) - 1.0) * spread
        return root, spread * (1.0 / ((MEMBERS - 1) * inflated)), increments

    root1, scaled1, inc1 = adjust(table[:, pl.ds(0, BATCH)], 0)

    later = table[:, pl.ds(BATCH, BATCH)]
    mean = jnp.sum(later, axis=0, keepdims=True) * (1.0 / MEMBERS)
    spread = root1 * (later - mean)
    cov = exact(jnp.transpose(scaled1), spread, ((1,), (0,)))
    for c in loads:
        c.wait()
    later = (mean + spread) + exact(inc1, taper[...] * cov, ((1,), (0,)))
    root2, scaled2, inc2 = adjust(later, 1)
    both_roots = jnp.sum(root1 * root2)

    sp1, sp2 = split(root1 * scaled1), split(root1 * root2 * scaled2)
    shift1 = jnp.sum(inc1, axis=0, keepdims=True) * (1.0 / MEMBERS)
    free1 = inc1 - shift1
    g1, g2 = split(root2 * free1 + shift1), split(inc2)
    f1, s2 = split(free1), split(root2 * scaled2)
    lane = lax.broadcasted_iota(jnp.int32, (1, SLOTS), 1)
    tall = lax.broadcasted_iota(jnp.int32, (SLOTS, 1), 0)
    rest = [a.astype(F32) for a in split(1.0 - root1 * root2)]
    for q in range(2):
        h1, h2 = hots[q, 0], hots[q, 1]
        lead_h, lead_l = [dot_nt(a, h1) + dot_nt(b, h2) for a, b in zip(sp1, sp2)]
        lead[q] = paired(jnp.where(lane == MEAN, 1.0 / MEMBERS, lead_h), lead_l)
        gain_h, gain_l = [dot_nt(h1, a) + dot_nt(h2, b) for a, b in zip(g1, g2)]
        gain[q] = paired(
            jnp.where(tall == MEAN, rest[0], gain_h), jnp.where(tall == MEAN, rest[1], gain_l)
        )
        one = dot_nt(h1, f1[0]) + dot_nt(h1, f1[1])
        two = dot_nt(h2, s2[0]) + dot_nt(h2, s2[1])
        link[q] = paired(*split(exact(one, two, ((1,), (1,)))))

    def put_edge(i, j, pair):
        state[INSIDE + i, j] = pair

    sides.wait()
    members_to_lanes(edges, 0, FIELDS, mid, put_edge)
    tail.wait()

    def times(pair, m):
        got = jnp.dot(pair, m, preferred_element_type=F32)
        return got[:, :MEMBERS] + got[:, MEMBERS:]

    def product(a, m):
        return times(jnp.concatenate(split(a), axis=1), m)

    def taper_of(spots, lon):
        base, at, scale = spots[0:SHARE], spots[SHARE : SHARE + 1], spots[SHARE + 8 : SHARE + 9]
        gap = at - lon
        t = jnp.maximum(base - gap * gap * scale, 0.0)
        return t * t

    def whole(pair):
        return pair[:, :MEMBERS].astype(F32) + pair[:, MEMBERS:].astype(F32)

    def short(pair, t, q):
        cov = times(pair, lead[q])
        cov = cov + product(t * cov, link[q])
        return both_roots * whole(pair) + product(t * cov, gain[q])

    def block(g, n):
        return state[pl.ds(g, n)].reshape(n * 8 * SHARE, 2 * MEMBERS)

    def part(g, at, n):
        return state[g, pl.ds(at, n)].reshape(n * SHARE, 2 * MEMBERS)

    def put_rest(x):
        for f in range(FIELDS):
            put(f, REST_AT, x[f * 2 * SHARE : (f + 1) * 2 * SHARE], 2)

    def put(f, lon, x, n):
        made[f, pl.ds(lon, n)] = x.reshape(n, SHARE, MEMBERS)

    def store(f):
        return pltpu.make_async_copy(made.at[f], out.at[f], stores.at[f])

    @pl.when(many[0] == 0)
    def _():
        for q, (lo, hi) in enumerate(((0, CUT), (CUT, WIDTH))):
            for lon in range(lo, hi):
                shapes[lon] = taper_of(where[q], float(lon))

        def shape(lon, n):
            return shapes[pl.ds(lon, n)].reshape(n * SHARE, SLOTS)

        pair = jnp.concatenate([block(INSIDE - 2, 1), part(INSIDE - 1, 0, 2)], axis=0)
        put_rest(short(pair, jnp.concatenate([shape(REST_AT, 2)] * FIELDS, axis=0), 1))

        def some(fs):
            for f in fs:
                inside(f).wait()
            n = INNER // 2
            for q, lon, edge in ((0, EDGE, 0), (1, CUT, WIDTH - EDGE)):
                pair = jnp.concatenate(
                    [
                        a
                        for f in fs
                        for a in (block(f * INNER + q * n, n), part(INSIDE + f, q * EDGE, EDGE))
                    ],
                    axis=0,
                )
                t = jnp.concatenate([shape(lon, 8 * n), shape(edge, EDGE)] * len(fs), axis=0)
                x = short(pair, t, q)
                r, m = (8 * n + EDGE) * SHARE, 8 * n * SHARE
                for i, f in enumerate(fs):
                    put(f, lon, x[i * r : i * r + m], 8 * n)
                    put(f, edge, x[i * r + m : (i + 1) * r], EDGE)
            for f in fs:
                store(f).start()

        some([0, 1])
        some([2, 3])
        some([4])

    @pl.when(many[0] != 0)
    def _():
        near, hot, spot, placed = finder(place, fact)
        roots = [jnp.sum(root1), jnp.sum(root2)]
        chunks = []
        for b, (sp, g) in enumerate(((split(scaled1), split(inc1)), (split(scaled2), g2))):
            slot, n = near(b, 0.0, WIDTH - 1.0)
            chunks.append((n.astype(jnp.int32) + SLOTS - 1) // SLOTS)
            for c in range(CHUNKS):
                h = hot(slot, float(c * SLOTS))
                long_lead[b, c] = paired(dot_nt(sp[0], h), dot_nt(sp[1], h))
                long_gain[b, c] = paired(dot_nt(h, g[0]), dot_nt(h, g[1]))
                lon, up = spot(b, h)
                long_where[b, c] = placed(lon, up, n - float(c * SLOTS), -1)
        for f in range(FIELDS):
            inside(f).wait()

        def long(pair, lons):
            x = whole(pair)
            for b in range(2):
                mean = jnp.sum(x, axis=1, keepdims=True) * (1.0 / MEMBERS)
                anomaly = x - mean
                big[pl.ds(0, x.shape[0]), :] = x + (roots[b] - 1.0) * anomaly
                anomaly = roots[b] * anomaly

                def chunk(c, _):
                    t = jnp.concatenate([taper_of(long_where[b, c], lon) for lon in lons], axis=0)
                    w = t * product(anomaly, long_lead[b, c])
                    big[pl.ds(0, x.shape[0]), :] += product(w, long_gain[b, c])
                    return 0

                lax.fori_loop(0, chunks[b], chunk, 0)
                x = big[pl.ds(0, x.shape[0]), :]
            return x

        def each(g, _):
            f, lon = g // INNER, 8 * (g % INNER) + EDGE
            at = lon.astype(F32)
            put(f, lon, long(block(g, 1), [at + j for j in range(8)]), 8)
            return 0

        lax.fori_loop(0, FIELDS * INNER, each, 0)
        last = long(part(INSIDE - 1, 0, 2), [float(REST_AT + j) for j in range(2)])
        first = long(block(INSIDE - 2, 1), [float(REST_AT + j % 2) for j in range(8)])
        put_rest(jnp.concatenate([first, last], axis=0))
        for f in range(FIELDS):
            for at, lon in ((0, 0), (EDGE, WIDTH - EDGE)):
                lons = [float(lon + j) for j in range(EDGE)]
                put(f, lon, long(part(INSIDE + f, at, EDGE), lons), EDGE)
        for f in range(FIELDS):
            store(f).start()

    for f in range(FIELDS):
        store(f).wait()


def analyse(place, many, priors, facts, where, hots, taper, state, sides):
    square = (2 * SLOTS, 2 * MEMBERS)
    return pl.pallas_call(
        analyse_kernel,
        out_shape=jax.ShapeDtypeStruct((FIELDS, WIDTH, SHARE, MEMBERS), F32),
        in_specs=[SMEM] * 2 + [VMEM] * 6 + [ANY] * 4,
        out_specs=ANY,
        scratch_shapes=[
            pltpu.VMEM(hots.shape, BF16),
            pltpu.VMEM(taper.shape, F32),
            pltpu.VMEM((GROUPS,) + state.shape[1:], BF16),
            pltpu.VMEM((BANDS, 8, SHARE, LAT), F32),
            pltpu.VMEM((8, MEMBERS, LAT), F32),
            pltpu.VMEM((MEMBERS, NOBS), F32),
            pltpu.VMEM((2,) + square, BF16),
            pltpu.VMEM((2,) + square, BF16),
            pltpu.VMEM((2,) + square, BF16),
            pltpu.VMEM((WIDTH, SHARE, SLOTS), F32),
            pltpu.VMEM((FIELDS, WIDTH, SHARE, MEMBERS), F32),
            pltpu.VMEM((8 * SHARE, MEMBERS), F32),
            pltpu.VMEM((2, CHUNKS) + square, BF16),
            pltpu.VMEM((2, CHUNKS) + square, BF16),
            pltpu.VMEM((2, CHUNKS, SHARE + 16, SLOTS), F32),
            pltpu.SemaphoreType.DMA((FIELDS + 4,)),
            pltpu.SemaphoreType.DMA((FIELDS,)),
        ],
        compiler_params=PARAMS,
        name="analyse",
    )(place, many, *priors, facts, where, hots, taper, state, sides)


def across(x, axis, bits):
    count = lax.axis_size(axis)
    return lax.ppermute(x, axis, [(i, i ^ bits) for i in range(count)])


def shards(
    ensemble,
    ocean_depth,
    planetary_vorticity,
    land_mask,
    obs_values,
    obs_error,
    obs_lon,
    obs_lat,
    obs_field,
    obs_order,
):
    member, sector = lax.axis_index("member"), lax.axis_index("sector")
    sectors = lax.axis_size("sector")
    vort = planetary_vorticity.reshape(1, LAT)
    ens = jnp.transpose(ensemble, (1, 2, 0, 3))
    west_side, east_side = edges(ens, ocean_depth, land_mask)
    left = lax.ppermute(east_side, "sector", [(i, (i + 1) % sectors) for i in range(sectors)])
    right = lax.ppermute(west_side, "sector", [((i + 1) % sectors, i) for i in range(sectors)])

    lon_f, lat_f = obs_lon.astype(F32), obs_lat.astype(F32)
    facts = in_order(
        obs_order, jnp.stack([lon_f, lat_f, obs_values, obs_error] + [jnp.zeros_like(lon_f)] * 4)
    )
    west = sector * WIDTH
    here = obs_lon - west
    cell = ((obs_field - 2) * WIDTH + here) * LAT + obs_lat
    cell = jnp.where((here >= 0) & (here < WIDTH), cell, -1)
    place = jnp.stack([west, member * SHARE, member])
    hots, taper, where, many = prepare(place, facts)

    messages, seen = forecast_inner(ens, ocean_depth, land_mask, vort)
    parts = lax.all_to_all(messages, "member", split_axis=0, concat_axis=0, tiled=True)
    sides, seen = forecast_outer(ens, left, right, ocean_depth, land_mask, vort, seen)
    sides = lax.all_to_all(sides, "member", split_axis=0, concat_axis=0, tiled=True)

    own = pick(obs_order, cell, seen.reshape(3 * WIDTH, SHARE, LAT), where)
    own = (own + across(own, "sector", 2)) + (across(own, "sector", 4) + across(own, "sector", 6))
    own = own + across(own, "sector", 1)
    axes = ("member", "sector")
    count = lax.axis_size("member") * sectors
    both = lax.ppermute(own, axes, [(i, i ^ (4 * sectors + 8)) for i in range(count)])
    own = jnp.stack([own + across(own, "sector", 8), across(own, "member", 4) + both])
    priors = [own] + [across(own, "member", x) for x in (1, 2, 3)]
    analysis = analyse(place, many, priors, facts, where, hots, taper, arrange(parts), sides)
    return jnp.transpose(analysis, (0, 2, 1, 3))


def solution(mesh):
    placed = (
        P("member", None, "sector", None),
        P("sector", None),
        P(),
        P("sector", None),
        P(),
        P(),
        P(),
        P(),
        P(),
        P(),
    )
    return jax.shard_map(
        shards,
        mesh=mesh,
        in_specs=placed,
        out_specs=P(None, "member", "sector", None),
        check_vma=False,
    )
```

```python
import jax
import jax.numpy as jnp
from jax import lax
from jax.experimental import pallas as pl
from jax.experimental.pallas import tpu as pltpu
from jax.sharding import PartitionSpec as P

NLON = 1440
LAT = 128
FIELDS = 5
MEMBERS = 128
NOBS = 1024
BATCH = 512
BLOCKS = NOBS // LAT
RADIUS = 48
SHARE = 16
BANDS = 8
WIDTH = 90
EDGE = 4
INNER = 10
REST_AT = EDGE + 8 * INNER
INSIDE = FIELDS * INNER + 2
GROUPS = INSIDE + FIELDS
RIGHT = 80
SETS = (INSIDE + 7) // 8
CUT = 44
SLOTS = 128
CHUNKS = BATCH // SLOTS
MEAN = SLOTS - 1
SCALE = 1.0 / (RADIUS * RADIUS)
F32 = jnp.float32
BF16 = jnp.bfloat16
SMEM = pl.BlockSpec(memory_space=pltpu.SMEM)
VMEM = pl.BlockSpec(memory_space=pltpu.VMEM)
ANY = pl.BlockSpec(memory_space=pl.ANY)
PARAMS = pltpu.CompilerParams(vmem_limit_bytes=56 * 1024 * 1024)


def edges_kernel(ens, depth, mask, west, east, deep, sea, sems):
    sides = ((west, 0), (east, WIDTH - EDGE))
    grids = ((0, 0, 8), (RIGHT, 8, WIDTH - RIGHT))
    copies = [
        pltpu.make_async_copy(ens.at[:, pl.ds(lon, EDGE)], out.at[pl.ds(0, FIELDS)], sems.at[i])
        for i, (out, lon) in enumerate(sides)
    ]
    for i, (lon, at, n) in enumerate(grids):
        for j, (grid, to) in enumerate(((depth, deep), (mask, sea))):
            copies.append(
                pltpu.make_async_copy(
                    grid.at[pl.ds(lon, n)], to.at[pl.ds(at, n)], sems.at[2 + 2 * i + j]
                )
            )
    for c in copies:
        c.start()
    for c in copies:
        c.wait()
    for (out, lon), (start, at, _) in zip(sides, grids):
        rows = pl.ds(at + lon - start, EDGE)
        out[FIELDS, 0, pl.ds(0, 8), :] = jnp.concatenate([deep[rows, :], sea[rows, :].astype(F32)], axis=0)


def edges(ens, depth, mask):
    side = jax.ShapeDtypeStruct((FIELDS + 1, EDGE, SHARE, LAT), F32)
    return pl.pallas_call(
        edges_kernel,
        out_shape=[side, side],
        in_specs=[ANY, ANY, ANY],
        out_specs=[VMEM, VMEM],
        scratch_shapes=[
            pltpu.VMEM((24, LAT), F32),
            pltpu.VMEM((24, LAT), jnp.int32),
            pltpu.SemaphoreType.DMA((6,)),
        ],
        compiler_params=PARAMS,
        name="pack_edges",
    )(ens, depth, mask)


def split(a):
    high = a.astype(BF16)
    return high, (a - high.astype(F32)).astype(BF16)


def bands(out):
    row = lax.broadcasted_iota(jnp.int32, (2 * LAT, 2 * LAT), 0) % LAT
    col = lax.broadcasted_iota(jnp.int32, (2 * LAT, 2 * LAT), 1)
    gap = row - col % LAT
    value = jnp.where(jnp.abs(gap) == 1, jnp.where(col < LAT, gap, 1), 0)
    out[...] = value.astype(F32).astype(BF16)


def stepper(dep, sea, vort, flux, band):
    spin = jnp.broadcast_to(vort[...], (SHARE, LAT))

    def halves(tiles):
        return jnp.concatenate(split(jnp.concatenate(tiles, axis=0)), axis=1)

    def difference(tiles):
        got = jnp.dot(halves(tiles), band[:, 0:LAT], preferred_element_type=F32)
        return [got[i * SHARE : (i + 1) * SHARE] for i in range(len(tiles))]

    def both(tiles):
        got = jnp.dot(halves(tiles), band[...], preferred_element_type=F32)
        rows = [got[i * SHARE : (i + 1) * SHARE] for i in range(len(tiles))]
        return [r[:, 0:LAT] for r in rows], [r[:, LAT:] for r in rows]

    def flow(src, dst, places):
        slope = difference([src[2, e] for e, _ in places])
        for (e, row), dh in zip(places, slope):
            u, v = src[0, e], src[1, e]
            m = sea[pl.ds(row, 1), :]
            un = m * (u + spin * v - 0.15 * (src[2, e + 1] - src[2, e - 1]))
            dst[0, e] = un
            dst[1, e] = m * (v - spin * u - 0.15 * dh)
            flux[e] = dep[pl.ds(row, 1), :] * un

    def others(src, dst, places):
        slope = difference([dep[pl.ds(row, 1), :] * dst[1, e] for e, row in places])
        for (e, _), dv in zip(places, slope):
            dst[2, e] = src[2, e] - 0.15 * (flux[e + 1] - flux[e - 1] + dv)
        for c in (3, 4):
            slope, total = both([src[c, e] for e, _ in places])
            for (e, _), dc, around in zip(places, slope, total):
                a, ae, aw = src[c, e], src[c, e + 1], src[c, e - 1]
                dst[c, e] = (
                    a
                    - 0.15 * (dst[0, e] * (ae - aw) + dst[1, e] * dc)
                    + 0.1 * (((ae + aw) + around) - 4.0 * a)
                )

    return flow, others


def in_blocks(stage, src, dst, lo, hi, row, n):
    def block(i, _):
        e = jnp.minimum(lo + i * n, hi - n)
        stage(src, dst, [(e + k, e + k + row) for k in range(n)])
        return 0

    lax.fori_loop(0, (hi - lo + n - 1) // n, block, 0)


def turn(tiles, out, g):
    tile = jnp.transpose(tiles.reshape(8 * SHARE, LAT))
    for b in range(BANDS):
        out[b, g] = tile[b * SHARE : (b + 1) * SHARE]


def inner_kernel(ens, depth, mask, vort, out, seen, now, nxt, flux, sea, band, made, sems):
    half = WIDTH // 2
    loads = [
        pltpu.make_async_copy(ens.at[:, pl.ds(at, n)], now.at[:, pl.ds(at, n)], sems.at[2 + i])
        for i, (at, n) in enumerate(((0, half + 1), (half + 1, half - 1)))
    ]
    for c in loads:
        c.start()
    sea[...] = mask[...].astype(F32)
    bands(band)
    flow, others = stepper(depth, sea, vort, flux, band)
    for at, c in zip((1, half), loads):
        c.wait()
        flow(now, nxt, [(at + k, at + k) for k in range(half - 1)])
    for d, stage, src, dst in ((2, others, now, nxt), (3, flow, nxt, now)):
        in_blocks(stage, src, dst, d, WIDTH - d, 0, half - d)

    def keep(i, at, n):
        return pltpu.make_async_copy(
            now.at[pl.ds(2, 3), pl.ds(at, n)], seen.at[:, pl.ds(at, n)], sems.at[i]
        )

    def send(i, g, n):
        at = pl.ds(g, n)
        return pltpu.make_async_copy(made.at[:, at], out.at[:, at], sems.at[4 + i])

    groups, sends = INNER // 2, []
    width = half - EDGE
    for part in range(2):
        at = EDGE + part * width
        others(nxt, now, [(at + k, at + k) for k in range(width)])
        sends.append(keep(part, at, width))
        sends[-1].start()
        if part == 1:
            turn(now[pl.ds(0, 4), pl.ds(REST_AT, 2)], made, INSIDE - 2)
            turn(jnp.concatenate([now[4, pl.ds(REST_AT, 2)]] * 4, axis=0), made, INSIDE - 1)
            sends.append(send(2 * FIELDS, INSIDE - 2, 2))
            sends[-1].start()
        for f in range(FIELDS):
            for i in range(part * groups, (part + 1) * groups):
                turn(now[f, pl.ds(EDGE + i * 8, 8)], made, f * INNER + i)
            sends.append(send(part * FIELDS + f, f * INNER + part * groups, groups))
            sends[-1].start()
    for c in sends:
        c.wait()


def forecast_inner(ens, depth, mask, vort):
    return pl.pallas_call(
        inner_kernel,
        out_shape=[
            jax.ShapeDtypeStruct((BANDS, INSIDE, SHARE, LAT), F32),
            jax.ShapeDtypeStruct((3, WIDTH, SHARE, LAT), F32),
        ],
        in_specs=[ANY, VMEM, VMEM, VMEM],
        out_specs=[ANY, ANY],
        scratch_shapes=[
            pltpu.VMEM((FIELDS, WIDTH, SHARE, LAT), F32),
            pltpu.VMEM((FIELDS, WIDTH, SHARE, LAT), F32),
            pltpu.VMEM((WIDTH, SHARE, LAT), F32),
            pltpu.VMEM((WIDTH, LAT), F32),
            pltpu.VMEM((2 * LAT, 2 * LAT), BF16),
            pltpu.VMEM((BANDS, INSIDE, SHARE, LAT), F32),
            pltpu.SemaphoreType.DMA((5 + 2 * FIELDS,)),
        ],
        compiler_params=PARAMS,
        name="forecast_inner",
    )(ens, depth, mask, vort)


def outer_kernel(
    ens, left, right, depth, mask, vort, _, out, seen, now, nxt, flux, dep, sea, band, made, sems
):
    own = 2 * EDGE
    second = own + EDGE
    loads = [
        pltpu.make_async_copy(ens.at[:, pl.ds(0, own)], now.at[:, pl.ds(EDGE, own)], sems.at[0]),
        pltpu.make_async_copy(
            ens.at[:, pl.ds(WIDTH - own, own)], now.at[:, pl.ds(second, own)], sems.at[1]
        ),
        pltpu.make_async_copy(left.at[pl.ds(0, FIELDS)], now.at[:, pl.ds(0, EDGE)], sems.at[2]),
        pltpu.make_async_copy(
            right.at[pl.ds(0, FIELDS)], now.at[:, pl.ds(second + own, EDGE)], sems.at[3]
        ),
    ]
    for c in loads:
        c.start()
    for grid, whole, at in ((dep, depth, 0), (sea, mask, EDGE)):
        grid[pl.ds(8, WIDTH), :] = whole[...].astype(F32)
        grid[pl.ds(4, EDGE), :] = left[FIELDS, 0, pl.ds(at, EDGE), :]
        grid[pl.ds(8 + WIDTH, EDGE), :] = right[FIELDS, 0, pl.ds(at, EDGE), :]
    bands(band)
    flow, others = stepper(dep, sea, vort, flux, band)
    for c in loads:
        c.wait()
    end = second + own + EDGE
    skip = 8 + WIDTH - own - second
    for d, stage, src, dst in (
        (1, flow, now, nxt),
        (2, others, now, nxt),
        (3, flow, nxt, now),
        (4, others, nxt, now),
    ):
        places = [(e, e + 4) for e in range(d, second - d)]
        stage(src, dst, places + [(e, e + skip) for e in range(second + d, end - d)])
    keeps = [
        pltpu.make_async_copy(
            now.at[pl.ds(2, 3), pl.ds(at, EDGE)], seen.at[:, pl.ds(lon, EDGE)], sems.at[i]
        )
        for i, (at, lon) in enumerate(((EDGE, 0), (second + EDGE, WIDTH - EDGE)))
    ]
    for c in keeps:
        c.start()
    for f in range(FIELDS):
        sides = [now[f, pl.ds(EDGE, EDGE)], now[f, pl.ds(second + EDGE, EDGE)]]
        turn(jnp.concatenate(sides, axis=0), made, f)
    send = pltpu.make_async_copy(made, out, sems.at[2])
    send.start()
    for c in [send] + keeps:
        c.wait()


def forecast_outer(ens, left, right, depth, mask, vort, seen):
    window = 6 * EDGE
    messages = jax.ShapeDtypeStruct((BANDS, FIELDS, SHARE, LAT), F32)
    return pl.pallas_call(
        outer_kernel,
        out_shape=[messages, jax.ShapeDtypeStruct(seen.shape, F32)],
        in_specs=[ANY] + [VMEM] * 5 + [ANY],
        out_specs=[ANY] * 2,
        scratch_shapes=[
            pltpu.VMEM((FIELDS, window, SHARE, LAT), F32),
            pltpu.VMEM((FIELDS, window, SHARE, LAT), F32),
            pltpu.VMEM((window, SHARE, LAT), F32),
            pltpu.VMEM((112, LAT), F32),
            pltpu.VMEM((112, LAT), F32),
            pltpu.VMEM((2 * LAT, 2 * LAT), BF16),
            pltpu.VMEM((BANDS, FIELDS, SHARE, LAT), F32),
            pltpu.SemaphoreType.DMA((4,)),
        ],
        input_output_aliases={6: 1},
        compiler_params=PARAMS,
        name="forecast_outer",
    )(ens, left, right, depth, mask, vort, seen)


def pick_kernel(order, cell, seen, _, out, own):
    lane = lax.broadcasted_iota(jnp.int32, (SHARE, LAT), 1)

    def listed(i, n):
        codes = [cell[order[i * 16 + k]] for k in range(16)]
        for k, at in enumerate(codes):
            own[n] = at + (i * 16 + k) * (1 << 16)
            n = n + jnp.where(at >= 0, 1, 0)
        return n

    total = lax.fori_loop(0, NOBS // 16, listed, 0)
    out[...] = jnp.zeros_like(out)

    def some(i, _):
        found = []
        for k in range(8):
            valid = i * 8 + k < total
            code = jnp.where(valid, own[i * 8 + k], 0)
            j, at, lat = code >> 16, (code >> 7) & 511, code & 127
            tile = pltpu.roll(seen[at], (j - lat) & (LAT - 1), 1)
            found.append((j >> 7, jnp.where(valid, j & 127, -1), tile))
        for b, r, tile in found:
            out[b] = jnp.where(lane == r, tile, out[b])
        return 0

    lax.fori_loop(0, (total + 7) // 8, some, 0)


def pick(order, cell, seen, before):
    return pl.pallas_call(
        pick_kernel,
        out_shape=jax.ShapeDtypeStruct((BLOCKS, SHARE, LAT), F32),
        in_specs=[SMEM, SMEM, VMEM, ANY],
        out_specs=VMEM,
        scratch_shapes=[pltpu.SMEM((NOBS + 16,), jnp.int32)],
        compiler_params=PARAMS,
        name="pick_priors",
    )(order, cell, seen, before)


def sort_kernel(order, facts, out):
    data = facts[...]
    high, rest = split(data)
    left = data - high.astype(F32)
    mid, low = split(left)
    parts = jnp.concatenate([high, mid, low, jnp.zeros_like(rest)], axis=0)
    row = lax.broadcasted_iota(jnp.int32, (NOBS, LAT), 0)

    def block(b, _):
        hot = jnp.where(row == order[b], 1.0, 0.0).astype(BF16)
        got = jnp.dot(parts, hot, preferred_element_type=F32)
        out[b] = got[0:8] + got[8:16] + got[16:24]
        return 0

    lax.fori_loop(0, BLOCKS, block, 0)


def in_order(order, facts):
    return pl.pallas_call(
        sort_kernel,
        out_shape=jax.ShapeDtypeStruct((BLOCKS, 8, LAT), F32),
        in_specs=[VMEM, VMEM],
        out_specs=VMEM,
        compiler_params=PARAMS,
        name="obs_in_batch_order",
    )(order.reshape(BLOCKS, 1, LAT), facts)


def dot_nt(a, b):
    return lax.dot_general(a, b, (((1,), (1,)), ((), ())), preferred_element_type=F32)


def exact(a, b, dims):
    (ah, al), (bh, bl) = split(a), split(b)

    def dot(x, y):
        return lax.dot_general(x, y, (dims, ((), ())), preferred_element_type=F32)

    return dot(ah, bh) + (dot(ah, bl) + dot(al, bh))


def paired(high, low):
    top = jnp.concatenate([high, low], axis=1)
    bottom = jnp.concatenate([high, jnp.zeros_like(low)], axis=1)
    return jnp.concatenate([top, bottom], axis=0).astype(BF16)


def batch_facts(facts):
    return [jnp.concatenate([facts[b * 4 + i] for i in range(4)], axis=1) for b in range(2)]


def finder(place, fact):
    west, south = place[0].astype(F32), place[1].astype(F32)
    later_than = lax.broadcasted_iota(jnp.int32, (BATCH, BATCH), 0)
    later_than = later_than <= lax.broadcasted_iota(jnp.int32, (BATCH, BATCH), 1)
    upper = jnp.where(later_than, 1.0, 0.0).astype(BF16)
    number = lax.broadcasted_iota(jnp.int32, (SLOTS, BATCH), 0).astype(F32)
    lane = lax.broadcasted_iota(jnp.int32, (1, SLOTS), 1).astype(F32)
    row = lax.broadcasted_iota(jnp.int32, (SHARE, SLOTS), 0).astype(F32)
    rel, lat = [], []
    for b in range(2):
        r = fact[b][0:1] - west
        r = jnp.where(r < -float(NLON // 2 - WIDTH // 2), r + NLON, r)
        r = jnp.where(r >= float(NLON // 2 + WIDTH // 2), r - NLON, r)
        rel.append(r)
        lat.append(fact[b][1:2] - south)

    def near(b, lo, hi):
        dl = jnp.maximum(jnp.maximum(lo - rel[b], rel[b] - hi), 0.0)
        dr = jnp.maximum(jnp.maximum(-lat[b], lat[b] - (SHARE - 1.0)), 0.0)
        flag = jnp.where(dl * dl + dr * dr < float(RADIUS * RADIUS), 1.0, 0.0)
        upto = jnp.dot(
            jnp.broadcast_to(flag, (16, BATCH)).astype(BF16), upper, preferred_element_type=F32
        )[0:1]
        return jnp.where(flag > 0.0, upto - 1.0, -float(NOBS)), jnp.sum(flag)

    def hot(slot, shift):
        return jnp.where(slot == number + shift, 1.0, 0.0).astype(BF16)

    def spot(b, h):
        both = jnp.concatenate(
            [jnp.broadcast_to(rel[b], (8, BATCH)), jnp.broadcast_to(lat[b], (8, BATCH))], axis=0
        )
        high, low = split(both)
        got = dot_nt(high, h) + dot_nt(low, h)
        return got[0:1], got[8:9]

    def placed(lon, up, used, mean):
        gap = row - up
        base = jnp.where(lane < used, 1.0 - gap * gap * SCALE, -1.0)
        base = jnp.where(lane == mean, 1.0, base)
        scale = jnp.where(lane == mean, 0.0, SCALE)
        rows = [jnp.broadcast_to(a, (8, SLOTS)) for a in (lon, scale)]
        return jnp.concatenate([base] + rows, axis=0)

    return near, hot, spot, placed


def prepare_kernel(place, facts, hots, taper, where, count):
    fact = batch_facts(facts)
    near, hot, spot, placed = finder(place, fact)

    def column(a):
        tall = jnp.transpose(jnp.broadcast_to(a, (LAT, BATCH)))
        return jnp.concatenate([tall] * (BATCH // LAT), axis=1)

    east = jnp.abs(column(fact[0][0:1]) - fact[1][0:1])
    east = jnp.minimum(east, NLON - east)
    up = column(fact[0][1:2]) - fact[1][1:2]
    t = jnp.maximum(1.0 - (east * east + up * up) * SCALE, 0.0)
    taper[...] = t * t
    full = jnp.float32(0.0)
    for q, (lo, hi) in enumerate(((0.0, CUT - 1.0), (float(CUT), WIDTH - 1.0))):
        slot1, n1 = near(0, lo, hi)
        slot2, n2 = near(1, lo, hi)
        full = jnp.maximum(full, n1 + n2)
        h1, h2 = hot(slot1, 0.0), hot(slot2, -n1)
        hots[q, 0], hots[q, 1] = h1, h2
        (lon1, lat1), (lon2, lat2) = spot(0, h1), spot(1, h2)
        where[q] = placed(lon1 + lon2, lat1 + lat2, n1 + n2, MEAN)
    count[0] = jnp.where(full > MEAN, 1, 0)


def prepare(place, facts):
    return pl.pallas_call(
        prepare_kernel,
        out_shape=[
            jax.ShapeDtypeStruct((2, 2, SLOTS, BATCH), BF16),
            jax.ShapeDtypeStruct((BATCH, BATCH), F32),
            jax.ShapeDtypeStruct((2, SHARE + 16, SLOTS), F32),
            jax.ShapeDtypeStruct((1,), jnp.int32),
        ],
        in_specs=[SMEM, VMEM],
        out_specs=[VMEM] * 3 + [SMEM],
        compiler_params=PARAMS,
        name="list_observations",
    )(place, facts)


def members_to_lanes(state, g, n, mid, halves):
    for s in range(8):
        tile = jnp.transpose(state[s, pl.ds(g, 8)].reshape(8 * SHARE, LAT))
        for j in range(8):
            mid[j, pl.ds(s * SHARE, SHARE), :] = tile[j * SHARE : (j + 1) * SHARE]
    for j in range(8):
        pair = jnp.concatenate(split(jnp.transpose(mid[j])), axis=1)
        for i in range(n):
            halves(i, j, pair[i * SHARE : (i + 1) * SHARE])


def arrange_kernel(parts, out, state, mid, halves, sems, stores):
    sets = [(g, min(8, INSIDE - g)) for g in range(0, INSIDE, 8)]
    loads = [
        pltpu.make_async_copy(parts.at[:, pl.ds(g, n)], state.at[:, pl.ds(g, n)], sems.at[t])
        for t, (g, n) in enumerate(sets)
    ]
    for c in loads:
        c.start()
    saves = []
    for t, (g, n) in enumerate(sets):
        loads[t].wait()

        def put(i, j, pair):
            halves[g + i, j] = pair

        members_to_lanes(state, g, n, mid, put)
        saves.append(
            pltpu.make_async_copy(halves.at[pl.ds(g, n)], out.at[pl.ds(g, n)], stores.at[t])
        )
        saves[-1].start()
    for c in saves:
        c.wait()


def arrange(parts):
    shape = jax.ShapeDtypeStruct((INSIDE, 8, SHARE, 2 * MEMBERS), BF16)
    return pl.pallas_call(
        arrange_kernel,
        out_shape=shape,
        in_specs=[ANY],
        out_specs=ANY,
        scratch_shapes=[
            pltpu.VMEM((BANDS, SETS * 8, SHARE, LAT), F32),
            pltpu.VMEM((8, MEMBERS, LAT), F32),
            pltpu.VMEM(shape.shape, BF16),
            pltpu.SemaphoreType.DMA((SETS,)),
            pltpu.SemaphoreType.DMA((SETS,)),
        ],
        compiler_params=PARAMS,
        name="arrange_members",
    )(parts)


def analyse_kernel(
    place, many, p0, p1, p2, p3, facts, where, hots_in, taper_in, given, given_edges, out,
    hots, taper, state, edges, mid, table, lead, link, gain, shapes, made, big, long_lead, long_gain, long_where, sems, stores,
):
    loads = [
        pltpu.make_async_copy(taper_in, taper, sems.at[FIELDS + 1]),
        pltpu.make_async_copy(hots_in, hots, sems.at[FIELDS + 2]),
    ]

    def inside(f):
        at = pl.ds(f * INNER, INNER)
        return pltpu.make_async_copy(given.at[at], state.at[at], sems.at[f])

    at = pl.ds(FIELDS * INNER, 2)
    tail = pltpu.make_async_copy(given.at[at], state.at[at], sems.at[FIELDS])
    sides = pltpu.make_async_copy(given_edges, edges.at[:, pl.ds(0, FIELDS)], sems.at[FIELDS + 3])
    for c in loads + [sides, tail] + [inside(f) for f in range(FIELDS)]:
        c.start()

    me = place[2]
    for x, got in enumerate((p0, p1, p2, p3)):
        for z in range(2):
            at = pl.multiple_of((me ^ (4 * z + x)) * SHARE, SHARE)
            for b in range(BLOCKS):
                table[pl.ds(at, SHARE), pl.ds(b * LAT, LAT)] = got[z, b]
    fact = batch_facts(facts)

    def adjust(picked, b):
        values, errors = fact[b][2:3], fact[b][3:4]
        mean = jnp.sum(picked, axis=0, keepdims=True) * (1.0 / MEMBERS)
        anomalies = picked - mean
        variance = jnp.sum(anomalies * anomalies, axis=0, keepdims=True) / (MEMBERS - 1) + 1e-6
        innovation = values - mean
        ratio = jnp.sum(innovation * innovation, axis=1, keepdims=True) / jnp.sum(
            variance + errors, axis=1, keepdims=True
        )
        root = jnp.sqrt(ratio)
        inflated = ratio * variance
        spread = root * anomalies
        post_var = 1.0 / (1.0 / inflated + 1.0 / errors)
        post_mean = post_var * (mean / inflated + values / errors)
        increments = post_mean - mean + (jnp.sqrt(post_var / inflated) - 1.0) * spread
        return root, spread * (1.0 / ((MEMBERS - 1) * inflated)), increments

    root1, scaled1, inc1 = adjust(table[:, pl.ds(0, BATCH)], 0)

    later = table[:, pl.ds(BATCH, BATCH)]
    mean = jnp.sum(later, axis=0, keepdims=True) * (1.0 / MEMBERS)
    spread = root1 * (later - mean)
    cov = exact(jnp.transpose(scaled1), spread, ((1,), (0,)))
    for c in loads:
        c.wait()
    later = (mean + spread) + exact(inc1, taper[...] * cov, ((1,), (0,)))
    root2, scaled2, inc2 = adjust(later, 1)
    both_roots = jnp.sum(root1 * root2)

    sp1, sp2 = split(root1 * scaled1), split(root1 * root2 * scaled2)
    shift1 = jnp.sum(inc1, axis=0, keepdims=True) * (1.0 / MEMBERS)
    free1 = inc1 - shift1
    g1, g2 = split(root2 * free1 + shift1), split(inc2)
    f1, s2 = split(free1), split(root2 * scaled2)
    lane = lax.broadcasted_iota(jnp.int32, (1, SLOTS), 1)
    tall = lax.broadcasted_iota(jnp.int32, (SLOTS, 1), 0)
    rest = [a.astype(F32) for a in split(1.0 - root1 * root2)]
    for q in range(2):
        h1, h2 = hots[q, 0], hots[q, 1]
        lead_h, lead_l = [dot_nt(a, h1) + dot_nt(b, h2) for a, b in zip(sp1, sp2)]
        lead[q] = paired(jnp.where(lane == MEAN, 1.0 / MEMBERS, lead_h), lead_l)
        gain_h, gain_l = [dot_nt(h1, a) + dot_nt(h2, b) for a, b in zip(g1, g2)]
        gain[q] = paired(
            jnp.where(tall == MEAN, rest[0], gain_h), jnp.where(tall == MEAN, rest[1], gain_l)
        )
        one = dot_nt(h1, f1[0]) + dot_nt(h1, f1[1])
        two = dot_nt(h2, s2[0]) + dot_nt(h2, s2[1])
        link[q] = paired(*split(exact(one, two, ((1,), (1,)))))

    def put_edge(i, j, pair):
        state[INSIDE + i, j] = pair

    sides.wait()
    members_to_lanes(edges, 0, FIELDS, mid, put_edge)
    tail.wait()

    def times(pair, m):
        got = jnp.dot(pair, m, preferred_element_type=F32)
        return got[:, :MEMBERS] + got[:, MEMBERS:]

    def product(a, m):
        return times(jnp.concatenate(split(a), axis=1), m)

    def taper_of(spots, lon):
        base, at, scale = spots[0:SHARE], spots[SHARE : SHARE + 1], spots[SHARE + 8 : SHARE + 9]
        gap = at - lon
        t = jnp.maximum(base - gap * gap * scale, 0.0)
        return t * t

    def whole(pair):
        return pair[:, :MEMBERS].astype(F32) + pair[:, MEMBERS:].astype(F32)

    def short(pair, t, q):
        cov = times(pair, lead[q])
        cov = cov + product(t * cov, link[q])
        return both_roots * whole(pair) + product(t * cov, gain[q])

    def block(g, n):
        return state[pl.ds(g, n)].reshape(n * 8 * SHARE, 2 * MEMBERS)

    def part(g, at, n):
        return state[g, pl.ds(at, n)].reshape(n * SHARE, 2 * MEMBERS)

    def put_rest(x):
        for f in range(FIELDS):
            put(f, REST_AT, x[f * 2 * SHARE : (f + 1) * 2 * SHARE], 2)

    def put(f, lon, x, n):
        made[f, pl.ds(lon, n)] = x.reshape(n, SHARE, MEMBERS)

    def store(f):
        return pltpu.make_async_copy(made.at[f], out.at[f], stores.at[f])

    @pl.when(many[0] == 0)
    def _():
        for q, (lo, hi) in enumerate(((0, CUT), (CUT, WIDTH))):
            for lon in range(lo, hi):
                shapes[lon] = taper_of(where[q], float(lon))

        def shape(lon, n):
            return shapes[pl.ds(lon, n)].reshape(n * SHARE, SLOTS)

        pair = jnp.concatenate([block(INSIDE - 2, 1), part(INSIDE - 1, 0, 2)], axis=0)
        put_rest(short(pair, jnp.concatenate([shape(REST_AT, 2)] * FIELDS, axis=0), 1))

        def some(fs):
            for f in fs:
                inside(f).wait()
            n = INNER // 2
            for q, lon, edge in ((0, EDGE, 0), (1, CUT, WIDTH - EDGE)):
                pair = jnp.concatenate(
                    [
                        a
                        for f in fs
                        for a in (block(f * INNER + q * n, n), part(INSIDE + f, q * EDGE, EDGE))
                    ],
                    axis=0,
                )
                t = jnp.concatenate([shape(lon, 8 * n), shape(edge, EDGE)] * len(fs), axis=0)
                x = short(pair, t, q)
                r, m = (8 * n + EDGE) * SHARE, 8 * n * SHARE
                for i, f in enumerate(fs):
                    put(f, lon, x[i * r : i * r + m], 8 * n)
                    put(f, edge, x[i * r + m : (i + 1) * r], EDGE)
            for f in fs:
                store(f).start()

        some([0, 1])
        some([2, 3])
        some([4])

    @pl.when(many[0] != 0)
    def _():
        near, hot, spot, placed = finder(place, fact)
        roots = [jnp.sum(root1), jnp.sum(root2)]
        chunks = []
        for b, (sp, g) in enumerate(((split(scaled1), split(inc1)), (split(scaled2), g2))):
            slot, n = near(b, 0.0, WIDTH - 1.0)
            chunks.append((n.astype(jnp.int32) + SLOTS - 1) // SLOTS)
            for c in range(CHUNKS):
                h = hot(slot, float(c * SLOTS))
                long_lead[b, c] = paired(dot_nt(sp[0], h), dot_nt(sp[1], h))
                long_gain[b, c] = paired(dot_nt(h, g[0]), dot_nt(h, g[1]))
                lon, up = spot(b, h)
                long_where[b, c] = placed(lon, up, n - float(c * SLOTS), -1)
        for f in range(FIELDS):
            inside(f).wait()

        def long(pair, lons):
            x = whole(pair)
            for b in range(2):
                mean = jnp.sum(x, axis=1, keepdims=True) * (1.0 / MEMBERS)
                anomaly = x - mean
                big[pl.ds(0, x.shape[0]), :] = x + (roots[b] - 1.0) * anomaly
                anomaly = roots[b] * anomaly

                def chunk(c, _):
                    t = jnp.concatenate([taper_of(long_where[b, c], lon) for lon in lons], axis=0)
                    w = t * product(anomaly, long_lead[b, c])
                    big[pl.ds(0, x.shape[0]), :] += product(w, long_gain[b, c])
                    return 0

                lax.fori_loop(0, chunks[b], chunk, 0)
                x = big[pl.ds(0, x.shape[0]), :]
            return x

        def each(g, _):
            f, lon = g // INNER, 8 * (g % INNER) + EDGE
            at = lon.astype(F32)
            put(f, lon, long(block(g, 1), [at + j for j in range(8)]), 8)
            return 0

        lax.fori_loop(0, FIELDS * INNER, each, 0)
        last = long(part(INSIDE - 1, 0, 2), [float(REST_AT + j) for j in range(2)])
        first = long(block(INSIDE - 2, 1), [float(REST_AT + j % 2) for j in range(8)])
        put_rest(jnp.concatenate([first, last], axis=0))
        for f in range(FIELDS):
            for at, lon in ((0, 0), (EDGE, WIDTH - EDGE)):
                lons = [float(lon + j) for j in range(EDGE)]
                put(f, lon, long(part(INSIDE + f, at, EDGE), lons), EDGE)
        for f in range(FIELDS):
            store(f).start()

    for f in range(FIELDS):
        store(f).wait()


def analyse(place, many, priors, facts, where, hots, taper, state, sides):
    square = (2 * SLOTS, 2 * MEMBERS)
    return pl.pallas_call(
        analyse_kernel,
        out_shape=jax.ShapeDtypeStruct((FIELDS, WIDTH, SHARE, MEMBERS), F32),
        in_specs=[SMEM] * 2 + [VMEM] * 6 + [ANY] * 4,
        out_specs=ANY,
        scratch_shapes=[
            pltpu.VMEM(hots.shape, BF16),
            pltpu.VMEM(taper.shape, F32),
            pltpu.VMEM((GROUPS,) + state.shape[1:], BF16),
            pltpu.VMEM((BANDS, 8, SHARE, LAT), F32),
            pltpu.VMEM((8, MEMBERS, LAT), F32),
            pltpu.VMEM((MEMBERS, NOBS), F32),
            pltpu.VMEM((2,) + square, BF16),
            pltpu.VMEM((2,) + square, BF16),
            pltpu.VMEM((2,) + square, BF16),
            pltpu.VMEM((WIDTH, SHARE, SLOTS), F32),
            pltpu.VMEM((FIELDS, WIDTH, SHARE, MEMBERS), F32),
            pltpu.VMEM((8 * SHARE, MEMBERS), F32),
            pltpu.VMEM((2, CHUNKS) + square, BF16),
            pltpu.VMEM((2, CHUNKS) + square, BF16),
            pltpu.VMEM((2, CHUNKS, SHARE + 16, SLOTS), F32),
            pltpu.SemaphoreType.DMA((FIELDS + 4,)),
            pltpu.SemaphoreType.DMA((FIELDS,)),
        ],
        compiler_params=PARAMS,
        name="analyse",
    )(place, many, *priors, facts, where, hots, taper, state, sides)


def across(x, axis, bits):
    count = lax.axis_size(axis)
    return lax.ppermute(x, axis, [(i, i ^ bits) for i in range(count)])


def shards(
    ensemble,
    ocean_depth,
    planetary_vorticity,
    land_mask,
    obs_values,
    obs_error,
    obs_lon,
    obs_lat,
    obs_field,
    obs_order,
):
    member, sector = lax.axis_index("member"), lax.axis_index("sector")
    sectors = lax.axis_size("sector")
    vort = planetary_vorticity.reshape(1, LAT)
    ens = jnp.transpose(ensemble, (1, 2, 0, 3))
    west_side, east_side = edges(ens, ocean_depth, land_mask)
    left = lax.ppermute(east_side, "sector", [(i, (i + 1) % sectors) for i in range(sectors)])
    right = lax.ppermute(west_side, "sector", [((i + 1) % sectors, i) for i in range(sectors)])

    lon_f, lat_f = obs_lon.astype(F32), obs_lat.astype(F32)
    facts = in_order(
        obs_order, jnp.stack([lon_f, lat_f, obs_values, obs_error] + [jnp.zeros_like(lon_f)] * 4)
    )
    west = sector * WIDTH
    here = obs_lon - west
    cell = ((obs_field - 2) * WIDTH + here) * LAT + obs_lat
    cell = jnp.where((here >= 0) & (here < WIDTH), cell, -1)
    place = jnp.stack([west, member * SHARE, member])
    hots, taper, where, many = prepare(place, facts)

    messages, seen = forecast_inner(ens, ocean_depth, land_mask, vort)
    parts = lax.all_to_all(messages, "member", split_axis=0, concat_axis=0, tiled=True)
    sides, seen = forecast_outer(ens, left, right, ocean_depth, land_mask, vort, seen)
    sides = lax.all_to_all(sides, "member", split_axis=0, concat_axis=0, tiled=True)

    own = pick(obs_order, cell, seen.reshape(3 * WIDTH, SHARE, LAT), where)
    own = (own + across(own, "sector", 2)) + (across(own, "sector", 4) + across(own, "sector", 6))
    own = own + across(own, "sector", 1)
    axes = ("member", "sector")
    count = lax.axis_size("member") * sectors
    both = lax.ppermute(own, axes, [(i, i ^ (4 * sectors + 8)) for i in range(count)])
    low, high = across(own, "sector", 8), across(own, "member", 4)
    own = jnp.stack([own, high]) + jnp.stack([low, both])
    priors = [own] + [across(own, "member", x) for x in (1, 2, 3)]
    analysis = analyse(place, many, priors, facts, where, hots, taper, arrange(parts), sides)
    return jnp.transpose(analysis, (0, 2, 1, 3))


def solution(mesh):
    placed = (
        P("member", None, "sector", None),
        P("sector", None),
        P(),
        P("sector", None),
        P(),
        P(),
        P(),
        P(),
        P(),
        P(),
    )
    return jax.shard_map(
        shards,
        mesh=mesh,
        in_specs=placed,
        out_specs=P(None, "member", "sector", None),
        check_vma=False,
    )
```

```python
import jax
import jax.numpy as jnp
from jax import lax
from jax.experimental import pallas as pl
from jax.experimental.pallas import tpu as pltpu
from jax.sharding import PartitionSpec as P

NLON = 1440
LAT = 128
FIELDS = 5
MEMBERS = 128
NOBS = 1024
BATCH = 512
BLOCKS = NOBS // LAT
RADIUS = 48
SHARE = 16
BANDS = 8
WIDTH = 90
EDGE = 4
INNER = 10
REST_AT = EDGE + 8 * INNER
INSIDE = FIELDS * INNER + 2
GROUPS = INSIDE + FIELDS
RIGHT = 80
SETS = (INSIDE + 7) // 8
CUT = 44
SLOTS = 128
CHUNKS = BATCH // SLOTS
MEAN = SLOTS - 1
SCALE = 1.0 / (RADIUS * RADIUS)
F32 = jnp.float32
BF16 = jnp.bfloat16
SMEM = pl.BlockSpec(memory_space=pltpu.SMEM)
VMEM = pl.BlockSpec(memory_space=pltpu.VMEM)
ANY = pl.BlockSpec(memory_space=pl.ANY)
PARAMS = pltpu.CompilerParams(vmem_limit_bytes=56 * 1024 * 1024)


def edges_kernel(ens, depth, mask, west, east, deep, sea, sems):
    sides = ((west, 0), (east, WIDTH - EDGE))
    grids = ((0, 0, 8), (RIGHT, 8, WIDTH - RIGHT))
    copies = [
        pltpu.make_async_copy(ens.at[:, pl.ds(lon, EDGE)], out.at[pl.ds(0, FIELDS)], sems.at[i])
        for i, (out, lon) in enumerate(sides)
    ]
    for i, (lon, at, n) in enumerate(grids):
        for j, (grid, to) in enumerate(((depth, deep), (mask, sea))):
            copies.append(
                pltpu.make_async_copy(
                    grid.at[pl.ds(lon, n)], to.at[pl.ds(at, n)], sems.at[2 + 2 * i + j]
                )
            )
    for c in copies:
        c.start()
    for c in copies:
        c.wait()
    for (out, lon), (start, at, _) in zip(sides, grids):
        rows = pl.ds(at + lon - start, EDGE)
        out[FIELDS, 0, pl.ds(0, 8), :] = jnp.concatenate([deep[rows, :], sea[rows, :].astype(F32)], axis=0)


def edges(ens, depth, mask):
    side = jax.ShapeDtypeStruct((FIELDS + 1, EDGE, SHARE, LAT), F32)
    return pl.pallas_call(
        edges_kernel,
        out_shape=[side, side],
        in_specs=[ANY, ANY, ANY],
        out_specs=[VMEM, VMEM],
        scratch_shapes=[
            pltpu.VMEM((24, LAT), F32),
            pltpu.VMEM((24, LAT), jnp.int32),
            pltpu.SemaphoreType.DMA((6,)),
        ],
        compiler_params=PARAMS,
        name="pack_edges",
    )(ens, depth, mask)


def split(a):
    high = a.astype(BF16)
    return high, (a - high.astype(F32)).astype(BF16)


def bands(out):
    row = lax.broadcasted_iota(jnp.int32, (2 * LAT, 2 * LAT), 0) % LAT
    col = lax.broadcasted_iota(jnp.int32, (2 * LAT, 2 * LAT), 1)
    gap = row - col % LAT
    value = jnp.where(jnp.abs(gap) == 1, jnp.where(col < LAT, gap, 1), 0)
    out[...] = value.astype(F32).astype(BF16)


def stepper(dep, sea, vort, flux, band):
    spin = jnp.broadcast_to(vort[...], (SHARE, LAT))

    def halves(tiles):
        return jnp.concatenate(split(jnp.concatenate(tiles, axis=0)), axis=1)

    def difference(tiles):
        got = jnp.dot(halves(tiles), band[:, 0:LAT], preferred_element_type=F32)
        return [got[i * SHARE : (i + 1) * SHARE] for i in range(len(tiles))]

    def both(tiles):
        got = jnp.dot(halves(tiles), band[...], preferred_element_type=F32)
        rows = [got[i * SHARE : (i + 1) * SHARE] for i in range(len(tiles))]
        return [r[:, 0:LAT] for r in rows], [r[:, LAT:] for r in rows]

    def flow(src, dst, places):
        slope = difference([src[2, e] for e, _ in places])
        for (e, row), dh in zip(places, slope):
            u, v = src[0, e], src[1, e]
            m = sea[pl.ds(row, 1), :]
            un = m * (u + spin * v - 0.15 * (src[2, e + 1] - src[2, e - 1]))
            dst[0, e] = un
            dst[1, e] = m * (v - spin * u - 0.15 * dh)
            flux[e] = dep[pl.ds(row, 1), :] * un

    def others(src, dst, places):
        slope = difference([dep[pl.ds(row, 1), :] * dst[1, e] for e, row in places])
        for (e, _), dv in zip(places, slope):
            dst[2, e] = src[2, e] - 0.15 * (flux[e + 1] - flux[e - 1] + dv)
        for c in (3, 4):
            slope, total = both([src[c, e] for e, _ in places])
            for (e, _), dc, around in zip(places, slope, total):
                a, ae, aw = src[c, e], src[c, e + 1], src[c, e - 1]
                dst[c, e] = (
                    a
                    - 0.15 * (dst[0, e] * (ae - aw) + dst[1, e] * dc)
                    + 0.1 * (((ae + aw) + around) - 4.0 * a)
                )

    return flow, others


def in_blocks(stage, src, dst, lo, hi, row, n):
    def block(i, _):
        e = jnp.minimum(lo + i * n, hi - n)
        stage(src, dst, [(e + k, e + k + row) for k in range(n)])
        return 0

    lax.fori_loop(0, (hi - lo + n - 1) // n, block, 0)


def turn(tiles, out, g):
    tile = jnp.transpose(tiles.reshape(8 * SHARE, LAT))
    for b in range(BANDS):
        out[b, g] = tile[b * SHARE : (b + 1) * SHARE]


def inner_kernel(ens, depth, mask, vort, out, seen, now, nxt, flux, sea, band, made, sems):
    half = WIDTH // 2
    loads = [
        pltpu.make_async_copy(ens.at[:, pl.ds(at, n)], now.at[:, pl.ds(at, n)], sems.at[2 + i])
        for i, (at, n) in enumerate(((0, half + 1), (half + 1, half - 1)))
    ]
    for c in loads:
        c.start()
    sea[...] = mask[...].astype(F32)
    bands(band)
    flow, others = stepper(depth, sea, vort, flux, band)
    for at, c in zip((1, half), loads):
        c.wait()
        flow(now, nxt, [(at + k, at + k) for k in range(half - 1)])
    for d, stage, src, dst in ((2, others, now, nxt), (3, flow, nxt, now)):
        in_blocks(stage, src, dst, d, WIDTH - d, 0, half - d)

    def keep(i, at, n):
        return pltpu.make_async_copy(
            now.at[pl.ds(2, 3), pl.ds(at, n)], seen.at[:, pl.ds(at, n)], sems.at[i]
        )

    def send(i, g, n):
        at = pl.ds(g, n)
        return pltpu.make_async_copy(made.at[:, at], out.at[:, at], sems.at[4 + i])

    groups, sends = INNER // 2, []
    width = half - EDGE
    for part in range(2):
        at = EDGE + part * width
        others(nxt, now, [(at + k, at + k) for k in range(width)])
        sends.append(keep(part, at, width))
        sends[-1].start()
        if part == 1:
            turn(now[pl.ds(0, 4), pl.ds(REST_AT, 2)], made, INSIDE - 2)
            turn(jnp.concatenate([now[4, pl.ds(REST_AT, 2)]] * 4, axis=0), made, INSIDE - 1)
            sends.append(send(2 * FIELDS, INSIDE - 2, 2))
            sends[-1].start()
        for f in range(FIELDS):
            for i in range(part * groups, (part + 1) * groups):
                turn(now[f, pl.ds(EDGE + i * 8, 8)], made, f * INNER + i)
            sends.append(send(part * FIELDS + f, f * INNER + part * groups, groups))
            sends[-1].start()
    for c in sends:
        c.wait()


def forecast_inner(ens, depth, mask, vort):
    return pl.pallas_call(
        inner_kernel,
        out_shape=[
            jax.ShapeDtypeStruct((BANDS, INSIDE, SHARE, LAT), F32),
            jax.ShapeDtypeStruct((3, WIDTH, SHARE, LAT), F32),
        ],
        in_specs=[ANY, VMEM, VMEM, VMEM],
        out_specs=[ANY, ANY],
        scratch_shapes=[
            pltpu.VMEM((FIELDS, WIDTH, SHARE, LAT), F32),
            pltpu.VMEM((FIELDS, WIDTH, SHARE, LAT), F32),
            pltpu.VMEM((WIDTH, SHARE, LAT), F32),
            pltpu.VMEM((WIDTH, LAT), F32),
            pltpu.VMEM((2 * LAT, 2 * LAT), BF16),
            pltpu.VMEM((BANDS, INSIDE, SHARE, LAT), F32),
            pltpu.SemaphoreType.DMA((5 + 2 * FIELDS,)),
        ],
        compiler_params=PARAMS,
        name="forecast_inner",
    )(ens, depth, mask, vort)


def outer_kernel(
    ens, left, right, depth, mask, vort, _, out, seen, now, nxt, flux, dep, sea, band, made, sems
):
    own = 2 * EDGE
    second = own + EDGE
    loads = [
        pltpu.make_async_copy(ens.at[:, pl.ds(0, own)], now.at[:, pl.ds(EDGE, own)], sems.at[0]),
        pltpu.make_async_copy(
            ens.at[:, pl.ds(WIDTH - own, own)], now.at[:, pl.ds(second, own)], sems.at[1]
        ),
        pltpu.make_async_copy(left.at[pl.ds(0, FIELDS)], now.at[:, pl.ds(0, EDGE)], sems.at[2]),
        pltpu.make_async_copy(
            right.at[pl.ds(0, FIELDS)], now.at[:, pl.ds(second + own, EDGE)], sems.at[3]
        ),
    ]
    for c in loads:
        c.start()
    for grid, whole, at in ((dep, depth, 0), (sea, mask, EDGE)):
        grid[pl.ds(8, WIDTH), :] = whole[...].astype(F32)
        grid[pl.ds(4, EDGE), :] = left[FIELDS, 0, pl.ds(at, EDGE), :]
        grid[pl.ds(8 + WIDTH, EDGE), :] = right[FIELDS, 0, pl.ds(at, EDGE), :]
    bands(band)
    flow, others = stepper(dep, sea, vort, flux, band)
    for c in loads:
        c.wait()
    end = second + own + EDGE
    skip = 8 + WIDTH - own - second
    for d, stage, src, dst in (
        (1, flow, now, nxt),
        (2, others, now, nxt),
        (3, flow, nxt, now),
        (4, others, nxt, now),
    ):
        places = [(e, e + 4) for e in range(d, second - d)]
        stage(src, dst, places + [(e, e + skip) for e in range(second + d, end - d)])
    keeps = [
        pltpu.make_async_copy(
            now.at[pl.ds(2, 3), pl.ds(at, EDGE)], seen.at[:, pl.ds(lon, EDGE)], sems.at[i]
        )
        for i, (at, lon) in enumerate(((EDGE, 0), (second + EDGE, WIDTH - EDGE)))
    ]
    for c in keeps:
        c.start()
    for f in range(FIELDS):
        sides = [now[f, pl.ds(EDGE, EDGE)], now[f, pl.ds(second + EDGE, EDGE)]]
        turn(jnp.concatenate(sides, axis=0), made, f)
    send = pltpu.make_async_copy(made, out, sems.at[2])
    send.start()
    for c in [send] + keeps:
        c.wait()


def forecast_outer(ens, left, right, depth, mask, vort, seen):
    window = 6 * EDGE
    messages = jax.ShapeDtypeStruct((BANDS, FIELDS, SHARE, LAT), F32)
    return pl.pallas_call(
        outer_kernel,
        out_shape=[messages, jax.ShapeDtypeStruct(seen.shape, F32)],
        in_specs=[ANY] + [VMEM] * 5 + [ANY],
        out_specs=[ANY] * 2,
        scratch_shapes=[
            pltpu.VMEM((FIELDS, window, SHARE, LAT), F32),
            pltpu.VMEM((FIELDS, window, SHARE, LAT), F32),
            pltpu.VMEM((window, SHARE, LAT), F32),
            pltpu.VMEM((112, LAT), F32),
            pltpu.VMEM((112, LAT), F32),
            pltpu.VMEM((2 * LAT, 2 * LAT), BF16),
            pltpu.VMEM((BANDS, FIELDS, SHARE, LAT), F32),
            pltpu.SemaphoreType.DMA((4,)),
        ],
        input_output_aliases={6: 1},
        compiler_params=PARAMS,
        name="forecast_outer",
    )(ens, left, right, depth, mask, vort, seen)


def pick_kernel(order, cell, seen, _, out, own):
    lane = lax.broadcasted_iota(jnp.int32, (SHARE, LAT), 1)

    def listed(i, n):
        codes = [cell[order[i * 16 + k]] for k in range(16)]
        for k, at in enumerate(codes):
            own[n] = at + (i * 16 + k) * (1 << 16)
            n = n + jnp.where(at >= 0, 1, 0)
        return n

    total = lax.fori_loop(0, NOBS // 16, listed, 0)
    out[...] = jnp.zeros_like(out)

    def some(i, _):
        found = []
        for k in range(8):
            valid = i * 8 + k < total
            code = jnp.where(valid, own[i * 8 + k], 0)
            j, at, lat = code >> 16, (code >> 7) & 511, code & 127
            tile = pltpu.roll(seen[at], (j - lat) & (LAT - 1), 1)
            found.append((j >> 7, jnp.where(valid, j & 127, -1), tile))
        for b, r, tile in found:
            out[b] = jnp.where(lane == r, tile, out[b])
        return 0

    lax.fori_loop(0, (total + 7) // 8, some, 0)


def pick(order, cell, seen, before):
    return pl.pallas_call(
        pick_kernel,
        out_shape=jax.ShapeDtypeStruct((BLOCKS, SHARE, LAT), F32),
        in_specs=[SMEM, SMEM, VMEM, ANY],
        out_specs=VMEM,
        scratch_shapes=[pltpu.SMEM((NOBS + 16,), jnp.int32)],
        compiler_params=PARAMS,
        name="pick_priors",
    )(order, cell, seen, before)


def sort_kernel(order, facts, out):
    data = facts[...]
    high, rest = split(data)
    left = data - high.astype(F32)
    mid, low = split(left)
    parts = jnp.concatenate([high, mid, low, jnp.zeros_like(rest)], axis=0)
    row = lax.broadcasted_iota(jnp.int32, (NOBS, LAT), 0)

    def block(b, _):
        hot = jnp.where(row == order[b], 1.0, 0.0).astype(BF16)
        got = jnp.dot(parts, hot, preferred_element_type=F32)
        out[b] = got[0:8] + got[8:16] + got[16:24]
        return 0

    lax.fori_loop(0, BLOCKS, block, 0)


def in_order(order, facts):
    return pl.pallas_call(
        sort_kernel,
        out_shape=jax.ShapeDtypeStruct((BLOCKS, 8, LAT), F32),
        in_specs=[VMEM, VMEM],
        out_specs=VMEM,
        compiler_params=PARAMS,
        name="obs_in_batch_order",
    )(order.reshape(BLOCKS, 1, LAT), facts)


def dot_nt(a, b):
    return lax.dot_general(a, b, (((1,), (1,)), ((), ())), preferred_element_type=F32)


def exact(a, b, dims):
    (ah, al), (bh, bl) = split(a), split(b)

    def dot(x, y):
        return lax.dot_general(x, y, (dims, ((), ())), preferred_element_type=F32)

    return dot(ah, bh) + (dot(ah, bl) + dot(al, bh))


def paired(high, low):
    top = jnp.concatenate([high, low], axis=1)
    bottom = jnp.concatenate([high, jnp.zeros_like(low)], axis=1)
    return jnp.concatenate([top, bottom], axis=0).astype(BF16)


def batch_facts(facts):
    return [jnp.concatenate([facts[b * 4 + i] for i in range(4)], axis=1) for b in range(2)]


def finder(place, fact):
    west, south = place[0].astype(F32), place[1].astype(F32)
    later_than = lax.broadcasted_iota(jnp.int32, (BATCH, BATCH), 0)
    later_than = later_than <= lax.broadcasted_iota(jnp.int32, (BATCH, BATCH), 1)
    upper = jnp.where(later_than, 1.0, 0.0).astype(BF16)
    number = lax.broadcasted_iota(jnp.int32, (SLOTS, BATCH), 0).astype(F32)
    lane = lax.broadcasted_iota(jnp.int32, (1, SLOTS), 1).astype(F32)
    row = lax.broadcasted_iota(jnp.int32, (SHARE, SLOTS), 0).astype(F32)
    rel, lat = [], []
    for b in range(2):
        r = fact[b][0:1] - west
        r = jnp.where(r < -float(NLON // 2 - WIDTH // 2), r + NLON, r)
        r = jnp.where(r >= float(NLON // 2 + WIDTH // 2), r - NLON, r)
        rel.append(r)
        lat.append(fact[b][1:2] - south)

    def near(b, lo, hi):
        dl = jnp.maximum(jnp.maximum(lo - rel[b], rel[b] - hi), 0.0)
        dr = jnp.maximum(jnp.maximum(-lat[b], lat[b] - (SHARE - 1.0)), 0.0)
        flag = jnp.where(dl * dl + dr * dr < float(RADIUS * RADIUS), 1.0, 0.0)
        upto = jnp.dot(
            jnp.broadcast_to(flag, (16, BATCH)).astype(BF16), upper, preferred_element_type=F32
        )[0:1]
        return jnp.where(flag > 0.0, upto - 1.0, -float(NOBS)), jnp.sum(flag)

    def hot(slot, shift):
        return jnp.where(slot == number + shift, 1.0, 0.0).astype(BF16)

    def spot(b, h):
        both = jnp.concatenate(
            [jnp.broadcast_to(rel[b], (8, BATCH)), jnp.broadcast_to(lat[b], (8, BATCH))], axis=0
        )
        high, low = split(both)
        got = dot_nt(high, h) + dot_nt(low, h)
        return got[0:1], got[8:9]

    def placed(lon, up, used, mean):
        gap = row - up
        base = jnp.where(lane < used, 1.0 - gap * gap * SCALE, -1.0)
        base = jnp.where(lane == mean, 1.0, base)
        scale = jnp.where(lane == mean, 0.0, SCALE)
        rows = [jnp.broadcast_to(a, (8, SLOTS)) for a in (lon, scale)]
        return jnp.concatenate([base] + rows, axis=0)

    return near, hot, spot, placed


def prepare_kernel(place, facts, hots, taper, where, count):
    fact = batch_facts(facts)
    near, hot, spot, placed = finder(place, fact)

    def column(a):
        tall = jnp.transpose(jnp.broadcast_to(a, (LAT, BATCH)))
        return jnp.concatenate([tall] * (BATCH // LAT), axis=1)

    east = jnp.abs(column(fact[0][0:1]) - fact[1][0:1])
    east = jnp.minimum(east, NLON - east)
    up = column(fact[0][1:2]) - fact[1][1:2]
    t = jnp.maximum(1.0 - (east * east + up * up) * SCALE, 0.0)
    taper[...] = t * t
    full = jnp.float32(0.0)
    for q, (lo, hi) in enumerate(((0.0, CUT - 1.0), (float(CUT), WIDTH - 1.0))):
        slot1, n1 = near(0, lo, hi)
        slot2, n2 = near(1, lo, hi)
        full = jnp.maximum(full, n1 + n2)
        h1, h2 = hot(slot1, 0.0), hot(slot2, -n1)
        hots[q, 0], hots[q, 1] = h1, h2
        (lon1, lat1), (lon2, lat2) = spot(0, h1), spot(1, h2)
        where[q] = placed(lon1 + lon2, lat1 + lat2, n1 + n2, MEAN)
    count[0] = jnp.where(full > MEAN, 1, 0)


def prepare(place, facts):
    return pl.pallas_call(
        prepare_kernel,
        out_shape=[
            jax.ShapeDtypeStruct((2, 2, SLOTS, BATCH), BF16),
            jax.ShapeDtypeStruct((BATCH, BATCH), F32),
            jax.ShapeDtypeStruct((2, SHARE + 16, SLOTS), F32),
            jax.ShapeDtypeStruct((1,), jnp.int32),
        ],
        in_specs=[SMEM, VMEM],
        out_specs=[VMEM] * 3 + [SMEM],
        compiler_params=PARAMS,
        name="list_observations",
    )(place, facts)


def members_to_lanes(state, g, n, mid, halves):
    for s in range(8):
        tile = jnp.transpose(state[s, pl.ds(g, 8)].reshape(8 * SHARE, LAT))
        for j in range(8):
            mid[j, pl.ds(s * SHARE, SHARE), :] = tile[j * SHARE : (j + 1) * SHARE]
    for j in range(8):
        pair = jnp.concatenate(split(jnp.transpose(mid[j])), axis=1)
        for i in range(n):
            halves(i, j, pair[i * SHARE : (i + 1) * SHARE])


def arrange_kernel(parts, out, state, mid, halves, sems, stores):
    sets = [(g, min(8, INSIDE - g)) for g in range(0, INSIDE, 8)]
    loads = [
        pltpu.make_async_copy(parts.at[:, pl.ds(g, n)], state.at[:, pl.ds(g, n)], sems.at[t])
        for t, (g, n) in enumerate(sets)
    ]
    for c in loads:
        c.start()
    saves = []
    for t, (g, n) in enumerate(sets):
        loads[t].wait()

        def put(i, j, pair):
            halves[g + i, j] = pair

        members_to_lanes(state, g, n, mid, put)
        saves.append(
            pltpu.make_async_copy(halves.at[pl.ds(g, n)], out.at[pl.ds(g, n)], stores.at[t])
        )
        saves[-1].start()
    for c in saves:
        c.wait()


def arrange(parts):
    shape = jax.ShapeDtypeStruct((INSIDE, 8, SHARE, 2 * MEMBERS), BF16)
    return pl.pallas_call(
        arrange_kernel,
        out_shape=shape,
        in_specs=[ANY],
        out_specs=ANY,
        scratch_shapes=[
            pltpu.VMEM((BANDS, SETS * 8, SHARE, LAT), F32),
            pltpu.VMEM((8, MEMBERS, LAT), F32),
            pltpu.VMEM(shape.shape, BF16),
            pltpu.SemaphoreType.DMA((SETS,)),
            pltpu.SemaphoreType.DMA((SETS,)),
        ],
        compiler_params=PARAMS,
        name="arrange_members",
    )(parts)


def analyse_kernel(
    place, many, p0, p1, p2, p3, facts, where, hots_in, taper_in, given, given_edges, out,
    hots, taper, state, edges, mid, table, lead, link, gain, shapes, made, big, long_lead, long_gain, long_where, sems, stores,
):
    loads = [
        pltpu.make_async_copy(taper_in, taper, sems.at[FIELDS + 1]),
        pltpu.make_async_copy(hots_in, hots, sems.at[FIELDS + 2]),
    ]

    def inside(f):
        at = pl.ds(f * INNER, INNER)
        return pltpu.make_async_copy(given.at[at], state.at[at], sems.at[f])

    at = pl.ds(FIELDS * INNER, 2)
    tail = pltpu.make_async_copy(given.at[at], state.at[at], sems.at[FIELDS])
    sides = pltpu.make_async_copy(given_edges, edges.at[:, pl.ds(0, FIELDS)], sems.at[FIELDS + 3])
    for c in loads + [sides, tail] + [inside(f) for f in range(FIELDS)]:
        c.start()

    me = place[2]
    for x, got in enumerate((p0, p1, p2, p3)):
        for z in range(2):
            at = pl.multiple_of((me ^ (4 * z + x)) * SHARE, SHARE)
            for b in range(BLOCKS):
                table[pl.ds(at, SHARE), pl.ds(b * LAT, LAT)] = got[z, b]
    fact = batch_facts(facts)

    def adjust(picked, b):
        values, errors = fact[b][2:3], fact[b][3:4]
        mean = jnp.sum(picked, axis=0, keepdims=True) * (1.0 / MEMBERS)
        anomalies = picked - mean
        variance = jnp.sum(anomalies * anomalies, axis=0, keepdims=True) / (MEMBERS - 1) + 1e-6
        innovation = values - mean
        ratio = jnp.sum(innovation * innovation, axis=1, keepdims=True) / jnp.sum(
            variance + errors, axis=1, keepdims=True
        )
        root = jnp.sqrt(ratio)
        inflated = ratio * variance
        spread = root * anomalies
        post_var = 1.0 / (1.0 / inflated + 1.0 / errors)
        post_mean = post_var * (mean / inflated + values / errors)
        increments = post_mean - mean + (jnp.sqrt(post_var / inflated) - 1.0) * spread
        return root, spread * (1.0 / ((MEMBERS - 1) * inflated)), increments

    def taper_of(spots, lon):
        base, at, scale = spots[0:SHARE], spots[SHARE : SHARE + 1], spots[SHARE + 8 : SHARE + 9]
        gap = at - lon
        t = jnp.maximum(base - gap * gap * scale, 0.0)
        return t * t

    for q, (lo, hi) in enumerate(((0, CUT), (CUT, WIDTH))):
        for lon in range(lo, hi):
            shapes[lon] = taper_of(where[q], float(lon))

    root1, scaled1, inc1 = adjust(table[:, pl.ds(0, BATCH)], 0)

    later = table[:, pl.ds(BATCH, BATCH)]
    mean = jnp.sum(later, axis=0, keepdims=True) * (1.0 / MEMBERS)
    spread = root1 * (later - mean)
    cov = exact(jnp.transpose(scaled1), spread, ((1,), (0,)))
    for c in loads:
        c.wait()
    later = (mean + spread) + exact(inc1, taper[...] * cov, ((1,), (0,)))
    root2, scaled2, inc2 = adjust(later, 1)
    both_roots = jnp.sum(root1 * root2)

    sp1, sp2 = split(root1 * scaled1), split(root1 * root2 * scaled2)
    shift1 = jnp.sum(inc1, axis=0, keepdims=True) * (1.0 / MEMBERS)
    free1 = inc1 - shift1
    g1, g2 = split(root2 * free1 + shift1), split(inc2)
    f1, s2 = split(free1), split(root2 * scaled2)
    lane = lax.broadcasted_iota(jnp.int32, (1, SLOTS), 1)
    tall = lax.broadcasted_iota(jnp.int32, (SLOTS, 1), 0)
    rest = [a.astype(F32) for a in split(1.0 - root1 * root2)]
    for q in range(2):
        h1, h2 = hots[q, 0], hots[q, 1]
        lead_h, lead_l = [dot_nt(a, h1) + dot_nt(b, h2) for a, b in zip(sp1, sp2)]
        lead[q] = paired(jnp.where(lane == MEAN, 1.0 / MEMBERS, lead_h), lead_l)
        gain_h, gain_l = [dot_nt(h1, a) + dot_nt(h2, b) for a, b in zip(g1, g2)]
        gain[q] = paired(
            jnp.where(tall == MEAN, rest[0], gain_h), jnp.where(tall == MEAN, rest[1], gain_l)
        )
        one = dot_nt(h1, f1[0]) + dot_nt(h1, f1[1])
        two = dot_nt(h2, s2[0]) + dot_nt(h2, s2[1])
        link[q] = paired(*split(exact(one, two, ((1,), (1,)))))

    def put_edge(i, j, pair):
        state[INSIDE + i, j] = pair

    sides.wait()
    members_to_lanes(edges, 0, FIELDS, mid, put_edge)
    tail.wait()

    def times(pair, m):
        got = jnp.dot(pair, m, preferred_element_type=F32)
        return got[:, :MEMBERS] + got[:, MEMBERS:]

    def product(a, m):
        return times(jnp.concatenate(split(a), axis=1), m)

    def whole(pair):
        return pair[:, :MEMBERS].astype(F32) + pair[:, MEMBERS:].astype(F32)

    def short(pair, t, q):
        cov = times(pair, lead[q])
        cov = cov + product(t * cov, link[q])
        return both_roots * whole(pair) + product(t * cov, gain[q])

    def block(g, n):
        return state[pl.ds(g, n)].reshape(n * 8 * SHARE, 2 * MEMBERS)

    def part(g, at, n):
        return state[g, pl.ds(at, n)].reshape(n * SHARE, 2 * MEMBERS)

    def put_rest(x):
        for f in range(FIELDS):
            put(f, REST_AT, x[f * 2 * SHARE : (f + 1) * 2 * SHARE], 2)

    def put(f, lon, x, n):
        made[f, pl.ds(lon, n)] = x.reshape(n, SHARE, MEMBERS)

    def store(f):
        return pltpu.make_async_copy(made.at[f], out.at[f], stores.at[f])

    @pl.when(many[0] == 0)
    def _():
        def shape(lon, n):
            return shapes[pl.ds(lon, n)].reshape(n * SHARE, SLOTS)

        pair = jnp.concatenate([block(INSIDE - 2, 1), part(INSIDE - 1, 0, 2)], axis=0)
        put_rest(short(pair, jnp.concatenate([shape(REST_AT, 2)] * FIELDS, axis=0), 1))

        def some(fs):
            for f in fs:
                inside(f).wait()
            n = INNER // 2
            for q, lon, edge in ((0, EDGE, 0), (1, CUT, WIDTH - EDGE)):
                pair = jnp.concatenate(
                    [
                        a
                        for f in fs
                        for a in (block(f * INNER + q * n, n), part(INSIDE + f, q * EDGE, EDGE))
                    ],
                    axis=0,
                )
                t = jnp.concatenate([shape(lon, 8 * n), shape(edge, EDGE)] * len(fs), axis=0)
                x = short(pair, t, q)
                r, m = (8 * n + EDGE) * SHARE, 8 * n * SHARE
                for i, f in enumerate(fs):
                    put(f, lon, x[i * r : i * r + m], 8 * n)
                    put(f, edge, x[i * r + m : (i + 1) * r], EDGE)
            for f in fs:
                store(f).start()

        some([0, 1, 2])
        some([3, 4])

    @pl.when(many[0] != 0)
    def _():
        near, hot, spot, placed = finder(place, fact)
        roots = [jnp.sum(root1), jnp.sum(root2)]
        chunks = []
        for b, (sp, g) in enumerate(((split(scaled1), split(inc1)), (split(scaled2), g2))):
            slot, n = near(b, 0.0, WIDTH - 1.0)
            chunks.append((n.astype(jnp.int32) + SLOTS - 1) // SLOTS)
            for c in range(CHUNKS):
                h = hot(slot, float(c * SLOTS))
                long_lead[b, c] = paired(dot_nt(sp[0], h), dot_nt(sp[1], h))
                long_gain[b, c] = paired(dot_nt(h, g[0]), dot_nt(h, g[1]))
                lon, up = spot(b, h)
                long_where[b, c] = placed(lon, up, n - float(c * SLOTS), -1)
        for f in range(FIELDS):
            inside(f).wait()

        def long(pair, lons):
            x = whole(pair)
            for b in range(2):
                mean = jnp.sum(x, axis=1, keepdims=True) * (1.0 / MEMBERS)
                anomaly = x - mean
                big[pl.ds(0, x.shape[0]), :] = x + (roots[b] - 1.0) * anomaly
                anomaly = roots[b] * anomaly

                def chunk(c, _):
                    t = jnp.concatenate([taper_of(long_where[b, c], lon) for lon in lons], axis=0)
                    w = t * product(anomaly, long_lead[b, c])
                    big[pl.ds(0, x.shape[0]), :] += product(w, long_gain[b, c])
                    return 0

                lax.fori_loop(0, chunks[b], chunk, 0)
                x = big[pl.ds(0, x.shape[0]), :]
            return x

        def each(g, _):
            f, lon = g // INNER, 8 * (g % INNER) + EDGE
            at = lon.astype(F32)
            put(f, lon, long(block(g, 1), [at + j for j in range(8)]), 8)
            return 0

        lax.fori_loop(0, FIELDS * INNER, each, 0)
        last = long(part(INSIDE - 1, 0, 2), [float(REST_AT + j) for j in range(2)])
        first = long(block(INSIDE - 2, 1), [float(REST_AT + j % 2) for j in range(8)])
        put_rest(jnp.concatenate([first, last], axis=0))
        for f in range(FIELDS):
            for at, lon in ((0, 0), (EDGE, WIDTH - EDGE)):
                lons = [float(lon + j) for j in range(EDGE)]
                put(f, lon, long(part(INSIDE + f, at, EDGE), lons), EDGE)
        for f in range(FIELDS):
            store(f).start()

    for f in range(FIELDS):
        store(f).wait()


def analyse(place, many, priors, facts, where, hots, taper, state, sides):
    square = (2 * SLOTS, 2 * MEMBERS)
    return pl.pallas_call(
        analyse_kernel,
        out_shape=jax.ShapeDtypeStruct((FIELDS, WIDTH, SHARE, MEMBERS), F32),
        in_specs=[SMEM] * 2 + [VMEM] * 6 + [ANY] * 4,
        out_specs=ANY,
        scratch_shapes=[
            pltpu.VMEM(hots.shape, BF16),
            pltpu.VMEM(taper.shape, F32),
            pltpu.VMEM((GROUPS,) + state.shape[1:], BF16),
            pltpu.VMEM((BANDS, 8, SHARE, LAT), F32),
            pltpu.VMEM((8, MEMBERS, LAT), F32),
            pltpu.VMEM((MEMBERS, NOBS), F32),
            pltpu.VMEM((2,) + square, BF16),
            pltpu.VMEM((2,) + square, BF16),
            pltpu.VMEM((2,) + square, BF16),
            pltpu.VMEM((WIDTH, SHARE, SLOTS), F32),
            pltpu.VMEM((FIELDS, WIDTH, SHARE, MEMBERS), F32),
            pltpu.VMEM((8 * SHARE, MEMBERS), F32),
            pltpu.VMEM((2, CHUNKS) + square, BF16),
            pltpu.VMEM((2, CHUNKS) + square, BF16),
            pltpu.VMEM((2, CHUNKS, SHARE + 16, SLOTS), F32),
            pltpu.SemaphoreType.DMA((FIELDS + 4,)),
            pltpu.SemaphoreType.DMA((FIELDS,)),
        ],
        compiler_params=PARAMS,
        name="analyse",
    )(place, many, *priors, facts, where, hots, taper, state, sides)


def across(x, axis, bits):
    count = lax.axis_size(axis)
    return lax.ppermute(x, axis, [(i, i ^ bits) for i in range(count)])


def shards(
    ensemble,
    ocean_depth,
    planetary_vorticity,
    land_mask,
    obs_values,
    obs_error,
    obs_lon,
    obs_lat,
    obs_field,
    obs_order,
):
    member, sector = lax.axis_index("member"), lax.axis_index("sector")
    sectors = lax.axis_size("sector")
    vort = planetary_vorticity.reshape(1, LAT)
    ens = jnp.transpose(ensemble, (1, 2, 0, 3))
    west_side, east_side = edges(ens, ocean_depth, land_mask)
    left = lax.ppermute(east_side, "sector", [(i, (i + 1) % sectors) for i in range(sectors)])
    right = lax.ppermute(west_side, "sector", [((i + 1) % sectors, i) for i in range(sectors)])

    lon_f, lat_f = obs_lon.astype(F32), obs_lat.astype(F32)
    facts = in_order(
        obs_order, jnp.stack([lon_f, lat_f, obs_values, obs_error] + [jnp.zeros_like(lon_f)] * 4)
    )
    west = sector * WIDTH
    here = obs_lon - west
    cell = ((obs_field - 2) * WIDTH + here) * LAT + obs_lat
    cell = jnp.where((here >= 0) & (here < WIDTH), cell, -1)
    place = jnp.stack([west, member * SHARE, member])
    hots, taper, where, many = prepare(place, facts)

    messages, seen = forecast_inner(ens, ocean_depth, land_mask, vort)
    parts = lax.all_to_all(messages, "member", split_axis=0, concat_axis=0, tiled=True)
    sides, seen = forecast_outer(ens, left, right, ocean_depth, land_mask, vort, seen)
    sides = lax.all_to_all(sides, "member", split_axis=0, concat_axis=0, tiled=True)

    own = pick(obs_order, cell, seen.reshape(3 * WIDTH, SHARE, LAT), where)
    own = (own + across(own, "sector", 2)) + (across(own, "sector", 4) + across(own, "sector", 6))
    own = own + across(own, "sector", 1)
    axes = ("member", "sector")
    count = lax.axis_size("member") * sectors
    both = lax.ppermute(own, axes, [(i, i ^ (4 * sectors + 8)) for i in range(count)])
    low, high = across(own, "sector", 8), across(own, "member", 4)
    own = jnp.stack([own, high]) + jnp.stack([low, both])
    priors = [own] + [across(own, "member", x) for x in (1, 2, 3)]
    analysis = analyse(place, many, priors, facts, where, hots, taper, arrange(parts), sides)
    return jnp.transpose(analysis, (0, 2, 1, 3))


def solution(mesh):
    placed = (
        P("member", None, "sector", None),
        P("sector", None),
        P(),
        P("sector", None),
        P(),
        P(),
        P(),
        P(),
        P(),
        P(),
    )
    return jax.shard_map(
        shards,
        mesh=mesh,
        in_specs=placed,
        out_specs=P(None, "member", "sector", None),
        check_vma=False,
    )
```
